256 devices in a mesh: aa: 64 (over z, y, core), pb: 4 (over x).
Axes of the slice: x: 4, y: 4, z: 8, core: 2. Of those that a mesh axis runs over, the one named last changes fastest.
Arguments:
- wave_field: float32 [64, 2, 128, 512], P('aa'), may hold values from -6 to 6
- scaled_dual: float32 [64, 2, 128, 512], P('aa', None, None, 'pb'), may hold values from -4 to 4
- intensity: float32 [64, 64, 4096], P('aa', 'pb'), may hold values from 0 to 2
- probe_field: float32 [2, 64, 64], replicated, may hold values from -5 to 5
- scan_rows: int32 [64, 64], P('aa', 'pb'), may hold values from 0 to 64
- scan_cols: int32 [64, 64], P('aa', 'pb'), may hold values from 0 to 448
- sample_mask: int32 [64, 64], P('aa', 'pb'), may hold values 0 or 1
- object_field: float32 [2, 128, 512, 512], P(None, 'aa', 'pb'), may hold values from -6 to 6
- ray_blocks: int32 [64, 8, 12], replicated, may hold values from 0 to 63
- ray_tables: int32 [64, 8, 12], replicated, may hold values from 0 to 11
- radon_weights: bfloat16 [4096, 768], replicated, may hold values from -0.02734375 to 0.02734375
Outputs:
- wave_next: float32 [64, 2, 128, 512], P('aa', None, None, 'pb')
- probe_next: float32 [2, 64, 64], replicated
- object_next: float32 [2, 128, 512, 512], P(None, 'aa', 'pb')
The draws below stay inside these ranges and needn't reach their ends.
Inputs may be any that keep to these rules, and one draw needn't show every extreme that they name: `scan_rows`: each scan window lies inside the projection. `scan_cols`: each scan window lies inside the projection. `ray_blocks`: a block may appear several times in one list.
All inputs are finite; a program needn't handle non-finite values. No bound on the sum of `sample_mask` on one device may be relied on, other than what follows from the above.
Results may differ from the reference program's by a relative error of at most 0.00065.
The reference program's roundings to bfloat16 on the way count: a program that leaves them out, or rounds other values in their place, can miss the bound.
Values may be sent and summed in bfloat16 or wider, within the bound.
A program may use at most 128 MiB of HBM per device.

```python
import math
import jax
import jax.numpy as jnp
from jax import lax

PAT = 64
NU = 512
BLK = 64
NW = 12
LIST = 12
ANGLES = 64
POSITIONS = 64
NZ = 128
NB = 8
BLOCKS = 64
BIN = 64
PIXB = 4096


def touch_ends(result, stream_key, smallest, high):
    longest = result.shape.index(max(result.shape))
    spots = []
    for shift in (0, 1):
        where = [jax.random.randint(jax.random.fold_in(stream_key, axis), (), 0, length) for axis, length in enumerate(result.shape)]
        where[longest] = (where[longest] + shift) % result.shape[longest]
        spots.append(tuple(where))
    return result.at[spots[0]].set(smallest).at[spots[1]].set(high)


def levels(key, shape, shards, low, top_value):
    gain = 1.0
    for axis_at, parts in shards:
        heights = jax.random.uniform(jax.random.fold_in(jax.random.fold_in(key, 6), axis_at), (parts,), jnp.float32, low / len(shards), top_value / len(shards))
        gain = gain * jnp.repeat(jnp.exp(heights), shape[axis_at] // parts).reshape((-1,) + (1,) * (len(shape) - 1 - axis_at))
    return gain


def normal_values(own_key, shape, width, reach, cuts=(), kind=jnp.bfloat16):
    array = jax.random.normal(own_key, shape, jnp.float32) * width
    if len(cuts) > 0:
        array = levels(own_key, shape, cuts, -0.22, 0.18) * array
    return jnp.clip(array, min=-reach, max=reach).astype(kind)


def setup_inputs(seed: int = 0) -> dict:
    key_of = jax.random.split(jax.random.key(seed), 12)
    return {
        "wave_field": normal_values(key_of[0], (ANGLES, 2, NZ, NU), 1.0, 6.0, ((0, 64),), jnp.float32),
        "scaled_dual": normal_values(key_of[1], (ANGLES, 2, NZ, NU), 0.5, 4.0, ((0, 64), (3, 4)), jnp.float32),
        "intensity": jnp.clip(2.0 * jax.random.uniform(key_of[2], (ANGLES, POSITIONS, PAT * PAT), jnp.float32) ** levels(key_of[2], (ANGLES, POSITIONS, PAT * PAT), ((0, 64), (1, 4)), -0.2, 0.2), 0.0, 2.0),
        "probe_field": normal_values(key_of[3], (2, PAT, PAT), 1.0, 5.0, (), jnp.float32),
        "scan_rows": touch_ends(jax.random.randint(key_of[4], (ANGLES, POSITIONS), 0, NZ - PAT + 1), jax.random.fold_in(key_of[4], 1), 0, NZ - PAT).astype(jnp.int32),
        "scan_cols": touch_ends(jax.random.randint(key_of[5], (ANGLES, POSITIONS), 0, NU - PAT + 1), jax.random.fold_in(key_of[5], 1), 0, NU - PAT).astype(jnp.int32),
        "sample_mask": touch_ends((jax.random.randint(key_of[6], (ANGLES, POSITIONS), 0, 4) < 3).astype(jnp.int32), jax.random.fold_in(key_of[6], 1), 0, 1),
        "object_field": normal_values(key_of[7], (2, NZ, NU, NU), 1.0, 6.0, ((1, 64), (2, 4)), jnp.float32),
        "ray_blocks": touch_ends(jax.random.randint(key_of[8], (ANGLES, NB, LIST), 0, BLOCKS), jax.random.fold_in(key_of[8], 1), 0, BLOCKS - 1).astype(jnp.int32),
        "ray_tables": touch_ends(jax.random.randint(key_of[9], (ANGLES, NB, LIST), 0, NW), jax.random.fold_in(key_of[9], 1), 0, NW - 1).astype(jnp.int32),
        "radon_weights": normal_values(key_of[10], (PIXB, NW * BIN), (PIXB * LIST) ** -0.5, 0.02734375),
    }


WAVE_STEP = 0.05
PENALTY = 1.0
PROBE_STEP = 0.05
OBJECT_STEP = 1.0

def dft_tables(size):
    index = jnp.arange(size, dtype=jnp.int32)
    phase = index[:, None] * index[None, :] % size
    angle = phase.astype(jnp.float32) * (-2.0 * math.pi / size)
    scale = 1.0 / math.sqrt(size)
    return (jnp.cos(angle) * scale, jnp.sin(angle) * scale)

def transform(field_re, field_im, tab_re, tab_im):
    highest = lax.Precision.HIGHEST

    def apply_left(table, field):
        return jnp.einsum('ik,nkl->nil', table, field, precision=highest)

    def apply_right(field, table):
        return jnp.einsum('nil,lj->nij', field, table, precision=highest)
    half_re = apply_left(tab_re, field_re) - apply_left(tab_im, field_im)
    half_im = apply_left(tab_re, field_im) + apply_left(tab_im, field_re)
    out_re = apply_right(half_re, tab_re) - apply_right(half_im, tab_im)
    out_im = apply_right(half_re, tab_im) + apply_right(half_im, tab_re)
    return (out_re, out_im)

def ptycho_grads(waves, probe, scan_rows, scan_cols, sample_mask, intensity):
    count_ang, count_pos = scan_rows.shape
    size = probe.shape[-1]
    angle_col = jnp.broadcast_to(jnp.arange(count_ang, dtype=jnp.int32)[:, None], (count_ang, count_pos))
    starts = jnp.stack([angle_col, scan_rows.astype(jnp.int32), scan_cols.astype(jnp.int32)], axis=-1).reshape(-1, 3)
    zero_index = jnp.zeros((), jnp.int32)

    def cut_window(start):
        piece = lax.dynamic_slice(waves, (start[0], zero_index, start[1], start[2]), (1, 2, size, size))
        return piece[0]
    windows = jax.vmap(cut_window)(starts)
    win_re = windows[:, 0]
    win_im = windows[:, 1]
    probe_re = probe[0]
    probe_im = probe[1]
    patch_re = probe_re * win_re - probe_im * win_im
    patch_im = probe_re * win_im + probe_im * win_re
    tab_re, tab_im = dft_tables(size)
    far_re, far_im = transform(patch_re, patch_im, tab_re, tab_im)
    live = sample_mask.reshape(-1, 1, 1).astype(jnp.float32)
    factor = live * (far_re * far_re + far_im * far_im - intensity.reshape(-1, size, size))
    back_re, back_im = transform(factor * far_re, factor * far_im, tab_re, -tab_im)
    grad_re = probe_re * back_re + probe_im * back_im
    grad_im = probe_re * back_im - probe_im * back_re
    updates = jnp.stack([grad_re, grad_im], axis=1)
    numbers = lax.ScatterDimensionNumbers(update_window_dims=(1, 2, 3), inserted_window_dims=(0,), scatter_dims_to_operand_dims=(0, 2, 3))
    wave_grad = lax.scatter_add(jnp.zeros(waves.shape, jnp.float32), starts, updates, numbers)
    probe_re_grad = lax.optimization_barrier(jnp.sum(win_re * back_re + win_im * back_im, axis=0))
    probe_im_grad = lax.optimization_barrier(jnp.sum(win_re * back_im - win_im * back_re, axis=0))
    return (wave_grad, jnp.stack([probe_re_grad, probe_im_grad]))

def ray_onehot(ray_blocks, ray_tables):
    keys = ray_blocks * NW + ray_tables
    columns = jnp.arange(BLOCKS * NW, dtype=jnp.int32)
    hits = jnp.zeros(keys.shape[:2] + (BLOCKS * NW,), jnp.float32)
    for entry in range(keys.shape[2]):
        hits = hits + (keys[:, :, entry, None] == columns).astype(jnp.float32)
    return hits.astype(jnp.bfloat16)

def reference(wave_field, scaled_dual, intensity, probe_field, scan_rows, scan_cols, sample_mask, object_field, ray_blocks, ray_tables, radon_weights):
    depth = object_field.shape[1]
    angles = ray_blocks.shape[0]
    hits = ray_onehot(ray_blocks, ray_tables).reshape(angles * NB, BLOCKS * NW)
    object_bf = object_field.astype(jnp.bfloat16)
    tiles = object_bf.reshape(2, depth, NB, BLK, NB, BLK).transpose(0, 1, 2, 4, 3, 5).reshape(-1, PIXB)
    products = jnp.dot(tiles, radon_weights, preferred_element_type=jnp.float32).astype(jnp.bfloat16)
    stacked = products.reshape(2, depth, BLOCKS, NW, BIN).transpose(2, 3, 0, 1, 4).reshape(BLOCKS * NW, 2 * depth * BIN)
    projection = jnp.dot(hits, stacked, preferred_element_type=jnp.float32)
    projection = projection.reshape(angles, NB, 2, depth, BIN).transpose(0, 2, 3, 1, 4).reshape(angles, 2, depth, NU)
    wave_grad, probe_grad = ptycho_grads(wave_field, probe_field, scan_rows, scan_cols, sample_mask, intensity)
    wave_next = wave_field - WAVE_STEP * (wave_grad + PENALTY * (wave_field - projection + scaled_dual))
    positions = scan_rows.shape[1]
    probe_next = probe_field - PROBE_STEP / (angles * positions) * probe_grad
    target = wave_next + scaled_dual
    misfit = (projection - target).astype(jnp.bfloat16)
    rays = misfit.reshape(angles, 2, depth, NB, BIN).transpose(0, 3, 1, 2, 4).reshape(angles * NB, 2 * depth * BIN)
    table_sums = lax.dot_general(hits, rays, (((0,), (0,)), ((), ())), preferred_element_type=jnp.float32).astype(jnp.bfloat16)
    spread = table_sums.reshape(BLOCKS, NW, 2, depth, BIN).transpose(2, 3, 0, 1, 4).reshape(2 * depth * BLOCKS, NW * BIN)
    object_grad = lax.dot_general(spread, radon_weights, (((1,), (1,)), ((), ())), preferred_element_type=jnp.float32)
    object_grad = object_grad.reshape(2, depth, NB, NB, BLK, BLK).transpose(0, 1, 2, 4, 3, 5).reshape(2, depth, NU, NU)
    object_next = object_field - OBJECT_STEP * object_grad
    return (wave_next, probe_next, object_next)
```

```python
import math

import jax
import jax.numpy as jnp
import ml_dtypes
import numpy as np
from jax import lax
from jax.experimental import pallas as pl
from jax.experimental.pallas import tpu as pltpu
from jax.sharding import PartitionSpec as P

BLK = 64
NW = 12
NB = 8
LIST = 12
AA = 64
PB = 4
ZC = 4
POS = 16
PAIRS = 8
KEYS = 192
MESH_Y_CORE = 8
SLOT = 8
WCH = 8
WROWS = 4096 // WCH

WAVE_STEP = 0.05
PENALTY = 1.0
PROBE_STEP = 0.05
OBJECT_STEP = 1.0

F32 = jnp.float32
BF16 = jnp.bfloat16


def split_np(table):
    high = table.astype(ml_dtypes.bfloat16)
    low = (table - high.astype(np.float64)).astype(ml_dtypes.bfloat16)
    return high, low


def dft_constants():
    index = np.arange(BLK)
    phase = (index[:, None] * index[None, :]) % BLK
    angle = phase.astype(np.float64) * (-2.0 * math.pi / BLK)
    f_re, f_im = np.cos(angle) / math.sqrt(BLK), np.sin(angle) / math.sqrt(BLK)
    pair = np.eye(2)

    def right(re, im):
        dre, dim = np.kron(pair, re), np.kron(pair, im)
        return np.block([[dre, dim], [-dim, dre]])

    def left(re, im):
        high, low = split_np(np.block([[re, -im], [im, re]]))
        return np.concatenate(
            [np.concatenate([high, high], 1), np.concatenate([low, low], 1)], 0
        )

    order = np.concatenate([np.arange(0, BLK, 2), np.arange(1, BLK, 2)])
    g_hi, g_lo = split_np(right(f_re, f_im))
    b_hi, b_lo = split_np(right(f_re, -f_im))
    l_fwd = left(f_re[order, :], f_im[order, :])
    l_bwd = left(f_re[:, order], -f_im[:, order])
    return np.stack([g_hi, g_lo, b_hi, b_lo, l_fwd, l_bwd])


def halves(value):
    high = value.astype(BF16)
    low = (value - high.astype(F32)).astype(BF16)
    return high, low


def dot(lhs, rhs):
    return jnp.dot(lhs, rhs, preferred_element_type=F32)


def right_apply(re, im, g_hi, g_lo):
    high, low = halves(jnp.concatenate([re, im], axis=1))
    out = dot(high, g_hi) + dot(low, g_hi) + dot(high, g_lo)
    return out[:, :128], out[:, 128:]


def left_apply(re, im, table):
    high, low = halves(jnp.concatenate([re, im], axis=0))
    out = dot(table, jnp.concatenate([high, low], axis=0))
    out = out[:128] + out[128:]
    return out[:64], out[64:]


def rows_to_lanes(value):
    return jnp.concatenate([value[q * 64 : (q + 1) * 64] for q in range(PAIRS)], axis=1)


def lanes_to_rows(value):
    return jnp.concatenate([value[:, q * 128 : (q + 1) * 128] for q in range(PAIRS)], axis=0)


def swap(value):
    return pltpu.roll(value, 64, 1)


def interleave(first, second):
    low = lax.broadcasted_iota(jnp.int32, first.shape, 1) < 64
    return jnp.where(low, first, swap(second)), jnp.where(low, swap(first), second)


def kernel(
    rows_ref,
    cols_ref,
    mask_ref,
    obj_hbm,
    wts_hbm,
    wave_hbm,
    dual_hbm,
    int_hbm,
    probe_hbm,
    tab_hbm,
    rowkey_hbm,
    colkey_hbm,
    wave_out,
    probe_out,
    obj_out,
    obj,
    wts,
    wave,
    dual,
    inten,
    probe,
    tab,
    rowkey,
    colkey,
    lhs,
    ptile,
    stk,
    hit_r,
    hit_c,
    win_r,
    win_i,
    gra_r,
    gra_i,
    pad,
    acc,
    share,
    base,
    send1,
    recv1,
    send2,
    recv2,
    wnext,
    rays,
    spread,
    onew,
    prow,
    pfull,
    pout,
    in_sem,
    w_sem,
    out_sem,
    x_send,
    x_recv,
    a_send,
    a_recv,
):
    me_a = lax.axis_index("aa")
    me_p = lax.axis_index("pb")
    z_base = (me_a // MESH_Y_CORE) * MESH_Y_CORE
    z_own = me_a // MESH_Y_CORE
    m_own = me_a % MESH_Y_CORE

    def lanes(shape):
        return lax.broadcasted_iota(jnp.int32, shape, 1)

    obj_in = [
        pltpu.make_async_copy(
            obj_hbm.at[:, pl.ds(t * 128, 128)], obj.at[pl.ds(t * 512, 512)], in_sem.at[t]
        )
        for t in range(4)
    ]
    wts_in = [
        pltpu.make_async_copy(
            wts_hbm.at[pl.ds(c * WROWS, WROWS)], wts.at[pl.ds(c * WROWS, WROWS)], w_sem.at[c]
        )
        for c in range(WCH)
    ]
    wave_in = [
        pltpu.make_async_copy(
            wave_hbm.at[:, pl.ds(t * 128, 128)], wave.at[pl.ds(t * 256, 256)], in_sem.at[4 + t]
        )
        for t in range(4)
    ]
    others = {
        name: pltpu.make_async_copy(src, dst, in_sem.at[8 + n])
        for n, (name, src, dst) in enumerate(
            [
                ("rowkey", rowkey_hbm, rowkey),
                ("colkey", colkey_hbm, colkey),
                ("probe", probe_hbm, probe),
                ("tab", tab_hbm, tab),
                ("inten", int_hbm, inten),
                ("dual", dual_hbm, dual),
            ]
        )
    }
    others["rowkey"].start()
    for copy in obj_in + wts_in + wave_in:
        copy.start()
    for name in ("probe", "tab", "inten", "dual", "colkey"):
        others[name].start()

    barrier = pltpu.get_barrier_semaphore()

    def greet(step, carry):
        peer = lax.rem(me_a + step, AA)
        pl.semaphore_signal(
            barrier, inc=1, device_id={"aa": peer}, device_id_type=pl.DeviceIdType.MESH
        )
        return carry

    lax.fori_loop(1, AA, greet, 0)
    for step in range(1, PB):
        pl.semaphore_signal(
            barrier,
            inc=1,
            device_id={"pb": lax.rem(me_p + step, PB)},
            device_id_type=pl.DeviceIdType.MESH,
        )

    others["rowkey"].wait()
    keys = rowkey[...]
    for t in range(6):
        column = lanes((128, 128)) + t * 128
        total = jnp.zeros((128, 128), F32)
        for e in range(LIST):
            total = total + jnp.where(keys[:, e : e + 1] == column, 1.0, 0.0)
        hit_r[:, t * 128 : (t + 1) * 128] = total.astype(BF16)

    for copy in obj_in:
        copy.wait()

    def fold(q, carry):
        for t in range(4):
            even = obj[pl.ds(t * 512 + 2 * q, 8, stride=64), :]
            odd = obj[pl.ds(t * 512 + 2 * q + 1, 8, stride=64), :]
            first, second = interleave(even, odd)
            at = pl.multiple_of(q * 64 + t * 16, 16)
            lhs[pl.ds(at, 16), :] = jnp.concatenate([first, second], axis=0)
        return carry

    lax.fori_loop(0, 32, fold, 0, unroll=4)
    products = jnp.zeros((64, 768), F32)
    per = 32 // WCH
    for c in range(WCH):
        wts_in[c].wait()
        part = jnp.concatenate(
            [lhs[(c * per + n) * 64 : (c * per + n + 1) * 64, :] for n in range(per)], axis=1
        ).astype(BF16)
        products = products + dot(part, wts[c * WROWS : (c + 1) * WROWS, :])
    for t in range(6):
        ptile[t * 64 : (t + 1) * 64, :] = products[:, t * 128 : (t + 1) * 128]
    own_stk = pl.multiple_of(me_p * KEYS, KEYS)
    for t in range(6):
        lists = [[], []], [[], []]
        for br in range(2):
            part = [ptile[pl.ds(t * 64 + cz * 2 + br, 8, stride=8), :] for cz in range(ZC)]
            for c in range(2):
                even, odd = interleave(part[2 * c], part[2 * c + 1])
                lists[0][c].append(even)
                lists[1][c].append(odd)
        for h in range(2):
            for c in range(2):
                stk[
                    pl.ds(pl.multiple_of(own_stk + (2 * t + h) * 16, 16), 16),
                    c * 128 : (c + 1) * 128,
                ] = jnp.concatenate(lists[h][c], axis=0).astype(BF16)

    pl.semaphore_wait(barrier, AA - 1 + PB - 1)

    def to_x(stage, step, src, dst):
        peer = lax.rem(me_p + step, PB)
        return pltpu.make_async_remote_copy(
            src_ref=src,
            dst_ref=dst,
            send_sem=x_send.at[stage * 3 + step - 1],
            recv_sem=x_recv.at[stage * 3 + step - 1],
            device_id={"pb": peer},
            device_id_type=pl.DeviceIdType.MESH,
        )

    own_block = stk.at[pl.ds(own_stk, KEYS)]
    gathers = [to_x(0, step, own_block, own_block) for step in range(1, PB)]
    for copy in gathers:
        copy.start()

    for copy in wave_in:
        copy.wait()

    def windows(q, carry):
        at = pl.multiple_of(q * 64, 64)
        for c, ref in ((0, win_r), (1, win_i)):
            found = []
            for h in range(2):
                row = rows_ref[0, 2 * q + h]
                col = cols_ref[0, 2 * q + h]
                tile = col // 128
                off = col % 128
                near = wave[pl.ds(tile * 256 + c * 128 + row, 64), :]
                far = wave[pl.ds(jnp.minimum(tile + 1, 3) * 256 + c * 128 + row, 64), :]
                both = jnp.where(lanes((64, 128)) >= off, near, far)
                found.append(pltpu.roll(both, (128 + 64 * h - off) % 128, 1))
            ref[pl.ds(at, 64), :] = jnp.where(lanes((64, 128)) < 64, found[0], found[1])
        return carry

    lax.fori_loop(0, PAIRS, windows, 0)
    others["probe"].wait()
    others["tab"].wait()
    others["inten"].wait()
    p_re = jnp.concatenate([probe[0]] * PAIRS, axis=0)
    p_im = jnp.concatenate([probe[1]] * PAIRS, axis=0)
    w_re, w_im = win_r[...], win_i[...]
    half_re, half_im = right_apply(
        p_re * w_re - p_im * w_im, p_re * w_im + p_im * w_re, tab[0], tab[1]
    )
    far_re, far_im = left_apply(rows_to_lanes(half_re), rows_to_lanes(half_im), tab[4])
    measured, live = [], []
    for q in range(PAIRS):
        even, odd = interleave(inten[2 * q], inten[2 * q + 1])
        measured.append(jnp.concatenate([even, odd], axis=0))
        live.append(
            jnp.where(
                lanes((1, 128)) < 64, mask_ref[0, 2 * q].astype(F32), mask_ref[0, 2 * q + 1].astype(F32)
            )
        )
    measured = jnp.concatenate(measured, axis=1)
    live = jnp.concatenate(live, axis=1)
    factor = live * (far_re * far_re + far_im * far_im - measured)
    half_re, half_im = left_apply(factor * far_re, factor * far_im, tab[5])
    back_re, back_im = right_apply(lanes_to_rows(half_re), lanes_to_rows(half_im), tab[2], tab[3])
    gra_r[...] = p_re * back_re + p_im * back_im
    gra_i[...] = p_re * back_im - p_im * back_re
    grad_re = jnp.sum((w_re * back_re + w_im * back_im).reshape(PAIRS, 64, 128), axis=0)
    grad_im = jnp.sum((w_re * back_im - w_im * back_re).reshape(PAIRS, 64, 128), axis=0)
    grad_re = grad_re + swap(grad_re)
    grad_im = grad_im + swap(grad_im)
    send1[pl.ds(4, 64, stride=SLOT), :] = jnp.where(lanes((64, 128)) < 64, grad_re, grad_im)

    pad[...] = jnp.zeros_like(pad)
    acc[...] = jnp.zeros_like(acc)

    def scatter(q, carry):
        at = pl.multiple_of(q * 64, 64)
        for h in range(2):
            row = rows_ref[0, 2 * q + h]
            col = cols_ref[0, 2 * q + h]
            turn = (col + 128 - 64 * h) % 128
            for c, ref in ((0, gra_r), (1, gra_i)):
                slot = (2 * h + c) * 192
                pad[slot + 64 : slot + 128, :] = pltpu.roll(ref[pl.ds(at, 64), :], turn, 1)
                moved = pad[pl.ds(slot + 64 - row, 128), :]
                for t in range(4):
                    place = lanes((128, 128)) + (t * 128 - col)
                    start = t * 256 + c * 128
                    acc[start : start + 128, :] = acc[start : start + 128, :] + jnp.where(
                        (place >= 0) & (place < 64), moved, 0.0
                    )
        return carry

    lax.fori_loop(0, PAIRS, scatter, 0)
    reduces = [
        to_x(
            1,
            step,
            acc.at[pl.ds(pl.multiple_of(lax.rem(me_p + step, PB) * 256, 256), 256)],
            share.at[pl.ds((step - 1) * 256, 256)],
        )
        for step in range(1, PB)
    ]
    for copy in reduces:
        copy.start()

    for copy in gathers:
        copy.wait_recv()
    projection = dot(hit_r[...], stk[...])
    for c in range(2):
        first, second = interleave(
            projection[:64, c * 128 : (c + 1) * 128], projection[64:, c * 128 : (c + 1) * 128]
        )
        send1[pl.ds(2 * c, 64, stride=SLOT), :] = first
        send1[pl.ds(2 * c + 1, 64, stride=SLOT), :] = second

    def to_a(stage, peer, src, dst):
        return pltpu.make_async_remote_copy(
            src_ref=src,
            dst_ref=dst,
            send_sem=a_send.at[stage],
            recv_sem=a_recv.at[stage],
            device_id={"aa": peer},
            device_id_type=pl.DeviceIdType.MESH,
        )

    def exchange(stage, source, target, count):
        def send(step, carry):
            peer = lax.rem(me_a + step, AA)
            to_a(
                stage,
                peer,
                source.at[pl.ds(pl.multiple_of(peer * SLOT, SLOT), count)],
                target.at[pl.ds(pl.multiple_of(me_a * SLOT, SLOT), count)],
            ).start()
            return carry

        lax.fori_loop(1, AA, send, 0)
        own = pl.ds(pl.multiple_of(me_a * SLOT, SLOT), count)
        target[own, :] = source[own, :]
        return to_a(
            stage,
            lax.rem(me_a + 1, AA),
            source.at[pl.ds(0, (AA - 1) * count)],
            target.at[pl.ds(0, (AA - 1) * count)],
        )

    first_move = exchange(0, send1, recv1, 5)

    others["colkey"].wait()
    for r in range(3):
        mine = lax.broadcasted_iota(jnp.int32, (64, 512), 0) + r * 64
        total = jnp.zeros((64, 512), F32)
        for e in range(LIST):
            total = total + jnp.where(colkey[e : e + 1, :] == mine, 1.0, 0.0)
        hit_c[r * 64 : (r + 1) * 64, :] = total.astype(BF16)

    others["dual"].wait()
    own_cols = pl.ds(pl.multiple_of(me_p * 256, 256), 256)
    mine = wave[own_cols, :]
    for copy in reduces:
        copy.wait_recv()
    gradient = acc[own_cols, :] + share[0:256, :] + share[256:512, :] + share[512:768, :]
    base[...] = mine - WAVE_STEP * (gradient + PENALTY * (mine + dual[...]))

    first_move.wait_recv()
    for c in range(2):
        for z in range(2):
            there = pl.ds(c * 128 + z, 64, stride=2)
            here = recv1[pl.ds(2 * c + z, 64, stride=SLOT), :]
            moved = base[there, :] + (WAVE_STEP * PENALTY) * here
            wnext[there, :] = moved
            misfit = here - (moved + dual[there, :])
            send2[pl.ds(2 * c + z, 64, stride=SLOT), :] = misfit.astype(BF16).astype(F32)
    second_move = exchange(1, send2, recv2, 4)
    wave_copy = pltpu.make_async_copy(wnext, wave_out, out_sem.at[0])
    wave_copy.start()

    own_row = pl.ds(pl.multiple_of(me_p * 8, 8), 1)
    prow[own_row, :] = jnp.sum(recv1[pl.ds(4, 64, stride=SLOT), :], axis=0, keepdims=True)
    probe_x = [to_x(3, step, prow.at[own_row], prow.at[own_row]) for step in range(1, PB)]
    for copy in probe_x:
        copy.start()
    for copy in probe_x:
        copy.wait_recv()
    pfull[pl.ds(me_a, 1), :] = (prow[0:1, :] + prow[8:9, :]) + (prow[16:17, :] + prow[24:25, :])

    def layer(step):
        peer = z_base + lax.rem(m_own + step, MESH_Y_CORE)
        row = pfull.at[pl.ds(me_a, 1)]
        return to_a(2, peer, row, row)

    for step in range(1, MESH_Y_CORE):
        layer(step).start()

    second_move.wait_recv()
    own_rays = pl.multiple_of(me_p * 128, 128)
    for c in range(2):
        first, second = interleave(
            recv2[pl.ds(2 * c, 64, stride=SLOT), :], recv2[pl.ds(2 * c + 1, 64, stride=SLOT), :]
        )
        rays[pl.ds(own_rays, 128), c * 128 : (c + 1) * 128] = jnp.concatenate(
            [first, second], axis=0
        ).astype(BF16)
    own_rows = rays.at[pl.ds(own_rays, 128)]
    ray_moves = [to_x(2, step, own_rows, own_rows) for step in range(1, PB)]
    for copy in ray_moves:
        copy.start()

    seven = pfull.at[pl.ds(0, MESH_Y_CORE - 1)]
    layer_all = to_a(2, z_base + lax.rem(m_own + 1, MESH_Y_CORE), seven, seven)
    layer_all.wait_recv()
    layer_all.wait_send()
    group = pfull.at[pl.ds(pl.multiple_of(z_base, 8), 8)]

    def stack(step):
        peer = lax.rem(z_own + step, AA // MESH_Y_CORE) * MESH_Y_CORE + m_own
        return to_a(3, peer, group, group)

    for step in range(1, AA // MESH_Y_CORE):
        stack(step).start()

    for copy in ray_moves:
        copy.wait_recv()

    sums = dot(hit_c[...], rays[...]).astype(BF16).astype(F32)
    for t in range(6):
        for br in range(2):
            for c in range(2):
                at = 2 * t * 16 + br * 8
                first, second = interleave(
                    sums[at : at + 8, c * 128 : (c + 1) * 128],
                    sums[at + 16 : at + 24, c * 128 : (c + 1) * 128],
                )
                spread[pl.ds(t * 64 + 4 * c + br, 8, stride=8), :] = first
                spread[pl.ds(t * 64 + 4 * c + 2 + br, 8, stride=8), :] = second
    table = jnp.concatenate(
        [spread[t * 64 : (t + 1) * 64, :] for t in range(6)], axis=1
    ).astype(BF16)
    for n in range(WCH):
        grad = lax.dot_general(
            table,
            wts[n * WROWS : (n + 1) * WROWS, :],
            (((1,), (1,)), ((), ())),
            preferred_element_type=F32,
        )
        for s in range(per):
            q = n * per + s
            for t in range(4):
                first, second = interleave(
                    grad[t * 16 : t * 16 + 8, s * 128 : (s + 1) * 128],
                    grad[t * 16 + 8 : t * 16 + 16, s * 128 : (s + 1) * 128],
                )
                even = pl.ds(t * 512 + 2 * q, 8, stride=64)
                odd = pl.ds(t * 512 + 2 * q + 1, 8, stride=64)
                onew[even, :] = obj[even, :] - OBJECT_STEP * first
                onew[odd, :] = obj[odd, :] - OBJECT_STEP * second
    obj_copies = [
        pltpu.make_async_copy(
            onew.at[pl.ds(t * 512, 512)], obj_out.at[:, pl.ds(t * 128, 128)], out_sem.at[1 + t]
        )
        for t in range(4)
    ]
    for copy in obj_copies:
        copy.start()

    others_all = pfull.at[pl.ds(0, 7 * MESH_Y_CORE)]
    stack_all = to_a(
        3, lax.rem(z_own + 1, AA // MESH_Y_CORE) * MESH_Y_CORE + m_own, others_all, others_all
    )
    stack_all.wait_recv()
    stack_all.wait_send()
    total = pfull[...]
    scale = PROBE_STEP / (AA * POS * PB)
    old_re, old_im = probe[0], probe[1]
    pout[0] = (old_re - scale * total)[:, :64]
    pout[1] = (old_im - scale * swap(total))[:, :64]
    probe_copy = pltpu.make_async_copy(pout, probe_out, out_sem.at[5])
    probe_copy.start()

    for copy in gathers + reduces + probe_x + ray_moves:
        copy.wait_send()
    first_move.wait_send()
    second_move.wait_send()
    wave_copy.wait()
    for copy in obj_copies:
        copy.wait()
    probe_copy.wait()


def shards(
    tables,
    wave_field,
    scaled_dual,
    intensity,
    probe_field,
    scan_rows,
    scan_cols,
    sample_mask,
    object_field,
    ray_blocks,
    ray_tables,
    radon_weights,
):
    column = lax.axis_index("pb")
    own_blocks = 64 // PB
    place = ray_tables * own_blocks + ray_blocks % own_blocks
    owner = ray_blocks // own_blocks
    own_lists = lax.dynamic_slice_in_dim(owner * KEYS + place, column * 2, 2, 1)
    row_keys = own_lists.transpose(1, 0, 2).reshape(2 * AA, LIST)
    col_keys = jnp.where(owner == column, place, -1).transpose(2, 1, 0).reshape(LIST, NB * AA)
    any_spec = pl.BlockSpec(memory_space=pl.ANY)
    smem = pl.BlockSpec(memory_space=pltpu.SMEM)
    vmem = pltpu.VMEM
    wave_next, probe_next, object_next = pl.pallas_call(
        kernel,
        out_shape=(
            jax.ShapeDtypeStruct((256, 128), F32),
            jax.ShapeDtypeStruct((2, 64, 64), F32),
            jax.ShapeDtypeStruct((512, 512), F32),
        ),
        in_specs=[smem] * 3 + [any_spec] * 9,
        out_specs=[any_spec] * 3,
        scratch_shapes=[
            vmem((2048, 128), F32),
            vmem((4096, 768), BF16),
            vmem((1024, 128), F32),
            vmem((256, 128), F32),
            vmem((POS, 32, 128), F32),
            vmem((2, 64, 128), F32),
            vmem((6, 256, 256), BF16),
            vmem((128, LIST), jnp.int32),
            vmem((LIST, 512), jnp.int32),
            vmem((2048, 128), F32),
            vmem((384, 128), F32),
            vmem((768, 256), BF16),
            vmem((128, 768), BF16),
            vmem((KEYS, 512), BF16),
            vmem((512, 128), F32),
            vmem((512, 128), F32),
            vmem((512, 128), F32),
            vmem((512, 128), F32),
            vmem((768, 128), F32),
            vmem((1024, 128), F32),
            vmem((768, 128), F32),
            vmem((256, 128), F32),
            vmem((AA * SLOT, 128), F32),
            vmem((AA * SLOT, 128), F32),
            vmem((AA * SLOT, 128), F32),
            vmem((AA * SLOT, 128), F32),
            vmem((256, 128), F32),
            vmem((512, 256), BF16),
            vmem((384, 128), F32),
            vmem((2048, 128), F32),
            vmem((32, 128), F32),
            vmem((64, 128), F32),
            vmem((2, 64, 64), F32),
            pltpu.SemaphoreType.DMA((14,)),
            pltpu.SemaphoreType.DMA((WCH,)),
            pltpu.SemaphoreType.DMA((6,)),
            pltpu.SemaphoreType.DMA((12,)),
            pltpu.SemaphoreType.DMA((12,)),
            pltpu.SemaphoreType.DMA((4,)),
            pltpu.SemaphoreType.DMA((4,)),
        ],
        compiler_params=pltpu.CompilerParams(
            collective_id=0, has_side_effects=True, vmem_limit_bytes=48 * 1024 * 1024
        ),
        name="admm",
    )(
        scan_rows,
        scan_cols,
        sample_mask,
        object_field.reshape(512, 512),
        radon_weights,
        wave_field.reshape(256, 512),
        scaled_dual.reshape(256, 128),
        intensity.reshape(POS, 32, 128),
        jnp.concatenate([probe_field, probe_field], axis=2),
        tables,
        row_keys,
        col_keys,
    )
    return (
        wave_next.reshape(1, 2, 128, 128),
        probe_next,
        object_next.reshape(2, 2, 128, 512),
    )


def solution(mesh):
    specs = (
        P("aa", None, None, None),
        P("aa", None, None, "pb"),
        P("aa", "pb", None),
        P(),
        P("aa", "pb"),
        P("aa", "pb"),
        P("aa", "pb"),
        P(None, "aa", "pb", None),
        P(),
        P(),
        P(),
    )
    mapped = jax.shard_map(
        shards,
        mesh=mesh,
        in_specs=(P(),) + specs,
        out_specs=(P("aa", None, None, "pb"), P(), P(None, "aa", "pb", None)),
        check_vma=False,
    )

    def step(*arrays):
        return mapped(jnp.asarray(dft_constants()), *arrays)

    return step
```

```python
import math

import jax
import jax.numpy as jnp
import numpy as np
from jax import lax
from jax.experimental import pallas as pl
from jax.experimental.pallas import tpu as pltpu
from jax.sharding import PartitionSpec as P

BLK = 64
NW = 12
NB = 8
LIST = 12
AA = 64
PB = 4
ZC = 4
POS = 16
PAIRS = 8
OWN = 64 // PB
KEYS = 192
LAYER = 8
DEPTH = 8
SLOT = 40
SLOT2 = 32
WCH = 8
WROWS = 4096 // WCH
OUTS = 4

WAVE_STEP = 0.05
PENALTY = 1.0
PROBE_STEP = 0.05
OBJECT_STEP = 1.0

F32 = jnp.float32
BF16 = jnp.bfloat16


def dft_constants():
    index = np.arange(BLK)
    phase = (index[:, None] * index[None, :]) % BLK
    angle = phase.astype(np.float64) * (-2.0 * math.pi / BLK)
    f_re, f_im = np.cos(angle) / math.sqrt(BLK), np.sin(angle) / math.sqrt(BLK)
    pair = np.eye(2)

    def right(re, im):
        dre, dim = np.kron(pair, re), np.kron(pair, im)
        return np.block([[dre, dim], [-dim, dre]])

    def left(re, im):
        return np.block([[re, -im], [im, re]])

    order = np.concatenate([np.arange(0, BLK, 2), np.arange(1, BLK, 2)])
    rights = [right(f_re, f_im), right(f_re, -f_im)]
    lefts = np.concatenate(
        [left(f_re[order, :], f_im[order, :]), left(f_re[:, order], -f_im[:, order])], axis=1
    )
    return np.concatenate(rights + [lefts], axis=0).astype(np.float32)


def halves(value):
    high = value.astype(BF16)
    low = (value - high.astype(F32)).astype(BF16)
    return high, low


def dot(lhs, rhs):
    return jnp.dot(lhs, rhs, preferred_element_type=F32)


def right_apply(re, im, g_hi, g_lo):
    high, low = halves(jnp.concatenate([re, im], axis=1))
    out = dot(high, g_hi) + dot(low, g_hi) + dot(high, g_lo)
    return out[:, :128], out[:, 128:]


def left_apply(re, im, table):
    high, low = halves(jnp.concatenate([re, im], axis=0))
    out = dot(table, jnp.concatenate([high, low], axis=0))
    out = out[:128] + out[128:]
    return out[:64], out[64:]


def rows_to_lanes(value):
    return jnp.concatenate([value[q * 64 : (q + 1) * 64] for q in range(PAIRS)], axis=1)


def lanes_to_rows(value):
    return jnp.concatenate([value[:, q * 128 : (q + 1) * 128] for q in range(PAIRS)], axis=0)


def swap(value):
    return pltpu.roll(value, 64, 1)


def interleave(first, second):
    low = lax.broadcasted_iota(jnp.int32, first.shape, 1) < 64
    return jnp.where(low, first, swap(second)), jnp.where(low, swap(first), second)


def kernel(
    rows_ref,
    cols_ref,
    mask_ref,
    obj_hbm,
    wts_hbm,
    wave_hbm,
    dual_hbm,
    int_hbm,
    probe_hbm,
    tab_hbm,
    blocks_hbm,
    tables_hbm,
    wts,
    obj,
    wnext,
    pfull,
    table,
    wave,
    dual,
    int_raw,
    inten,
    probe,
    tab_raw,
    tab,
    blocks,
    tables,
    colkey,
    lhs,
    ptile,
    stk,
    hit_r,
    hit_c,
    win_r,
    win_i,
    gra_r,
    gra_i,
    pad,
    acc,
    share,
    base,
    send1,
    mid1,
    turn1,
    recv1,
    loose,
    send2,
    mid2,
    loose2,
    turn2,
    recv2,
    rays,
    spread,
    prow,
    in_sem,
    w_sem,
    x_send,
    x_recv,
    a_send,
    a_recv,
):
    me_a = lax.axis_index("aa")
    me_p = lax.axis_index("pb")
    z_own = me_a // LAYER
    m_own = me_a % LAYER
    z_base = z_own * LAYER

    def layer_peer(step):
        return z_base + lax.rem(m_own + step, LAYER)

    def depth_peer(step):
        return lax.rem(z_own + step, DEPTH) * LAYER + m_own

    def lanes(shape):
        return lax.broadcasted_iota(jnp.int32, shape, 1)

    obj_in = [
        pltpu.make_async_copy(
            obj_hbm.at[:, pl.ds(t * 128, 128)], obj.at[pl.ds(t * 512, 512)], in_sem.at[t]
        )
        for t in range(4)
    ]
    wts_in = [
        pltpu.make_async_copy(
            wts_hbm.at[pl.ds(c * WROWS, WROWS)], wts.at[pl.ds(c * WROWS, WROWS)], w_sem.at[c]
        )
        for c in range(WCH)
    ]
    wave_in = [
        pltpu.make_async_copy(
            wave_hbm.at[:, pl.ds(t * 128, 128)], wave.at[pl.ds(t * 256, 256)], in_sem.at[4 + t]
        )
        for t in range(4)
    ]
    others = {
        name: pltpu.make_async_copy(src, dst, in_sem.at[8 + n])
        for n, (name, src, dst) in enumerate(
            [
                ("blocks", blocks_hbm, blocks),
                ("tables", tables_hbm, tables),
                ("probe", probe_hbm, probe),
                ("tab", tab_hbm, tab_raw),
                ("inten", int_hbm, int_raw),
                ("dual", dual_hbm, dual),
            ]
        )
    }
    others["blocks"].start()
    others["tables"].start()
    for copy in obj_in + wts_in + wave_in:
        copy.start()
    for name in ("probe", "tab", "inten", "dual"):
        others[name].start()

    barrier = pltpu.get_barrier_semaphore()

    for step in range(1, LAYER):
        for peer in (layer_peer(step), depth_peer(step)):
            pl.semaphore_signal(
                barrier, inc=1, device_id={"aa": peer}, device_id_type=pl.DeviceIdType.MESH
            )
    for step in range(1, PB):
        pl.semaphore_signal(
            barrier,
            inc=1,
            device_id={"pb": lax.rem(me_p + step, PB)},
            device_id_type=pl.DeviceIdType.MESH,
        )

    others["blocks"].wait()
    others["tables"].wait()
    keys = []
    for jj in range(2):
        there = pl.ds(me_p * 2 + jj, LIST, stride=NB)
        block = blocks[there, :]
        keys.append((block // OWN) * KEYS + tables[there, :] * OWN + block % OWN)
    keys = jnp.concatenate(
        [jnp.concatenate(keys, axis=1), jnp.zeros((128 - LIST, 128), jnp.int32)], axis=0
    )
    keys = jnp.transpose(keys.astype(F32)).astype(jnp.int32)
    for t in range(6):
        column = lanes((128, 128)) + t * 128
        total = jnp.zeros((128, 128), F32)
        for e in range(LIST):
            total = total + jnp.where(keys[:, e : e + 1] == column, 1.0, 0.0)
        hit_r[:, t * 128 : (t + 1) * 128] = total.astype(BF16)

    for copy in obj_in:
        copy.wait()

    def fold(q, carry):
        for t in range(4):
            even = obj[pl.ds(t * 512 + 2 * q, 8, stride=64), :]
            odd = obj[pl.ds(t * 512 + 2 * q + 1, 8, stride=64), :]
            first, second = interleave(even, odd)
            at = pl.multiple_of(q * 64 + t * 16, 16)
            lhs[pl.ds(at, 16), :] = jnp.concatenate([first, second], axis=0)
        return carry

    lax.fori_loop(0, 32, fold, 0, unroll=4)
    products = jnp.zeros((64, 768), F32)
    per = 32 // WCH
    for c in range(WCH):
        wts_in[c].wait()
        part = jnp.concatenate(
            [lhs[(c * per + n) * 64 : (c * per + n + 1) * 64, :] for n in range(per)], axis=1
        ).astype(BF16)
        products = products + dot(part, wts[c * WROWS : (c + 1) * WROWS, :])
    for t in range(6):
        ptile[t * 64 : (t + 1) * 64, :] = products[:, t * 128 : (t + 1) * 128]
    own_stk = pl.multiple_of(me_p * KEYS, KEYS)
    for t in range(6):
        lists = [[], []], [[], []]
        for br in range(2):
            part = [ptile[pl.ds(t * 64 + cz * 2 + br, 8, stride=8), :] for cz in range(ZC)]
            for c in range(2):
                even, odd = interleave(part[2 * c], part[2 * c + 1])
                lists[0][c].append(even)
                lists[1][c].append(odd)
        for h in range(2):
            for c in range(2):
                stk[
                    pl.ds(pl.multiple_of(own_stk + (2 * t + h) * 16, 16), 16),
                    c * 128 : (c + 1) * 128,
                ] = jnp.concatenate(lists[h][c], axis=0).astype(BF16)

    pl.semaphore_wait(barrier, LAYER - 1 + DEPTH - 1 + PB - 1)

    def to_x(stage, step, src, dst):
        peer = lax.rem(me_p + step, PB)
        return pltpu.make_async_remote_copy(
            src_ref=src,
            dst_ref=dst,
            send_sem=x_send.at[stage * 3 + step - 1],
            recv_sem=x_recv.at[stage * 3 + step - 1],
            device_id={"pb": peer},
            device_id_type=pl.DeviceIdType.MESH,
        )

    own_block = stk.at[pl.ds(own_stk, KEYS)]
    gathers = [to_x(0, step, own_block, own_block) for step in range(1, PB)]
    for copy in gathers:
        copy.start()

    def scatter_rows(ref, slot, k, value):
        for h in range(8):
            ref[pl.ds(k * 8 + h, 8, stride=slot), :] = value[h * 8 : (h + 1) * 8]

    def turn_rows(source, target, slot):
        for h in range(8):
            target[h * slot : h * slot + 32, :] = jnp.concatenate(
                [source[pl.ds(k * 8 + h, 8, stride=slot), :] for k in range(4)], axis=0
            ).astype(target.dtype)

    def gather_rows(value, slot, k):
        return jnp.concatenate(
            [value[h * slot + k * 8 : h * slot + k * 8 + 8] for h in range(8)], axis=0
        )

    for copy in wave_in:
        copy.wait()

    def windows(q, carry):
        at = pl.multiple_of(q * 64, 64)
        for c, ref in ((0, win_r), (1, win_i)):
            found = []
            for h in range(2):
                row = rows_ref[0, 2 * q + h]
                col = cols_ref[0, 2 * q + h]
                tile = col // 128
                off = col % 128
                near = wave[pl.ds(tile * 256 + c * 128 + row, 64), :]
                far = wave[pl.ds(jnp.minimum(tile + 1, 3) * 256 + c * 128 + row, 64), :]
                both = jnp.where(lanes((64, 128)) >= off, near, far)
                found.append(pltpu.roll(both, (128 + 64 * h - off) % 128, 1))
            ref[pl.ds(at, 64), :] = jnp.where(lanes((64, 128)) < 64, found[0], found[1])
        return carry

    lax.fori_loop(0, PAIRS, windows, 0)
    others["probe"].wait()
    others["tab"].wait()
    others["inten"].wait()
    for octet in range(2):
        for t in range(32):
            inten[pl.ds(octet * 256 + t, 8, stride=32), :] = int_raw[
                octet * 8 : octet * 8 + 8, t * 128 : (t + 1) * 128
            ]
    for n in range(2):
        tab[2 * n], tab[2 * n + 1] = halves(tab_raw[n * 256 : (n + 1) * 256, :])
        high, low = halves(tab_raw[512:640, n * 128 : (n + 1) * 128])
        tab[4 + n] = jnp.concatenate(
            [jnp.concatenate([high] * 2, axis=1), jnp.concatenate([low] * 2, axis=1)], axis=0
        )
    one_re = jnp.concatenate([probe[0]] * 2, axis=1)
    one_im = jnp.concatenate([probe[1]] * 2, axis=1)
    p_re = jnp.concatenate([one_re] * PAIRS, axis=0)
    p_im = jnp.concatenate([one_im] * PAIRS, axis=0)
    w_re, w_im = win_r[...], win_i[...]
    half_re, half_im = right_apply(
        p_re * w_re - p_im * w_im, p_re * w_im + p_im * w_re, tab[0], tab[1]
    )
    far_re, far_im = left_apply(rows_to_lanes(half_re), rows_to_lanes(half_im), tab[4])
    measured, live = [], []
    for q in range(PAIRS):
        even, odd = interleave(
            inten[2 * q * 32 : 2 * q * 32 + 32, :], inten[2 * q * 32 + 32 : 2 * q * 32 + 64, :]
        )
        measured.append(jnp.concatenate([even, odd], axis=0))
        live.append(
            jnp.where(
                lanes((1, 128)) < 64, mask_ref[0, 2 * q].astype(F32), mask_ref[0, 2 * q + 1].astype(F32)
            )
        )
    measured = jnp.concatenate(measured, axis=1)
    live = jnp.concatenate(live, axis=1)
    factor = live * (far_re * far_re + far_im * far_im - measured)
    half_re, half_im = left_apply(factor * far_re, factor * far_im, tab[5])
    back_re, back_im = right_apply(lanes_to_rows(half_re), lanes_to_rows(half_im), tab[2], tab[3])
    gra_r[...] = p_re * back_re + p_im * back_im
    gra_i[...] = p_re * back_im - p_im * back_re
    grad_re = jnp.sum((w_re * back_re + w_im * back_im).reshape(PAIRS, 64, 128), axis=0)
    grad_im = jnp.sum((w_re * back_im - w_im * back_re).reshape(PAIRS, 64, 128), axis=0)
    grad_re = grad_re + swap(grad_re)
    grad_im = grad_im + swap(grad_im)
    scatter_rows(send1, SLOT, 4, jnp.where(lanes((64, 128)) < 64, grad_re, grad_im))

    pad[...] = jnp.zeros_like(pad)
    acc[...] = jnp.zeros_like(acc)

    def scatter(q, carry):
        at = pl.multiple_of(q * 64, 64)
        for h in range(2):
            row = rows_ref[0, 2 * q + h]
            col = cols_ref[0, 2 * q + h]
            turn = (col + 128 - 64 * h) % 128
            for c, ref in ((0, gra_r), (1, gra_i)):
                slot = (2 * h + c) * 192
                pad[slot + 64 : slot + 128, :] = pltpu.roll(ref[pl.ds(at, 64), :], turn, 1)
                moved = pad[pl.ds(slot + 64 - row, 128), :]
                for t in range(4):
                    place = lanes((128, 128)) + (t * 128 - col)
                    start = t * 256 + c * 128
                    acc[start : start + 128, :] = acc[start : start + 128, :] + jnp.where(
                        (place >= 0) & (place < 64), moved, 0.0
                    )
        return carry

    lax.fori_loop(0, PAIRS, scatter, 0)
    reduces = [
        to_x(
            1,
            step,
            acc.at[pl.ds(pl.multiple_of(lax.rem(me_p + step, PB) * 256, 256), 256)],
            share.at[pl.ds((step - 1) * 256, 256)],
        )
        for step in range(1, PB)
    ]
    for copy in reduces:
        copy.start()

    for copy in gathers:
        copy.wait_recv()
    projection = dot(hit_r[...], stk[...])
    for c in range(2):
        first, second = interleave(
            projection[:64, c * 128 : (c + 1) * 128], projection[64:, c * 128 : (c + 1) * 128]
        )
        scatter_rows(send1, SLOT, 2 * c, first)
        scatter_rows(send1, SLOT, 2 * c + 1, second)

    def to_a(stage, peer, src, dst):
        return pltpu.make_async_remote_copy(
            src_ref=src,
            dst_ref=dst,
            send_sem=a_send.at[stage],
            recv_sem=a_recv.at[stage],
            device_id={"aa": peer},
            device_id_type=pl.DeviceIdType.MESH,
        )

    def exchange(stage, source, target, slot, count):
        own = (m_own, z_own)[stage % 2]
        for step in range(1, 8):
            there = lax.rem(own + step, 8)
            to_a(
                stage,
                (layer_peer, depth_peer)[stage % 2](step),
                source.at[pl.ds(pl.multiple_of(there * slot, 8), count)],
                target.at[pl.ds(pl.multiple_of(own * slot, 8), count)],
            ).start()
        here = pl.ds(pl.multiple_of(own * slot, 16 if slot == SLOT2 else 8), count)
        target[here, :] = source[here, :]
        return to_a(
            stage,
            (layer_peer, depth_peer)[stage % 2](1),
            source.at[pl.ds(0, 7 * count)],
            target.at[pl.ds(0, 7 * count)],
        )

    moves = [exchange(0, send1, mid1, SLOT, SLOT)]

    for p in range(PB):
        parts = []
        for jj in range(2):
            there = pl.ds(p * 2 + jj, LIST, stride=NB)
            block = blocks[there, :]
            place = tables[there, :] * OWN + block % OWN
            parts.append(jnp.where(block // OWN == me_p, place, -1))
        colkey[:, p * 128 : (p + 1) * 128] = jnp.concatenate(parts, axis=1)
    for r in range(3):
        mine = lax.broadcasted_iota(jnp.int32, (64, 512), 0) + r * 64
        total = jnp.zeros((64, 512), F32)
        for e in range(LIST):
            total = total + jnp.where(colkey[e : e + 1, :] == mine, 1.0, 0.0)
        hit_c[r * 64 : (r + 1) * 64, :] = total.astype(BF16)

    moves[0].wait_recv()
    turn_rows(mid1, turn1, SLOT)
    partial = mid1[32:40, :]
    for l in range(1, 8):
        partial = partial + mid1[l * SLOT + 32 : l * SLOT + 40, :]
    turn1[pl.ds(32, 8, stride=SLOT), :] = partial
    moves.append(exchange(1, turn1, recv1, SLOT, 33))

    others["dual"].wait()
    own_cols = pl.ds(pl.multiple_of(me_p * 256, 256), 256)
    mine = wave[own_cols, :]
    for copy in reduces:
        copy.wait_recv()
    gradient = acc[own_cols, :] + share[0:256, :] + share[256:512, :] + share[512:768, :]
    base[...] = mine - WAVE_STEP * (gradient + PENALTY * (mine + dual[...]))

    moves[1].wait_recv()
    for c in range(2):
        for z in range(2):
            there = pl.ds(c * 128 + z, 64, stride=2)
            here = gather_rows(recv1, SLOT, 2 * c + z)
            moved = base[there, :] + (WAVE_STEP * PENALTY) * here
            wnext[there, :] = moved
            scatter_rows(loose, SLOT2, 2 * c + z, here - (moved + dual[there, :]))
    send2[...] = loose[...].astype(BF16)
    moves.append(exchange(2, send2, mid2, SLOT2, SLOT2))

    own_row = pl.ds(pl.multiple_of(me_p * 8, 8), 1)
    prow[own_row, :] = jnp.sum(recv1[pl.ds(32, 8, stride=SLOT), :], axis=0, keepdims=True)
    probe_x = [to_x(3, step, prow.at[own_row], prow.at[own_row]) for step in range(1, PB)]
    for copy in probe_x:
        copy.start()
    moves[2].wait_recv()
    loose2[...] = mid2[...].astype(F32)
    turn_rows(loose2, turn2, SLOT2)
    moves.append(exchange(3, turn2, recv2, SLOT2, SLOT2))

    for copy in probe_x:
        copy.wait_recv()
    pfull[pl.ds(me_a, 1), :] = (prow[0:1, :] + prow[8:9, :]) + (prow[16:17, :] + prow[24:25, :])

    def layer(step):
        row = pfull.at[pl.ds(me_a, 1)]
        return to_a(4, layer_peer(step), row, row)

    for step in range(1, LAYER):
        layer(step).start()

    moves[3].wait_recv()
    own_rays = pl.multiple_of(me_p * 128, 128)
    arrived = recv2[...].astype(F32)
    for c in range(2):
        first, second = interleave(
            gather_rows(arrived, SLOT2, 2 * c), gather_rows(arrived, SLOT2, 2 * c + 1)
        )
        rays[pl.ds(own_rays, 128), c * 128 : (c + 1) * 128] = jnp.concatenate(
            [first, second], axis=0
        ).astype(BF16)
    own_rows = rays.at[pl.ds(own_rays, 128)]
    ray_moves = [to_x(2, step, own_rows, own_rows) for step in range(1, PB)]
    for copy in ray_moves:
        copy.start()

    seven = pfull.at[pl.ds(0, LAYER - 1)]
    layer_all = to_a(4, layer_peer(1), seven, seven)
    layer_all.wait_recv()
    layer_all.wait_send()
    group = pfull.at[pl.ds(pl.multiple_of(z_base, 8), 8)]

    def stack(step):
        return to_a(5, depth_peer(step), group, group)

    for step in range(1, DEPTH):
        stack(step).start()

    for copy in ray_moves:
        copy.wait_recv()

    sums = dot(hit_c[...], rays[...]).astype(BF16).astype(F32)
    for t in range(6):
        for br in range(2):
            for c in range(2):
                at = 2 * t * 16 + br * 8
                first, second = interleave(
                    sums[at : at + 8, c * 128 : (c + 1) * 128],
                    sums[at + 16 : at + 24, c * 128 : (c + 1) * 128],
                )
                spread[pl.ds(t * 64 + 4 * c + br, 8, stride=8), :] = first
                spread[pl.ds(t * 64 + 4 * c + 2 + br, 8, stride=8), :] = second
    table[...] = jnp.concatenate(
        [spread[t * 64 : (t + 1) * 64, :] for t in range(6)], axis=1
    ).astype(BF16)

    others_all = pfull.at[pl.ds(0, 7 * LAYER)]
    stack_all = to_a(5, depth_peer(1), others_all, others_all)
    stack_all.wait_recv()
    stack_all.wait_send()
    for copy in gathers + reduces + probe_x + ray_moves:
        copy.wait_send()
    for copy in moves:
        copy.wait_send()


def tail(
    probe_hbm,
    wts,
    obj,
    wnext,
    pfull,
    table,
    wave_out,
    probe_out,
    obj_out,
    onew,
    probe,
    pout,
    sem,
):
    probe_in = pltpu.make_async_copy(probe_hbm, probe, sem.at[0])
    probe_in.start()
    wave_copy = pltpu.make_async_copy(wnext, wave_out, sem.at[1])
    wave_copy.start()

    probe_in.wait()
    scale = PROBE_STEP / (AA * POS * PB)
    pout[0] = probe[0] - scale * pfull[:, :64]
    pout[1] = probe[1] - scale * swap(pfull[...])[:, :64]
    probe_copy = pltpu.make_async_copy(pout, probe_out, sem.at[2])
    probe_copy.start()

    per = 32 // WCH
    rows = 64 // OUTS
    obj_copies = []
    for n in range(WCH):
        grad = lax.dot_general(
            table[...],
            wts[n * WROWS : (n + 1) * WROWS, :],
            (((1,), (1,)), ((), ())),
            preferred_element_type=F32,
        )
        for s in range(per):
            q = n * per + s
            for t in range(4):
                first, second = interleave(
                    grad[t * 16 : t * 16 + 8, s * 128 : (s + 1) * 128],
                    grad[t * 16 + 8 : t * 16 + 16, s * 128 : (s + 1) * 128],
                )
                even = pl.ds(t * 512 + 2 * q, 8, stride=64)
                odd = pl.ds(t * 512 + 2 * q + 1, 8, stride=64)
                onew[even, :] = obj[even, :] - OBJECT_STEP * first
                onew[odd, :] = obj[odd, :] - OBJECT_STEP * second
        if (n + 1) % (WCH // OUTS) == 0:
            part = pl.ds(n // (WCH // OUTS) * rows, rows)
            for t in range(4):
                copy = pltpu.make_async_copy(
                    onew.reshape(4, 8, 64, 128).at[t, :, part, :],
                    obj_out.at[:, part, pl.ds(t * 128, 128)],
                    sem.at[3 + len(obj_copies)],
                )
                copy.start()
                obj_copies.append(copy)
    wave_copy.wait()
    probe_copy.wait()
    for copy in obj_copies:
        copy.wait()


def shards(
    tables,
    wave_field,
    scaled_dual,
    intensity,
    probe_field,
    scan_rows,
    scan_cols,
    sample_mask,
    object_field,
    ray_blocks,
    ray_tables,
    radon_weights,
):
    smem = pl.BlockSpec(memory_space=pltpu.SMEM)
    vmem = pltpu.VMEM
    hbm_spec = pl.BlockSpec(memory_space=pltpu.HBM)
    vmem_spec = pl.BlockSpec(memory_space=pltpu.VMEM)
    kept = pl.pallas_call(
        kernel,
        out_shape=(
            pltpu.VMEM((4096, 768), BF16),
            pltpu.VMEM((2048, 128), F32),
            pltpu.VMEM((256, 128), F32),
            pltpu.VMEM((64, 128), F32),
            pltpu.VMEM((64, 768), BF16),
        ),
        in_specs=[smem] * 3 + [hbm_spec] * 9,
        out_specs=[vmem_spec] * 5,
        scratch_shapes=[
            vmem((1024, 128), F32),
            vmem((256, 128), F32),
            vmem((POS, 4096), F32),
            vmem((POS * 32, 128), F32),
            vmem((2, 64, 64), F32),
            vmem((640, 256), F32),
            vmem((6, 256, 256), BF16),
            vmem((LIST * NB, AA), jnp.int32),
            vmem((LIST * NB, AA), jnp.int32),
            vmem((LIST, 512), jnp.int32),
            vmem((2048, 128), F32),
            vmem((384, 128), F32),
            vmem((768, 256), BF16),
            vmem((128, 768), BF16),
            vmem((KEYS, 512), BF16),
            vmem((512, 128), F32),
            vmem((512, 128), F32),
            vmem((512, 128), F32),
            vmem((512, 128), F32),
            vmem((768, 128), F32),
            vmem((1024, 128), F32),
            vmem((768, 128), F32),
            vmem((256, 128), F32),
            vmem((8 * SLOT, 128), F32),
            vmem((8 * SLOT, 128), F32),
            vmem((8 * SLOT, 128), F32),
            vmem((8 * SLOT, 128), F32),
            vmem((256, 128), F32),
            vmem((256, 128), BF16),
            vmem((256, 128), BF16),
            vmem((256, 128), F32),
            vmem((256, 128), BF16),
            vmem((256, 128), BF16),
            vmem((512, 256), BF16),
            vmem((384, 128), F32),
            vmem((32, 128), F32),
            pltpu.SemaphoreType.DMA((14,)),
            pltpu.SemaphoreType.DMA((WCH,)),
            pltpu.SemaphoreType.DMA((12,)),
            pltpu.SemaphoreType.DMA((12,)),
            pltpu.SemaphoreType.DMA((6,)),
            pltpu.SemaphoreType.DMA((6,)),
        ],
        compiler_params=pltpu.CompilerParams(
            collective_id=0, has_side_effects=True, vmem_limit_bytes=54 * 1024 * 1024
        ),
        name="admm",
    )(
        scan_rows,
        scan_cols,
        sample_mask,
        object_field.reshape(512, 512),
        radon_weights,
        wave_field.reshape(256, 512),
        scaled_dual.reshape(256, 128),
        intensity.reshape(POS, 4096),
        probe_field,
        tables,
        ray_blocks.transpose(2, 1, 0).reshape(LIST * NB, AA),
        ray_tables.transpose(2, 1, 0).reshape(LIST * NB, AA),
    )
    wave_next, probe_next, object_next = pl.pallas_call(
        tail,
        out_shape=(
            jax.ShapeDtypeStruct((256, 128), F32),
            jax.ShapeDtypeStruct((2, 64, 64), F32),
            jax.ShapeDtypeStruct((8, 64, 512), F32),
        ),
        in_specs=[hbm_spec] + [vmem_spec] * 5,
        out_specs=[hbm_spec] * 3,
        scratch_shapes=[
            vmem((2048, 128), F32),
            vmem((2, 64, 64), F32),
            vmem((2, 64, 64), F32),
            pltpu.SemaphoreType.DMA((3 + 4 * OUTS,)),
        ],
        compiler_params=pltpu.CompilerParams(vmem_limit_bytes=16 * 1024 * 1024),
        name="tail",
    )(probe_field, *kept)
    return (
        wave_next.reshape(1, 2, 128, 128),
        probe_next,
        object_next.reshape(2, 2, 128, 512),
    )


def solution(mesh):
    specs = (
        P("aa", None, None, None),
        P("aa", None, None, "pb"),
        P("aa", "pb", None),
        P(),
        P("aa", "pb"),
        P("aa", "pb"),
        P("aa", "pb"),
        P(None, "aa", "pb", None),
        P(),
        P(),
        P(),
    )
    mapped = jax.shard_map(
        shards,
        mesh=mesh,
        in_specs=(P(),) + specs,
        out_specs=(P("aa", None, None, "pb"), P(), P(None, "aa", "pb", None)),
        check_vma=False,
    )

    def step(*arrays):
        return mapped(jnp.asarray(dft_constants()), *arrays)

    return step
```

```python
import math

import jax
import jax.numpy as jnp
import numpy as np
from jax import lax
from jax.experimental import pallas as pl
from jax.experimental.pallas import tpu as pltpu
from jax.sharding import PartitionSpec as P

BLK = 64
NW = 12
NB = 8
LIST = 12
AA = 64
PB = 4
ZC = 4
POS = 16
PAIRS = 8
OWN = 64 // PB
KEYS = 192
LAYER = 8
DEPTH = 8
ROWS = 4
CHIPS = 32
SLOT1 = 16
SLOT2 = 8
OFFSETS = sorted(
    [(dz, dy) for dz in range(DEPTH) for dy in range(ROWS) if dz + dy > 0],
    key=lambda o: (-min(o[0], DEPTH - o[0]) - min(o[1], ROWS - o[1]), o),
)
WCH = 8
WROWS = 4096 // WCH
WIDE = 384
OUTS = 4

WAVE_STEP = 0.05
PENALTY = 1.0
PROBE_STEP = 0.05
OBJECT_STEP = 1.0

F32 = jnp.float32
BF16 = jnp.bfloat16


def dft_constants():
    index = np.arange(BLK)
    phase = (index[:, None] * index[None, :]) % BLK
    angle = phase.astype(np.float64) * (-2.0 * math.pi / BLK)
    f_re, f_im = np.cos(angle) / math.sqrt(BLK), np.sin(angle) / math.sqrt(BLK)
    pair = np.eye(2)

    def right(re, im):
        dre, dim = np.kron(pair, re), np.kron(pair, im)
        return np.block([[dre, dim], [-dim, dre]])

    def left(re, im):
        return np.block([[re, -im], [im, re]])

    order = np.concatenate([np.arange(0, BLK, 2), np.arange(1, BLK, 2)])
    rights = [right(f_re, f_im), right(f_re, -f_im)]
    lefts = np.concatenate(
        [left(f_re[order, :], f_im[order, :]), left(f_re[:, order], -f_im[:, order])], axis=1
    )
    return np.concatenate(rights + [lefts], axis=0).astype(np.float32)


def halves(value):
    high = value.astype(BF16)
    low = (value - high.astype(F32)).astype(BF16)
    return high, low


def dot(lhs, rhs):
    return jnp.dot(lhs, rhs, preferred_element_type=F32)


def right_apply(re, im, g_hi, g_lo):
    high, low = halves(jnp.concatenate([re, im], axis=1))
    out = dot(high, g_hi) + dot(low, g_hi) + dot(high, g_lo)
    return out[:, :128], out[:, 128:]


def left_apply(re, im, table):
    high, low = halves(jnp.concatenate([re, im], axis=0))
    out = dot(table, jnp.concatenate([high, low], axis=0))
    out = out[:128] + out[128:]
    return out[:64], out[64:]


def rows_to_lanes(value):
    return jnp.concatenate([value[q * 64 : (q + 1) * 64] for q in range(PAIRS)], axis=1)


def lanes_to_rows(value):
    return jnp.concatenate([value[:, q * 128 : (q + 1) * 128] for q in range(PAIRS)], axis=0)


def swap(value):
    return pltpu.roll(value, 64, 1)


def interleave(first, second):
    low = lax.broadcasted_iota(jnp.int32, first.shape, 1) < 64
    return jnp.where(low, first, swap(second)), jnp.where(low, swap(first), second)


def kernel(
    rows_ref,
    cols_ref,
    mask_ref,
    obj_hbm,
    wts_hbm,
    wave_hbm,
    dual_hbm,
    int_hbm,
    probe_hbm,
    tab_hbm,
    blocks_hbm,
    tables_hbm,
    wts,
    obj,
    wnext,
    pfull,
    table,
    wave,
    dual,
    int_raw,
    inten,
    probe,
    tab_raw,
    tab,
    blocks,
    tables,
    colkey,
    lhs,
    ptile,
    stk,
    hit_r,
    hit_c,
    win_r,
    win_i,
    gra_r,
    gra_i,
    pad,
    acc,
    share,
    base,
    loose1,
    across1,
    arrived1,
    message1,
    recv1,
    loose2,
    across2,
    arrived2,
    message2,
    recv2,
    rays,
    spread,
    prow,
    in_sem,
    w_sem,
    x_send,
    x_recv,
    a_send,
    a_recv,
):
    me_a = lax.axis_index("aa")
    me_p = lax.axis_index("pb")
    core = me_a % 2
    chip = me_a // 2
    z_own = me_a // LAYER
    y_own = chip % ROWS
    z_base = z_own * LAYER
    sibling = me_a + 1 - 2 * core

    def chip_at(dz, dy):
        return lax.rem(z_own + dz, DEPTH) * ROWS + lax.rem(y_own + dy, ROWS)

    def lanes(shape):
        return lax.broadcasted_iota(jnp.int32, shape, 1)

    obj_in = [
        pltpu.make_async_copy(
            obj_hbm.at[:, pl.ds(t * 128, 128)], obj.at[pl.ds(t * 512, 512)], in_sem.at[t]
        )
        for t in range(4)
    ]
    wts_in = [
        pltpu.make_async_copy(
            wts_hbm.at[pl.ds(c * 1024, 1024), pl.ds(h * WIDE, WIDE)],
            wts.at[pl.ds(c * 1024, 1024), pl.ds(h * WIDE, WIDE)],
            w_sem.at[h * 4 + c],
        )
        for h in range(2)
        for c in range(4)
    ]
    wave_in = [
        pltpu.make_async_copy(
            wave_hbm.at[:, pl.ds(t * 128, 128)], wave.at[pl.ds(t * 256, 256)], in_sem.at[4 + t]
        )
        for t in range(4)
    ]
    others = {
        name: pltpu.make_async_copy(src, dst, in_sem.at[8 + n])
        for n, (name, src, dst) in enumerate(
            [
                ("blocks", blocks_hbm, blocks),
                ("tables", tables_hbm, tables),
                ("probe", probe_hbm, probe),
                ("tab", tab_hbm, tab_raw),
                ("inten", int_hbm, int_raw),
                ("dual", dual_hbm, dual),
            ]
        )
    }
    others["blocks"].start()
    others["tables"].start()
    for copy in obj_in + wts_in + wave_in:
        copy.start()
    for name in ("probe", "tab", "inten", "dual"):
        others[name].start()

    barrier = pltpu.get_barrier_semaphore()

    for step in range(1, PB):
        pl.semaphore_signal(
            barrier,
            inc=1,
            device_id={"pb": lax.rem(me_p + step, PB)},
            device_id_type=pl.DeviceIdType.MESH,
        )
    for peer in [chip_at(dz, dy) * 2 + core for dz, dy in OFFSETS] + [sibling]:
        pl.semaphore_signal(
            barrier, inc=1, device_id={"aa": peer}, device_id_type=pl.DeviceIdType.MESH
        )

    others["blocks"].wait()
    others["tables"].wait()
    keys = []
    for jj in range(2):
        there = pl.ds(me_p * 2 + jj, LIST, stride=NB)
        block = blocks[there, :]
        keys.append((block // OWN) * KEYS + tables[there, :] * OWN + block % OWN)
    keys = jnp.concatenate(
        [jnp.concatenate(keys, axis=1), jnp.zeros((128 - LIST, 128), jnp.int32)], axis=0
    )
    keys = jnp.transpose(keys.astype(F32)).astype(jnp.int32)
    for t in range(6):
        column = lanes((128, 128)) + t * 128
        total = jnp.zeros((128, 128), F32)
        for e in range(LIST):
            total = total + jnp.where(keys[:, e : e + 1] == column, 1.0, 0.0)
        hit_r[:, t * 128 : (t + 1) * 128] = total.astype(BF16)

    for copy in obj_in:
        copy.wait()

    def fold(q, carry):
        for t in range(4):
            even = obj[pl.ds(t * 512 + 2 * q, 8, stride=64), :]
            odd = obj[pl.ds(t * 512 + 2 * q + 1, 8, stride=64), :]
            first, second = interleave(even, odd)
            at = pl.multiple_of(q * 64 + t * 16, 16)
            lhs[pl.ds(at, 16), :] = jnp.concatenate([first, second], axis=0)
        return carry

    lax.fori_loop(0, 32, fold, 0, unroll=4)
    own_stk = pl.multiple_of(me_p * KEYS, KEYS)

    def to_x(stage, step, src, dst):
        peer = lax.rem(me_p + step, PB)
        return pltpu.make_async_remote_copy(
            src_ref=src,
            dst_ref=dst,
            send_sem=x_send.at[stage * 3 + step - 1],
            recv_sem=x_recv.at[stage * 3 + step - 1],
            device_id={"pb": peer},
            device_id_type=pl.DeviceIdType.MESH,
        )

    gathers = []
    for half in range(2):
        products = jnp.zeros((64, WIDE), F32)
        for c in range(4):
            wts_in[half * 4 + c].wait()
            part = jnp.concatenate(
                [lhs[(c * 8 + n) * 64 : (c * 8 + n + 1) * 64, :] for n in range(8)], axis=1
            ).astype(BF16)
            products = products + dot(
                part, wts[c * 1024 : (c + 1) * 1024, half * WIDE : (half + 1) * WIDE]
            )
        for i in range(3):
            t = half * 3 + i
            ptile[t * 64 : (t + 1) * 64, :] = products[:, i * 128 : (i + 1) * 128]
            lists = [[], []], [[], []]
            for br in range(2):
                part = [ptile[pl.ds(t * 64 + cz * 2 + br, 8, stride=8), :] for cz in range(ZC)]
                for c in range(2):
                    even, odd = interleave(part[2 * c], part[2 * c + 1])
                    lists[0][c].append(even)
                    lists[1][c].append(odd)
            for h in range(2):
                for c in range(2):
                    stk[
                        pl.ds(pl.multiple_of(own_stk + (2 * t + h) * 16, 16), 16),
                        c * 128 : (c + 1) * 128,
                    ] = jnp.concatenate(lists[h][c], axis=0).astype(BF16)
        if half == 0:
            pl.semaphore_wait(barrier, CHIPS + PB - 1)
        own_block = stk.at[pl.ds(pl.multiple_of(own_stk + half * 96, 96), 96)]
        for step in (2, 1, 3):
            copy = to_x(4 * half, step, own_block, own_block)
            copy.start()
            gathers.append(copy)

    for copy in wave_in:
        copy.wait()

    def windows(q, carry):
        at = pl.multiple_of(q * 64, 64)
        for c, ref in ((0, win_r), (1, win_i)):
            found = []
            for h in range(2):
                row = rows_ref[0, 2 * q + h]
                col = cols_ref[0, 2 * q + h]
                tile = col // 128
                off = col % 128
                near = wave[pl.ds(tile * 256 + c * 128 + row, 64), :]
                far = wave[pl.ds(jnp.minimum(tile + 1, 3) * 256 + c * 128 + row, 64), :]
                both = jnp.where(lanes((64, 128)) >= off, near, far)
                found.append(pltpu.roll(both, (128 + 64 * h - off) % 128, 1))
            ref[pl.ds(at, 64), :] = jnp.where(lanes((64, 128)) < 64, found[0], found[1])
        return carry

    lax.fori_loop(0, PAIRS, windows, 0)
    others["probe"].wait()
    others["tab"].wait()
    others["inten"].wait()
    for octet in range(2):
        for t in range(32):
            inten[pl.ds(octet * 256 + t, 8, stride=32), :] = int_raw[
                octet * 8 : octet * 8 + 8, t * 128 : (t + 1) * 128
            ]
    for n in range(2):
        tab[2 * n], tab[2 * n + 1] = halves(tab_raw[n * 256 : (n + 1) * 256, :])
        high, low = halves(tab_raw[512:640, n * 128 : (n + 1) * 128])
        tab[4 + n] = jnp.concatenate(
            [jnp.concatenate([high] * 2, axis=1), jnp.concatenate([low] * 2, axis=1)], axis=0
        )
    one_re = jnp.concatenate([probe[0]] * 2, axis=1)
    one_im = jnp.concatenate([probe[1]] * 2, axis=1)
    p_re = jnp.concatenate([one_re] * PAIRS, axis=0)
    p_im = jnp.concatenate([one_im] * PAIRS, axis=0)
    w_re, w_im = win_r[...], win_i[...]
    half_re, half_im = right_apply(
        p_re * w_re - p_im * w_im, p_re * w_im + p_im * w_re, tab[0], tab[1]
    )
    far_re, far_im = left_apply(rows_to_lanes(half_re), rows_to_lanes(half_im), tab[4])
    measured, live = [], []
    for q in range(PAIRS):
        even, odd = interleave(
            inten[2 * q * 32 : 2 * q * 32 + 32, :], inten[2 * q * 32 + 32 : 2 * q * 32 + 64, :]
        )
        measured.append(jnp.concatenate([even, odd], axis=0))
        live.append(
            jnp.where(
                lanes((1, 128)) < 64, mask_ref[0, 2 * q].astype(F32), mask_ref[0, 2 * q + 1].astype(F32)
            )
        )
    measured = jnp.concatenate(measured, axis=1)
    live = jnp.concatenate(live, axis=1)
    factor = live * (far_re * far_re + far_im * far_im - measured)
    half_re, half_im = left_apply(factor * far_re, factor * far_im, tab[5])
    back_re, back_im = right_apply(lanes_to_rows(half_re), lanes_to_rows(half_im), tab[2], tab[3])
    gra_r[...] = p_re * back_re + p_im * back_im
    gra_i[...] = p_re * back_im - p_im * back_re
    grad_re = jnp.sum((w_re * back_re + w_im * back_im).reshape(PAIRS, 64, 128), axis=0)
    grad_im = jnp.sum((w_re * back_im - w_im * back_re).reshape(PAIRS, 64, 128), axis=0)
    grad_re = grad_re + swap(grad_re)
    grad_im = grad_im + swap(grad_im)
    loose1[256:320, :] = jnp.where(lanes((64, 128)) < 64, grad_re, grad_im)

    pad[...] = jnp.zeros_like(pad)
    acc[...] = jnp.zeros_like(acc)

    def scatter(q, carry):
        at = pl.multiple_of(q * 64, 64)
        for h in range(2):
            row = rows_ref[0, 2 * q + h]
            col = cols_ref[0, 2 * q + h]
            turn = (col + 128 - 64 * h) % 128
            for c, ref in ((0, gra_r), (1, gra_i)):
                slot = (2 * h + c) * 192
                pad[slot + 64 : slot + 128, :] = pltpu.roll(ref[pl.ds(at, 64), :], turn, 1)
                moved = pad[pl.ds(slot + 64 - row, 128), :]
                for t in range(4):
                    place = lanes((128, 128)) + (t * 128 - col)
                    start = t * 256 + c * 128
                    acc[start : start + 128, :] = acc[start : start + 128, :] + jnp.where(
                        (place >= 0) & (place < 64), moved, 0.0
                    )
        return carry

    lax.fori_loop(0, PAIRS, scatter, 0)
    reduces = [
        to_x(
            1,
            step,
            acc.at[pl.ds(pl.multiple_of(lax.rem(me_p + step, PB) * 256, 256), 256)],
            share.at[pl.ds((step - 1) * 256, 256)],
        )
        for step in range(1, PB)
    ]
    for copy in reduces:
        copy.start()

    for copy in gathers:
        copy.wait_recv()
    projection = dot(hit_r[...], stk[...])
    for c in range(2):
        first, second = interleave(
            projection[:64, c * 128 : (c + 1) * 128], projection[64:, c * 128 : (c + 1) * 128]
        )
        loose1[2 * c * 64 : 2 * c * 64 + 64, :] = first
        loose1[2 * c * 64 + 64 : 2 * c * 64 + 128, :] = second

    def to_a(stage, peer, src, dst):
        return pltpu.make_async_remote_copy(
            src_ref=src,
            dst_ref=dst,
            send_sem=a_send.at[stage],
            recv_sem=a_recv.at[stage],
            device_id={"aa": peer},
            device_id_type=pl.DeviceIdType.MESH,
        )

    def exchange(stage, loose, across, arrived, message, target, slot, count):
        rows = 160 if slot == SLOT1 else 128
        for k in range(rows // 32):
            across[k * 32 : k * 32 + 32, :] = loose[pl.ds(k * 64 + 1 - core, 32, stride=2), :]
        swapped = to_a(stage, sibling, across.at[pl.ds(0, rows)], arrived.at[pl.ds(0, rows)])
        swapped.start()
        for k in range(4):
            message[pl.ds(core * 4 + k, 32, stride=slot), :] = loose[
                pl.ds(k * 64 + core, 32, stride=2), :
            ]
        swapped.wait_recv()
        for k in range(4):
            message[pl.ds((1 - core) * 4 + k, 32, stride=slot), :] = arrived[
                k * 32 : k * 32 + 32, :
            ]
        if slot == SLOT1:
            message[pl.ds(8, 32, stride=slot), :] = (
                loose[pl.ds(256 + core, 32, stride=2), :] + arrived[128:160, :]
            )
        here = pl.ds(pl.multiple_of(chip * slot, 8), count)
        for dz, dy in OFFSETS:
            there = chip_at(dz, dy)
            to_a(
                stage + 1,
                there * 2 + core,
                message.at[pl.ds(pl.multiple_of(there * slot, 8), count)],
                target.at[here],
            ).start()
        target[here, :] = message[here, :]
        rows = (CHIPS - 1) * count
        moved = to_a(
            stage + 1,
            chip_at(0, 1) * 2 + core,
            message.at[pl.ds(0, rows)],
            target.at[pl.ds(0, rows)],
        )
        return [swapped, moved]

    moves = exchange(0, loose1, across1, arrived1, message1, recv1, SLOT1, 9)

    for p in range(PB):
        parts = []
        for jj in range(2):
            there = pl.ds(p * 2 + jj, LIST, stride=NB)
            block = blocks[there, :]
            place = tables[there, :] * OWN + block % OWN
            parts.append(jnp.where(block // OWN == me_p, place, -1))
        colkey[:, p * 128 : (p + 1) * 128] = jnp.concatenate(parts, axis=1)
    for r in range(3):
        mine = lax.broadcasted_iota(jnp.int32, (64, 512), 0) + r * 64
        total = jnp.zeros((64, 512), F32)
        for e in range(LIST):
            total = total + jnp.where(colkey[e : e + 1, :] == mine, 1.0, 0.0)
        hit_c[r * 64 : (r + 1) * 64, :] = total.astype(BF16)

    others["dual"].wait()
    own_cols = pl.ds(pl.multiple_of(me_p * 256, 256), 256)
    mine = wave[own_cols, :]
    for copy in reduces:
        copy.wait_recv()
    gradient = acc[own_cols, :] + share[0:256, :] + share[256:512, :] + share[512:768, :]
    base[...] = mine - WAVE_STEP * (gradient + PENALTY * (mine + dual[...]))

    moves[1].wait_recv()
    for half in range(2):
        for c in range(2):
            for z in range(2):
                k = 2 * c + z
                there = pl.ds(c * 128 + 2 * half + z, 32, stride=4)
                here = recv1[pl.ds(half * 4 + k, 32, stride=SLOT1), :]
                moved = base[there, :] + (WAVE_STEP * PENALTY) * here
                wnext[there, :] = moved
                misfit = here - (moved + dual[there, :])
                loose2[pl.ds(k * 64 + half, 32, stride=2), :] = misfit.astype(BF16).astype(F32)
    moves += exchange(2, loose2, across2, arrived2, message2, recv2, SLOT2, 8)

    own_row = pl.ds(pl.multiple_of(me_p * 8, 8), 1)
    prow[own_row, :] = jnp.sum(recv1[pl.ds(8, 32, stride=SLOT1), :], axis=0, keepdims=True)
    probe_x = [to_x(3, step, prow.at[own_row], prow.at[own_row]) for step in range(1, PB)]
    for copy in probe_x:
        copy.start()
    for copy in probe_x:
        copy.wait_recv()
    pfull[pl.ds(me_a, 1), :] = (prow[0:1, :] + prow[8:9, :]) + (prow[16:17, :] + prow[24:25, :])

    own_row = pfull.at[pl.ds(me_a, 1)]
    probe_core = to_a(4, sibling, own_row, own_row)
    probe_core.start()
    probe_core.wait_recv()
    two = pfull.at[pl.ds(chip * 2, 2)]
    for step in range(1, ROWS):
        to_a(5, chip_at(0, step) * 2 + core, two, two).start()

    moves[3].wait_recv()
    own_rays = pl.multiple_of(me_p * 128, 128)
    for c in range(2):
        first, second = interleave(
            recv2[pl.ds(2 * c, 64, stride=4), :], recv2[pl.ds(2 * c + 1, 64, stride=4), :]
        )
        rays[pl.ds(own_rays, 128), c * 128 : (c + 1) * 128] = jnp.concatenate(
            [first, second], axis=0
        ).astype(BF16)
    own_rows = rays.at[pl.ds(own_rays, 128)]
    ray_moves = [to_x(2, step, own_rows, own_rows) for step in range(1, PB)]
    for copy in ray_moves:
        copy.start()

    six = pfull.at[pl.ds(0, 6)]
    layer_all = to_a(5, chip_at(0, 1) * 2 + core, six, six)
    layer_all.wait_recv()
    group = pfull.at[pl.ds(pl.multiple_of(z_base, 8), 8)]

    def stack(step):
        return to_a(6, chip_at(step, 0) * 2 + core, group, group)

    for step in range(1, DEPTH):
        stack(step).start()

    for copy in ray_moves:
        copy.wait_recv()

    sums = dot(hit_c[...], rays[...]).astype(BF16).astype(F32)
    for t in range(6):
        for br in range(2):
            for c in range(2):
                at = 2 * t * 16 + br * 8
                first, second = interleave(
                    sums[at : at + 8, c * 128 : (c + 1) * 128],
                    sums[at + 16 : at + 24, c * 128 : (c + 1) * 128],
                )
                spread[pl.ds(t * 64 + 4 * c + br, 8, stride=8), :] = first
                spread[pl.ds(t * 64 + 4 * c + 2 + br, 8, stride=8), :] = second
    table[...] = jnp.concatenate(
        [spread[t * 64 : (t + 1) * 64, :] for t in range(6)], axis=1
    ).astype(BF16)

    others_all = pfull.at[pl.ds(0, 7 * LAYER)]
    stack_all = to_a(6, chip_at(1, 0) * 2 + core, others_all, others_all)
    stack_all.wait_recv()
    stack_all.wait_send()
    for copy in gathers + reduces + probe_x + ray_moves:
        copy.wait_send()
    for copy in moves + [probe_core, layer_all]:
        copy.wait_send()


def tail(
    probe_hbm,
    wts,
    obj,
    wnext,
    pfull,
    table,
    wave_out,
    probe_out,
    obj_out,
    onew,
    probe,
    pout,
    sem,
):
    probe_in = pltpu.make_async_copy(probe_hbm, probe, sem.at[0])
    probe_in.start()
    wave_copy = pltpu.make_async_copy(wnext, wave_out, sem.at[1])
    wave_copy.start()

    probe_in.wait()
    scale = PROBE_STEP / (AA * POS * PB)
    pout[0] = probe[0] - scale * pfull[:, :64]
    pout[1] = probe[1] - scale * swap(pfull[...])[:, :64]
    probe_copy = pltpu.make_async_copy(pout, probe_out, sem.at[2])
    probe_copy.start()

    per = 32 // WCH
    rows = 64 // OUTS
    obj_copies = []
    for n in range(WCH):
        grad = lax.dot_general(
            table[...],
            wts[n * WROWS : (n + 1) * WROWS, :],
            (((1,), (1,)), ((), ())),
            preferred_element_type=F32,
        )
        for s in range(per):
            q = n * per + s
            for t in range(4):
                first, second = interleave(
                    grad[t * 16 : t * 16 + 8, s * 128 : (s + 1) * 128],
                    grad[t * 16 + 8 : t * 16 + 16, s * 128 : (s + 1) * 128],
                )
                even = pl.ds(t * 512 + 2 * q, 8, stride=64)
                odd = pl.ds(t * 512 + 2 * q + 1, 8, stride=64)
                onew[even, :] = obj[even, :] - OBJECT_STEP * first
                onew[odd, :] = obj[odd, :] - OBJECT_STEP * second
        if (n + 1) % (WCH // OUTS) == 0:
            part = pl.ds(n // (WCH // OUTS) * rows, rows)
            for t in range(4):
                copy = pltpu.make_async_copy(
                    onew.reshape(4, 8, 64, 128).at[t, :, part, :],
                    obj_out.at[:, part, pl.ds(t * 128, 128)],
                    sem.at[3 + len(obj_copies)],
                )
                copy.start()
                obj_copies.append(copy)
    wave_copy.wait()
    probe_copy.wait()
    for copy in obj_copies:
        copy.wait()


def shards(
    tables,
    wave_field,
    scaled_dual,
    intensity,
    probe_field,
    scan_rows,
    scan_cols,
    sample_mask,
    object_field,
    ray_blocks,
    ray_tables,
    radon_weights,
):
    smem = pl.BlockSpec(memory_space=pltpu.SMEM)
    vmem = pltpu.VMEM
    hbm_spec = pl.BlockSpec(memory_space=pltpu.HBM)
    vmem_spec = pl.BlockSpec(memory_space=pltpu.VMEM)
    kept = pl.pallas_call(
        kernel,
        out_shape=(
            pltpu.VMEM((4096, 768), BF16),
            pltpu.VMEM((2048, 128), F32),
            pltpu.VMEM((256, 128), F32),
            pltpu.VMEM((64, 128), F32),
            pltpu.VMEM((64, 768), BF16),
        ),
        in_specs=[smem] * 3 + [hbm_spec] * 9,
        out_specs=[vmem_spec] * 5,
        scratch_shapes=[
            vmem((1024, 128), F32),
            vmem((256, 128), F32),
            vmem((POS, 4096), F32),
            vmem((POS * 32, 128), F32),
            vmem((2, 64, 64), F32),
            vmem((640, 256), F32),
            vmem((6, 256, 256), BF16),
            vmem((LIST * NB, AA), jnp.int32),
            vmem((LIST * NB, AA), jnp.int32),
            vmem((LIST, 512), jnp.int32),
            vmem((2048, 128), F32),
            vmem((384, 128), F32),
            vmem((768, 256), BF16),
            vmem((128, 768), BF16),
            vmem((KEYS, 512), BF16),
            vmem((512, 128), F32),
            vmem((512, 128), F32),
            vmem((512, 128), F32),
            vmem((512, 128), F32),
            vmem((768, 128), F32),
            vmem((1024, 128), F32),
            vmem((768, 128), F32),
            vmem((256, 128), F32),
            vmem((320, 128), F32),
            vmem((160, 128), F32),
            vmem((160, 128), F32),
            vmem((CHIPS * SLOT1, 128), F32),
            vmem((CHIPS * SLOT1, 128), F32),
            vmem((256, 128), F32),
            vmem((128, 128), F32),
            vmem((128, 128), F32),
            vmem((CHIPS * SLOT2, 128), F32),
            vmem((CHIPS * SLOT2, 128), F32),
            vmem((512, 256), BF16),
            vmem((384, 128), F32),
            vmem((32, 128), F32),
            pltpu.SemaphoreType.DMA((14,)),
            pltpu.SemaphoreType.DMA((WCH,)),
            pltpu.SemaphoreType.DMA((15,)),
            pltpu.SemaphoreType.DMA((15,)),
            pltpu.SemaphoreType.DMA((7,)),
            pltpu.SemaphoreType.DMA((7,)),
        ],
        compiler_params=pltpu.CompilerParams(
            collective_id=0, has_side_effects=True, vmem_limit_bytes=54 * 1024 * 1024
        ),
        name="admm",
    )(
        scan_rows,
        scan_cols,
        sample_mask,
        object_field.reshape(512, 512),
        radon_weights,
        wave_field.reshape(256, 512),
        scaled_dual.reshape(256, 128),
        intensity.reshape(POS, 4096),
        probe_field,
        tables,
        ray_blocks.transpose(2, 1, 0).reshape(LIST * NB, AA),
        ray_tables.transpose(2, 1, 0).reshape(LIST * NB, AA),
    )
    wave_next, probe_next, object_next = pl.pallas_call(
        tail,
        out_shape=(
            jax.ShapeDtypeStruct((256, 128), F32),
            jax.ShapeDtypeStruct((2, 64, 64), F32),
            jax.ShapeDtypeStruct((8, 64, 512), F32),
        ),
        in_specs=[hbm_spec] + [vmem_spec] * 5,
        out_specs=[hbm_spec] * 3,
        scratch_shapes=[
            vmem((2048, 128), F32),
            vmem((2, 64, 64), F32),
            vmem((2, 64, 64), F32),
            pltpu.SemaphoreType.DMA((3 + 4 * OUTS,)),
        ],
        compiler_params=pltpu.CompilerParams(vmem_limit_bytes=16 * 1024 * 1024),
        name="tail",
    )(probe_field, *kept)
    return (
        wave_next.reshape(1, 2, 128, 128),
        probe_next,
        object_next.reshape(2, 2, 128, 512),
    )


def solution(mesh):
    specs = (
        P("aa", None, None, None),
        P("aa", None, None, "pb"),
        P("aa", "pb", None),
        P(),
        P("aa", "pb"),
        P("aa", "pb"),
        P("aa", "pb"),
        P(None, "aa", "pb", None),
        P(),
        P(),
        P(),
    )
    mapped = jax.shard_map(
        shards,
        mesh=mesh,
        in_specs=(P(),) + specs,
        out_specs=(P("aa", None, None, "pb"), P(), P(None, "aa", "pb", None)),
        check_vma=False,
    )

    def step(*arrays):
        return mapped(jnp.asarray(dft_constants()), *arrays)

    return step
```

```python
import math

import jax
import jax.numpy as jnp
import numpy as np
from jax import lax
from jax.experimental import pallas as pl
from jax.experimental.pallas import tpu as pltpu
from jax.sharding import PartitionSpec as P

BLK = 64
NW = 12
NB = 8
LIST = 12
AA = 64
PB = 4
ZC = 4
POS = 16
PAIRS = 8
OWN = 64 // PB
KEYS = 192
LAYER = 8
DEPTH = 8
ROWS = 4
CHIPS = 32
SLOT = 16
SHARE = 272
OFFSETS = sorted(
    [(dz, dy) for dz in range(DEPTH) for dy in range(ROWS) if dz + dy > 0],
    key=lambda o: (-min(o[0], DEPTH - o[0]) - min(o[1], ROWS - o[1]), o),
)
WCH = 8
WROWS = 4096 // WCH
WIDE = 384

WAVE_STEP = 0.05
PENALTY = 1.0
PROBE_STEP = 0.05
OBJECT_STEP = 1.0

F32 = jnp.float32
BF16 = jnp.bfloat16


def dft_constants():
    index = np.arange(BLK)
    phase = (index[:, None] * index[None, :]) % BLK
    angle = phase.astype(np.float64) * (-2.0 * math.pi / BLK)
    f_re, f_im = np.cos(angle) / math.sqrt(BLK), np.sin(angle) / math.sqrt(BLK)
    pair = np.eye(2)

    def right(re, im):
        dre, dim = np.kron(pair, re), np.kron(pair, im)
        return np.block([[dre, dim], [-dim, dre]])

    def left(re, im):
        return np.block([[re, -im], [im, re]])

    order = np.concatenate([np.arange(0, BLK, 2), np.arange(1, BLK, 2)])
    rights = [right(f_re, f_im), right(f_re, -f_im)]
    lefts = np.concatenate(
        [left(f_re[order, :], f_im[order, :]), left(f_re[:, order], -f_im[:, order])], axis=1
    )
    return np.concatenate(rights + [lefts], axis=0).astype(np.float32)


def halves(value):
    high = value.astype(BF16)
    low = (value - high.astype(F32)).astype(BF16)
    return high, low


def dot(lhs, rhs):
    return jnp.dot(lhs, rhs, preferred_element_type=F32)


def right_apply(re, im, g_hi, g_lo):
    high, low = halves(jnp.concatenate([re, im], axis=1))
    out = dot(high, g_hi) + dot(low, g_hi) + dot(high, g_lo)
    return out[:, :128], out[:, 128:]


def left_apply(re, im, table):
    high, low = halves(jnp.concatenate([re, im], axis=0))
    out = dot(table, jnp.concatenate([high, low], axis=0))
    out = out[:128] + out[128:]
    return out[:64], out[64:]


def rows_to_lanes(value):
    return jnp.concatenate([value[q * 64 : (q + 1) * 64] for q in range(PAIRS)], axis=1)


def lanes_to_rows(value):
    return jnp.concatenate([value[:, q * 128 : (q + 1) * 128] for q in range(PAIRS)], axis=0)


def swap(value):
    return pltpu.roll(value, 64, 1)


def interleave(first, second):
    low = lax.broadcasted_iota(jnp.int32, first.shape, 1) < 64
    return jnp.where(low, first, swap(second)), jnp.where(low, swap(first), second)


def kernel(
    rows_ref,
    cols_ref,
    mask_ref,
    obj_hbm,
    wts_hbm,
    wave_hbm,
    dual_hbm,
    int_hbm,
    probe_hbm,
    tab_hbm,
    blocks_hbm,
    tables_hbm,
    wnext,
    pnext,
    onew,
    wts,
    obj,
    wave,
    dual,
    int_raw,
    inten,
    probe,
    tab_raw,
    tab,
    blocks,
    tables,
    colkey,
    lhs,
    ptile,
    stk,
    hit_r,
    hit_c,
    win_r,
    win_i,
    gra_r,
    gra_i,
    pad,
    acc,
    share,
    base,
    loose1,
    across1,
    arrived1,
    message1,
    recv1,
    loose2,
    misfit,
    across2,
    arrived2,
    message2,
    recv2,
    rays,
    spread,
    prow,
    in_sem,
    w_sem,
    x_send,
    x_recv,
    a_send,
    a_recv,
):
    me_a = lax.axis_index("aa")
    me_p = lax.axis_index("pb")
    core = me_a % 2
    chip = me_a // 2
    z_own = me_a // LAYER
    y_own = chip % ROWS
    z_base = z_own * LAYER
    sibling = me_a + 1 - 2 * core

    def chip_at(dz, dy):
        return lax.rem(z_own + dz, DEPTH) * ROWS + lax.rem(y_own + dy, ROWS)

    def lanes(shape):
        return lax.broadcasted_iota(jnp.int32, shape, 1)

    obj_in = [
        pltpu.make_async_copy(
            obj_hbm.at[:, pl.ds(t * 128, 128)], obj.at[pl.ds(t * 512, 512)], in_sem.at[t]
        )
        for t in range(4)
    ]
    wts_in = [
        pltpu.make_async_copy(
            wts_hbm.at[pl.ds(c * 1024, 1024), pl.ds(h * WIDE, WIDE)],
            wts.at[pl.ds(c * 1024, 1024), pl.ds(h * WIDE, WIDE)],
            w_sem.at[h * 4 + c],
        )
        for h in range(2)
        for c in range(4)
    ]
    wave_in = [
        pltpu.make_async_copy(
            wave_hbm.at[:, pl.ds(t * 128, 128)], wave.at[pl.ds(t * 256, 256)], in_sem.at[4 + t]
        )
        for t in range(4)
    ]
    others = {
        name: pltpu.make_async_copy(src, dst, in_sem.at[8 + n])
        for n, (name, src, dst) in enumerate(
            [
                ("blocks", blocks_hbm, blocks),
                ("tables", tables_hbm, tables),
                ("probe", probe_hbm, probe),
                ("tab", tab_hbm, tab_raw),
                ("inten", int_hbm, int_raw),
                ("dual", dual_hbm, dual),
            ]
        )
    }
    for copy in wave_in:
        copy.start()
    for name in ("probe", "tab", "inten"):
        others[name].start()
    for copy in obj_in + wts_in:
        copy.start()
    for name in ("dual", "blocks", "tables"):
        others[name].start()

    barrier = pltpu.get_barrier_semaphore()

    for step in range(1, PB):
        pl.semaphore_signal(
            barrier,
            inc=1,
            device_id={"pb": lax.rem(me_p + step, PB)},
            device_id_type=pl.DeviceIdType.MESH,
        )
    for peer in [chip_at(dz, dy) * 2 + core for dz, dy in OFFSETS] + [sibling]:
        pl.semaphore_signal(
            barrier, inc=1, device_id={"aa": peer}, device_id_type=pl.DeviceIdType.MESH
        )

    for copy in wave_in:
        copy.wait()

    def windows(q, carry):
        at = pl.multiple_of(q * 64, 64)
        for c, ref in ((0, win_r), (1, win_i)):
            found = []
            for h in range(2):
                row = rows_ref[0, 2 * q + h]
                col = cols_ref[0, 2 * q + h]
                tile = col // 128
                off = col % 128
                near = wave[pl.ds(tile * 256 + c * 128 + row, 64), :]
                far = wave[pl.ds(jnp.minimum(tile + 1, 3) * 256 + c * 128 + row, 64), :]
                both = jnp.where(lanes((64, 128)) >= off, near, far)
                found.append(pltpu.roll(both, (128 + 64 * h - off) % 128, 1))
            ref[pl.ds(at, 64), :] = jnp.where(lanes((64, 128)) < 64, found[0], found[1])
        return carry

    lax.fori_loop(0, PAIRS, windows, 0)
    others["probe"].wait()
    others["tab"].wait()
    others["inten"].wait()
    for octet in range(2):
        for t in range(32):
            inten[pl.ds(octet * 256 + t, 8, stride=32), :] = int_raw[
                octet * 8 : octet * 8 + 8, t * 128 : (t + 1) * 128
            ]
    for n in range(2):
        tab[2 * n], tab[2 * n + 1] = halves(tab_raw[n * 256 : (n + 1) * 256, :])
        high, low = halves(tab_raw[512:640, n * 128 : (n + 1) * 128])
        tab[4 + n] = jnp.concatenate(
            [jnp.concatenate([high] * 2, axis=1), jnp.concatenate([low] * 2, axis=1)], axis=0
        )
    one_re = jnp.concatenate([probe[0]] * 2, axis=1)
    one_im = jnp.concatenate([probe[1]] * 2, axis=1)
    p_re = jnp.concatenate([one_re] * PAIRS, axis=0)
    p_im = jnp.concatenate([one_im] * PAIRS, axis=0)
    w_re, w_im = win_r[...], win_i[...]
    half_re, half_im = right_apply(
        p_re * w_re - p_im * w_im, p_re * w_im + p_im * w_re, tab[0], tab[1]
    )
    far_re, far_im = left_apply(rows_to_lanes(half_re), rows_to_lanes(half_im), tab[4])
    measured, live = [], []
    for q in range(PAIRS):
        even, odd = interleave(
            inten[2 * q * 32 : 2 * q * 32 + 32, :], inten[2 * q * 32 + 32 : 2 * q * 32 + 64, :]
        )
        measured.append(jnp.concatenate([even, odd], axis=0))
        live.append(
            jnp.where(
                lanes((1, 128)) < 64, mask_ref[0, 2 * q].astype(F32), mask_ref[0, 2 * q + 1].astype(F32)
            )
        )
    measured = jnp.concatenate(measured, axis=1)
    live = jnp.concatenate(live, axis=1)
    factor = live * (far_re * far_re + far_im * far_im - measured)
    half_re, half_im = left_apply(factor * far_re, factor * far_im, tab[5])
    back_re, back_im = right_apply(lanes_to_rows(half_re), lanes_to_rows(half_im), tab[2], tab[3])
    gra_r[...] = p_re * back_re + p_im * back_im
    gra_i[...] = p_re * back_im - p_im * back_re
    grad_re = jnp.sum((w_re * back_re + w_im * back_im).reshape(PAIRS, 64, 128), axis=0)
    grad_im = jnp.sum((w_re * back_im - w_im * back_re).reshape(PAIRS, 64, 128), axis=0)
    grad_re = grad_re + swap(grad_re)
    grad_im = grad_im + swap(grad_im)
    probe_part = jnp.where(lanes((64, 128)) < 64, grad_re, grad_im)

    pad[...] = jnp.zeros_like(pad)
    acc[...] = jnp.zeros_like(acc)
    for t in range(PB):
        acc[t * SHARE + 256 : (t + 1) * SHARE, :] = probe_part[t * 16 : (t + 1) * 16]

    def scatter(q, carry):
        at = pl.multiple_of(q * 64, 64)
        for h in range(2):
            row = rows_ref[0, 2 * q + h]
            col = cols_ref[0, 2 * q + h]
            turn = (col + 128 - 64 * h) % 128
            for c, ref in ((0, gra_r), (1, gra_i)):
                slot = (2 * h + c) * 192
                pad[slot + 64 : slot + 128, :] = pltpu.roll(ref[pl.ds(at, 64), :], turn, 1)
                moved = pad[pl.ds(slot + 64 - row, 128), :]
                for t in range(4):
                    place = lanes((128, 128)) + (t * 128 - col)
                    start = t * SHARE + c * 128
                    acc[start : start + 128, :] = acc[start : start + 128, :] + jnp.where(
                        (place >= 0) & (place < 64), moved, 0.0
                    )
        return carry

    lax.fori_loop(0, PAIRS, scatter, 0)
    def to_x(stage, step, src, dst):
        peer = lax.rem(me_p + step, PB)
        return pltpu.make_async_remote_copy(
            src_ref=src,
            dst_ref=dst,
            send_sem=x_send.at[stage * 3 + step - 1],
            recv_sem=x_recv.at[stage * 3 + step - 1],
            device_id={"pb": peer},
            device_id_type=pl.DeviceIdType.MESH,
        )

    pl.semaphore_wait(barrier, CHIPS + PB - 1)
    reduces = [
        to_x(
            0,
            step,
            acc.at[pl.ds(pl.multiple_of(lax.rem(me_p + step, PB) * SHARE, 16), SHARE)],
            share.at[pl.ds((step - 1) * SHARE, SHARE)],
        )
        for step in (2, 1, 3)
    ]
    for copy in reduces:
        copy.start()

    for copy in obj_in:
        copy.wait()

    def fold(q, carry):
        for t in range(4):
            even = obj[pl.ds(t * 512 + 2 * q, 8, stride=64), :]
            odd = obj[pl.ds(t * 512 + 2 * q + 1, 8, stride=64), :]
            first, second = interleave(even, odd)
            at = pl.multiple_of(q * 64 + t * 16, 16)
            lhs[pl.ds(at, 16), :] = jnp.concatenate([first, second], axis=0)
        return carry

    lax.fori_loop(0, 32, fold, 0, unroll=4)
    own_stk = pl.multiple_of(me_p * KEYS, KEYS)
    for half in range(2):
        products = jnp.zeros((64, WIDE), F32)
        for c in range(4):
            wts_in[half * 4 + c].wait()
            part = jnp.concatenate(
                [lhs[(c * 8 + n) * 64 : (c * 8 + n + 1) * 64, :] for n in range(8)], axis=1
            ).astype(BF16)
            products = products + dot(
                part, wts[c * 1024 : (c + 1) * 1024, half * WIDE : (half + 1) * WIDE]
            )
        for i in range(3):
            t = half * 3 + i
            ptile[t * 64 : (t + 1) * 64, :] = products[:, i * 128 : (i + 1) * 128]
            lists = [[], []], [[], []]
            for br in range(2):
                part = [ptile[pl.ds(t * 64 + cz * 2 + br, 8, stride=8), :] for cz in range(ZC)]
                for c in range(2):
                    even, odd = interleave(part[2 * c], part[2 * c + 1])
                    lists[0][c].append(even)
                    lists[1][c].append(odd)
            for h in range(2):
                for c in range(2):
                    stk[
                        pl.ds(pl.multiple_of(own_stk + (2 * t + h) * 16, 16), 16),
                        c * 128 : (c + 1) * 128,
                    ] = jnp.concatenate(lists[h][c], axis=0).astype(BF16)

    others["blocks"].wait()
    others["tables"].wait()
    keys = []
    for jj in range(2):
        there = pl.ds(me_p * 2 + jj, LIST, stride=NB)
        block = blocks[there, :]
        keys.append((block // OWN) * KEYS + tables[there, :] * OWN + block % OWN)
    keys = jnp.concatenate(
        [jnp.concatenate(keys, axis=1), jnp.zeros((128 - LIST, 128), jnp.int32)], axis=0
    )
    keys = jnp.transpose(keys.astype(F32)).astype(jnp.int32)
    for t in range(6):
        column = lanes((128, 128)) + t * 128
        total = jnp.zeros((128, 128), F32)
        for e in range(LIST):
            total = total + jnp.where(keys[:, e : e + 1] == column, 1.0, 0.0)
        hit_r[:, t * 128 : (t + 1) * 128] = total.astype(BF16)

    for p in range(PB):
        parts = []
        for jj in range(2):
            there = pl.ds(p * 2 + jj, LIST, stride=NB)
            block = blocks[there, :]
            place = tables[there, :] * OWN + block % OWN
            parts.append(jnp.where(block // OWN == me_p, place, -1))
        colkey[:, p * 128 : (p + 1) * 128] = jnp.concatenate(parts, axis=1)
    for r in range(3):
        mine = lax.broadcasted_iota(jnp.int32, (64, 512), 0) + r * 64
        total = jnp.zeros((64, 512), F32)
        for e in range(LIST):
            total = total + jnp.where(colkey[e : e + 1, :] == mine, 1.0, 0.0)
        hit_c[r * 64 : (r + 1) * 64, :] = total.astype(BF16)

    def to_a(stage, peer, src, dst):
        return pltpu.make_async_remote_copy(
            src_ref=src,
            dst_ref=dst,
            send_sem=a_send.at[stage],
            recv_sem=a_recv.at[stage],
            device_id={"aa": peer},
            device_id_type=pl.DeviceIdType.MESH,
        )

    def swap_cores(stage, loose, extra, across, arrived):
        for k in range(4):
            across[k * 32 : k * 32 + 32, :] = loose[pl.ds(k * 64 + 1 - core, 32, stride=2), :]
        if extra is not None:
            across[128:144, :] = extra
        rows = 128 if extra is None else 144
        copy = to_a(stage, sibling, across.at[pl.ds(0, rows)], arrived.at[pl.ds(0, rows)])
        copy.start()
        return copy

    def fill(loose, arrived, message):
        for k in range(4):
            message[pl.ds(core * 4 + k, 32, stride=SLOT), :] = loose[
                pl.ds(k * 64 + core, 32, stride=2), :
            ]
            message[pl.ds((1 - core) * 4 + k, 32, stride=SLOT), :] = arrived[
                k * 32 : k * 32 + 32, :
            ]

    def exchange(stage, message, target, count):
        here = pl.ds(pl.multiple_of(chip * SLOT, SLOT), count)
        for dz, dy in OFFSETS:
            there = chip_at(dz, dy)
            to_a(
                stage,
                there * 2 + core,
                message.at[pl.ds(pl.multiple_of(there * SLOT, SLOT), count)],
                target.at[here],
            ).start()
        target[here, :] = message[here, :]
        rows = (CHIPS - 1) * count
        return to_a(
            stage,
            chip_at(0, 1) * 2 + core,
            message.at[pl.ds(0, rows)],
            target.at[pl.ds(0, rows)],
        )

    others["dual"].wait()
    mine = wave[pl.ds(pl.multiple_of(me_p * 256, 256), 256), :]
    for copy in reduces:
        copy.wait_recv()
    own_share = pl.multiple_of(me_p * SHARE, 16)
    gradient = acc[pl.ds(own_share, 256), :]
    probe_share = acc[pl.ds(own_share + 256, 16), :]
    for n in range(PB - 1):
        gradient = gradient + share[n * SHARE : n * SHARE + 256, :]
        probe_share = probe_share + share[n * SHARE + 256 : (n + 1) * SHARE, :]
    base[...] = mine - WAVE_STEP * (gradient + PENALTY * (mine + dual[...]))
    for c in range(2):
        for z in range(2):
            there = pl.ds(c * 128 + z, 64, stride=2)
            k = 2 * c + z
            loose1[k * 64 : k * 64 + 64, :] = base[there, :] + dual[there, :]
    swap1 = swap_cores(0, loose1, probe_share, across1, arrived1)
    own_block = stk.at[pl.ds(own_stk, KEYS)]
    gathers = [to_x(1, step, own_block, own_block) for step in (2, 1, 3)]
    for copy in gathers:
        copy.start()
    swap1.wait_recv()
    fill(loose1, arrived1, message1)
    probe_chip = probe_share + arrived1[128:144, :]
    message1[pl.ds(8, 32, stride=SLOT), :] = jnp.concatenate([probe_chip] * 2, axis=0)
    move1 = exchange(1, message1, recv1, 9)

    for copy in gathers:
        copy.wait_recv()
    projection = dot(hit_r[...], stk[...])
    for c in range(2):
        first, second = interleave(
            projection[:64, c * 128 : (c + 1) * 128], projection[64:, c * 128 : (c + 1) * 128]
        )
        loose2[2 * c * 64 : 2 * c * 64 + 64, :] = first
        loose2[2 * c * 64 + 64 : 2 * c * 64 + 128, :] = second

    move1.wait_recv()
    for half in range(2):
        for k in range(4):
            there = pl.ds(k * 64 + half, 32, stride=2)
            own = loose2[there, :]
            rest = recv1[pl.ds(half * 4 + k, 32, stride=SLOT), :]
            misfit[there, :] = own - (rest + (WAVE_STEP * PENALTY) * own)
    own_rays = pl.multiple_of(me_p * 128, 128)
    for c in range(2):
        first, second = interleave(
            misfit[2 * c * 64 : 2 * c * 64 + 64, :], misfit[2 * c * 64 + 64 : 2 * c * 64 + 128, :]
        )
        rays[pl.ds(own_rays, 128), c * 128 : (c + 1) * 128] = jnp.concatenate(
            [first, second], axis=0
        ).astype(BF16)
    own_rows = rays.at[pl.ds(own_rays, 128)]
    ray_moves = [to_x(2, step, own_rows, own_rows) for step in (2, 1, 3)]
    for copy in ray_moves:
        copy.start()

    own_row = pl.ds(pl.multiple_of(me_p * 8, 8), 1)
    prow[own_row, :] = jnp.sum(recv1[pl.ds(8, 32, stride=SLOT), :], axis=0, keepdims=True)
    probe_x = [to_x(3, step, prow.at[own_row], prow.at[own_row]) for step in (2, 1, 3)]
    for copy in probe_x:
        copy.start()

    swap2 = swap_cores(2, loose2, None, across2, arrived2)
    swap2.wait_recv()
    fill(loose2, arrived2, message2)
    for copy in probe_x:
        copy.wait_recv()
    for p in range(PB):
        message2[pl.ds(8 + p, 32, stride=SLOT), :] = jnp.broadcast_to(
            prow[p * 8 : p * 8 + 1, :], (32, 128)
        )
    move2 = exchange(3, message2, recv2, 12)

    for copy in ray_moves:
        copy.wait_recv()

    sums = dot(hit_c[...], rays[...]).astype(BF16).astype(F32)
    for t in range(6):
        for br in range(2):
            for c in range(2):
                at = 2 * t * 16 + br * 8
                first, second = interleave(
                    sums[at : at + 8, c * 128 : (c + 1) * 128],
                    sums[at + 16 : at + 24, c * 128 : (c + 1) * 128],
                )
                spread[pl.ds(t * 64 + 4 * c + br, 8, stride=8), :] = first
                spread[pl.ds(t * 64 + 4 * c + 2 + br, 8, stride=8), :] = second
    table = jnp.concatenate(
        [spread[t * 64 : (t + 1) * 64, :] for t in range(6)], axis=1
    ).astype(BF16)

    for n in range(WCH):
        grad = lax.dot_general(
            table,
            wts[n * WROWS : (n + 1) * WROWS, :],
            (((1,), (1,)), ((), ())),
            preferred_element_type=F32,
        )
        per = 32 // WCH
        for s in range(per):
            q = n * per + s
            for t in range(4):
                first, second = interleave(
                    grad[t * 16 : t * 16 + 8, s * 128 : (s + 1) * 128],
                    grad[t * 16 + 8 : t * 16 + 16, s * 128 : (s + 1) * 128],
                )
                even = pl.ds(t * 512 + 2 * q, 8, stride=64)
                odd = pl.ds(t * 512 + 2 * q + 1, 8, stride=64)
                onew[even, :] = obj[even, :] - OBJECT_STEP * first
                onew[odd, :] = obj[odd, :] - OBJECT_STEP * second

    move2.wait_recv()
    for half in range(2):
        for c in range(2):
            for z in range(2):
                there = pl.ds(c * 128 + 2 * half + z, 32, stride=4)
                here = recv2[pl.ds(half * 4 + 2 * c + z, 32, stride=SLOT), :]
                wnext[there, :] = base[there, :] + (WAVE_STEP * PENALTY) * here
    total = jnp.concatenate(
        [recv2[pl.ds(8 + p, 16, stride=SLOT), :] for p in range(PB)], axis=0
    )
    scale = PROBE_STEP / (AA * POS * PB)
    pnext[0] = probe[0] - scale * total[:, :64]
    pnext[1] = probe[1] - scale * swap(total)[:, :64]

    for copy in gathers + reduces + probe_x + ray_moves + [swap1, move1, swap2, move2]:
        copy.wait_send()


def tail(wnext, pnext, onew, wave_out, probe_out, obj_out, sem):
    pairs = [
        (onew.at[pl.ds(t * 512, 512)], obj_out.at[:, pl.ds(t * 128, 128)]) for t in range(4)
    ] + [(wnext, wave_out), (pnext, probe_out)]
    copies = [pltpu.make_async_copy(src, dst, sem.at[n]) for n, (src, dst) in enumerate(pairs)]
    for copy in copies:
        copy.start()
    for copy in copies:
        copy.wait()


def shards(
    tables,
    wave_field,
    scaled_dual,
    intensity,
    probe_field,
    scan_rows,
    scan_cols,
    sample_mask,
    object_field,
    ray_blocks,
    ray_tables,
    radon_weights,
):
    smem = pl.BlockSpec(memory_space=pltpu.SMEM)
    vmem = pltpu.VMEM
    hbm_spec = pl.BlockSpec(memory_space=pltpu.HBM)
    vmem_spec = pl.BlockSpec(memory_space=pltpu.VMEM)
    kept = pl.pallas_call(
        kernel,
        out_shape=(
            pltpu.VMEM((256, 128), F32),
            pltpu.VMEM((2, 64, 64), F32),
            pltpu.VMEM((2048, 128), F32),
        ),
        in_specs=[smem] * 3 + [hbm_spec] * 9,
        out_specs=[vmem_spec] * 3,
        scratch_shapes=[
            vmem((4096, 768), BF16),
            vmem((2048, 128), F32),
            vmem((1024, 128), F32),
            vmem((256, 128), F32),
            vmem((POS, 4096), F32),
            vmem((POS * 32, 128), F32),
            vmem((2, 64, 64), F32),
            vmem((640, 256), F32),
            vmem((6, 256, 256), BF16),
            vmem((LIST * NB, AA), jnp.int32),
            vmem((LIST * NB, AA), jnp.int32),
            vmem((LIST, 512), jnp.int32),
            vmem((2048, 128), F32),
            vmem((384, 128), F32),
            vmem((768, 256), BF16),
            vmem((128, 768), BF16),
            vmem((KEYS, 512), BF16),
            vmem((512, 128), F32),
            vmem((512, 128), F32),
            vmem((512, 128), F32),
            vmem((512, 128), F32),
            vmem((768, 128), F32),
            vmem((PB * SHARE, 128), F32),
            vmem(((PB - 1) * SHARE, 128), F32),
            vmem((256, 128), F32),
            vmem((256, 128), F32),
            vmem((144, 128), F32),
            vmem((144, 128), F32),
            vmem((CHIPS * SLOT, 128), F32),
            vmem((CHIPS * SLOT, 128), F32),
            vmem((256, 128), F32),
            vmem((256, 128), F32),
            vmem((128, 128), F32),
            vmem((128, 128), F32),
            vmem((CHIPS * SLOT, 128), F32),
            vmem((CHIPS * SLOT, 128), F32),
            vmem((512, 256), BF16),
            vmem((384, 128), F32),
            vmem((32, 128), F32),
            pltpu.SemaphoreType.DMA((14,)),
            pltpu.SemaphoreType.DMA((WCH,)),
            pltpu.SemaphoreType.DMA((12,)),
            pltpu.SemaphoreType.DMA((12,)),
            pltpu.SemaphoreType.DMA((4,)),
            pltpu.SemaphoreType.DMA((4,)),
        ],
        compiler_params=pltpu.CompilerParams(
            collective_id=0, has_side_effects=True, vmem_limit_bytes=60 * 1024 * 1024
        ),
        name="admm",
    )(
        scan_rows,
        scan_cols,
        sample_mask,
        object_field.reshape(512, 512),
        radon_weights,
        wave_field.reshape(256, 512),
        scaled_dual.reshape(256, 128),
        intensity.reshape(POS, 4096),
        probe_field,
        tables,
        ray_blocks.transpose(2, 1, 0).reshape(LIST * NB, AA),
        ray_tables.transpose(2, 1, 0).reshape(LIST * NB, AA),
    )
    wave_next, probe_next, object_next = pl.pallas_call(
        tail,
        out_shape=(
            jax.ShapeDtypeStruct((256, 128), F32),
            jax.ShapeDtypeStruct((2, 64, 64), F32),
            jax.ShapeDtypeStruct((512, 512), F32),
        ),
        in_specs=[vmem_spec] * 3,
        out_specs=[hbm_spec] * 3,
        scratch_shapes=[pltpu.SemaphoreType.DMA((6,))],
        compiler_params=pltpu.CompilerParams(vmem_limit_bytes=16 * 1024 * 1024),
        name="tail",
    )(*kept)
    return (
        wave_next.reshape(1, 2, 128, 128),
        probe_next,
        object_next.reshape(2, 2, 128, 512),
    )


def solution(mesh):
    specs = (
        P("aa", None, None, None),
        P("aa", None, None, "pb"),
        P("aa", "pb", None),
        P(),
        P("aa", "pb"),
        P("aa", "pb"),
        P("aa", "pb"),
        P(None, "aa", "pb", None),
        P(),
        P(),
        P(),
    )
    mapped = jax.shard_map(
        shards,
        mesh=mesh,
        in_specs=(P(),) + specs,
        out_specs=(P("aa", None, None, "pb"), P(), P(None, "aa", "pb", None)),
        check_vma=False,
    )

    def step(*arrays):
        return mapped(jnp.asarray(dft_constants()), *arrays)

    return step
```

```python
import math

import jax
import jax.numpy as jnp
import numpy as np
from jax import lax
from jax.experimental import pallas as pl
from jax.experimental.pallas import tpu as pltpu
from jax.sharding import PartitionSpec as P

BLK = 64
NW = 12
NB = 8
LIST = 12
AA = 64
PB = 4
ZC = 4
POS = 16
PAIRS = 8
OWN = 64 // PB
KEYS = 192
LAYER = 8
DEPTH = 8
ROWS = 4
CHIPS = 32
SLOT = 16
SHARE = 272
OFFSETS = sorted(
    [(dz, dy) for dz in range(DEPTH) for dy in range(ROWS) if dz + dy > 0],
    key=lambda o: (-min(o[0], DEPTH - o[0]) - min(o[1], ROWS - o[1]), o),
)
WCH = 8
WROWS = 4096 // WCH
WIDE = 384

WAVE_STEP = 0.05
PENALTY = 1.0
PROBE_STEP = 0.05
OBJECT_STEP = 1.0

F32 = jnp.float32
BF16 = jnp.bfloat16


def dft_constants():
    index = np.arange(BLK)
    phase = (index[:, None] * index[None, :]) % BLK
    angle = phase.astype(np.float64) * (-2.0 * math.pi / BLK)
    f_re, f_im = np.cos(angle) / math.sqrt(BLK), np.sin(angle) / math.sqrt(BLK)
    pair = np.eye(2)

    def right(re, im):
        dre, dim = np.kron(pair, re), np.kron(pair, im)
        return np.block([[dre, dim], [-dim, dre]])

    def left(re, im):
        return np.block([[re, -im], [im, re]])

    order = np.concatenate([np.arange(0, BLK, 2), np.arange(1, BLK, 2)])
    rights = [right(f_re, f_im), right(f_re, -f_im)]
    lefts = np.concatenate(
        [left(f_re[order, :], f_im[order, :]), left(f_re[:, order], -f_im[:, order])], axis=1
    )
    return np.concatenate(rights + [lefts], axis=0).astype(np.float32)


def halves(value):
    high = value.astype(BF16)
    low = (value - high.astype(F32)).astype(BF16)
    return high, low


def dot(lhs, rhs):
    return jnp.dot(lhs, rhs, preferred_element_type=F32)


def right_apply(re, im, g_hi, g_lo):
    high, low = halves(jnp.concatenate([re, im], axis=1))
    out = dot(high, g_hi) + dot(low, g_hi) + dot(high, g_lo)
    return out[:, :128], out[:, 128:]


def left_apply(re, im, table):
    high, low = halves(jnp.concatenate([re, im], axis=0))
    out = dot(table, jnp.concatenate([high, low], axis=0))
    out = out[:128] + out[128:]
    return out[:64], out[64:]


def rows_to_lanes(value):
    return jnp.concatenate([value[q * 64 : (q + 1) * 64] for q in range(PAIRS)], axis=1)


def lanes_to_rows(value):
    return jnp.concatenate([value[:, q * 128 : (q + 1) * 128] for q in range(PAIRS)], axis=0)


def swap(value):
    return pltpu.roll(value, 64, 1)


def interleave(first, second):
    low = lax.broadcasted_iota(jnp.int32, first.shape, 1) < 64
    return jnp.where(low, first, swap(second)), jnp.where(low, swap(first), second)


def kernel(
    rows_ref,
    cols_ref,
    mask_ref,
    obj_hbm,
    wts_hbm,
    wave_hbm,
    dual_hbm,
    int_hbm,
    probe_hbm,
    tab_hbm,
    blocks_hbm,
    tables_hbm,
    wnext,
    pnext,
    onew,
    wts,
    obj,
    wave,
    dual,
    int_raw,
    inten,
    probe,
    tab_raw,
    tab,
    blocks,
    tables,
    colkey,
    lhs,
    ptile,
    stk,
    hit_r,
    hit_c,
    win_r,
    win_i,
    gra_r,
    gra_i,
    pad,
    acc,
    share,
    base,
    loose1,
    across1,
    arrived1,
    message1,
    recv1,
    loose2,
    misfit,
    across2,
    arrived2,
    message2,
    recv2,
    rays,
    spread,
    prow,
    pfull,
    probe_part,
    in_sem,
    w_sem,
    x_send,
    x_recv,
    a_send,
    a_recv,
):
    me_a = lax.axis_index("aa")
    me_p = lax.axis_index("pb")
    core = me_a % 2
    chip = me_a // 2
    z_own = me_a // LAYER
    y_own = chip % ROWS
    z_base = z_own * LAYER
    sibling = me_a + 1 - 2 * core

    def chip_at(dz, dy):
        return lax.rem(z_own + dz, DEPTH) * ROWS + lax.rem(y_own + dy, ROWS)

    def lanes(shape):
        return lax.broadcasted_iota(jnp.int32, shape, 1)

    obj_in = [
        pltpu.make_async_copy(
            obj_hbm.at[:, pl.ds(t * 128, 128)], obj.at[pl.ds(t * 512, 512)], in_sem.at[t]
        )
        for t in range(4)
    ]
    wts_in = [
        pltpu.make_async_copy(
            wts_hbm.at[pl.ds(c * 1024, 1024), pl.ds(h * WIDE, WIDE)],
            wts.at[pl.ds(c * 1024, 1024), pl.ds(h * WIDE, WIDE)],
            w_sem.at[h * 4 + c],
        )
        for h in range(2)
        for c in range(4)
    ]
    wave_in = [
        pltpu.make_async_copy(
            wave_hbm.at[:, pl.ds(t * 128, 128)], wave.at[pl.ds(t * 256, 256)], in_sem.at[4 + t]
        )
        for t in range(4)
    ]
    others = {
        name: pltpu.make_async_copy(src, dst, in_sem.at[8 + n])
        for n, (name, src, dst) in enumerate(
            [
                ("blocks", blocks_hbm, blocks),
                ("tables", tables_hbm, tables),
                ("probe", probe_hbm, probe),
                ("tab", tab_hbm, tab_raw),
                ("inten", int_hbm, int_raw),
                ("dual", dual_hbm, dual),
            ]
        )
    }
    for copy in wave_in:
        copy.start()
    for name in ("probe", "tab", "inten"):
        others[name].start()
    for copy in obj_in + wts_in:
        copy.start()
    for name in ("dual", "blocks", "tables"):
        others[name].start()

    barrier = pltpu.get_barrier_semaphore()

    for step in range(1, PB):
        pl.semaphore_signal(
            barrier,
            inc=1,
            device_id={"pb": lax.rem(me_p + step, PB)},
            device_id_type=pl.DeviceIdType.MESH,
        )
    def clear(n, carry):
        for at in (0, 128):
            pad[pl.ds(pl.multiple_of(n * 192 + at, 64), 64), :] = jnp.zeros((64, 128), F32)
        return carry

    lax.fori_loop(0, 2 * POS, clear, 0)

    for copy in wave_in:
        copy.wait()

    def windows(q, carry):
        at = pl.multiple_of(q * 64, 64)
        for n in range(CHIPS // PAIRS):
            ahead = q * (CHIPS // PAIRS) + n
            peer = jnp.where(ahead == 0, sibling, lax.rem(chip + ahead, CHIPS) * 2 + core)
            pl.semaphore_signal(
                barrier, inc=1, device_id={"aa": peer}, device_id_type=pl.DeviceIdType.MESH
            )
        for c, ref in ((0, win_r), (1, win_i)):
            found = []
            for h in range(2):
                row = rows_ref[0, 2 * q + h]
                col = cols_ref[0, 2 * q + h]
                tile = col // 128
                off = col % 128
                near = wave[pl.ds(tile * 256 + c * 128 + row, 64), :]
                far = wave[pl.ds(jnp.minimum(tile + 1, 3) * 256 + c * 128 + row, 64), :]
                both = jnp.where(lanes((64, 128)) >= off, near, far)
                found.append(pltpu.roll(both, (128 + 64 * h - off) % 128, 1))
            ref[pl.ds(at, 64), :] = jnp.where(lanes((64, 128)) < 64, found[0], found[1])
        return carry

    lax.fori_loop(0, PAIRS, windows, 0)
    others["probe"].wait()
    others["tab"].wait()
    others["inten"].wait()
    for octet in range(2):
        for t in range(32):
            inten[pl.ds(octet * 256 + t, 8, stride=32), :] = int_raw[
                octet * 8 : octet * 8 + 8, t * 128 : (t + 1) * 128
            ]
    for n in range(2):
        tab[2 * n], tab[2 * n + 1] = halves(tab_raw[n * 256 : (n + 1) * 256, :])
        high, low = halves(tab_raw[512:640, n * 128 : (n + 1) * 128])
        tab[4 + n] = jnp.concatenate(
            [jnp.concatenate([high] * 2, axis=1), jnp.concatenate([low] * 2, axis=1)], axis=0
        )
    one_re = jnp.concatenate([probe[0]] * 2, axis=1)
    one_im = jnp.concatenate([probe[1]] * 2, axis=1)
    p_re = jnp.concatenate([one_re] * PAIRS, axis=0)
    p_im = jnp.concatenate([one_im] * PAIRS, axis=0)
    w_re, w_im = win_r[...], win_i[...]
    half_re, half_im = right_apply(
        p_re * w_re - p_im * w_im, p_re * w_im + p_im * w_re, tab[0], tab[1]
    )
    far_re, far_im = left_apply(rows_to_lanes(half_re), rows_to_lanes(half_im), tab[4])
    measured, live = [], []
    for q in range(PAIRS):
        even, odd = interleave(
            inten[2 * q * 32 : 2 * q * 32 + 32, :], inten[2 * q * 32 + 32 : 2 * q * 32 + 64, :]
        )
        measured.append(jnp.concatenate([even, odd], axis=0))
        live.append(
            jnp.where(
                lanes((1, 128)) < 64, mask_ref[0, 2 * q].astype(F32), mask_ref[0, 2 * q + 1].astype(F32)
            )
        )
    measured = jnp.concatenate(measured, axis=1)
    live = jnp.concatenate(live, axis=1)
    factor = live * (far_re * far_re + far_im * far_im - measured)
    half_re, half_im = left_apply(factor * far_re, factor * far_im, tab[5])
    back_re, back_im = right_apply(lanes_to_rows(half_re), lanes_to_rows(half_im), tab[2], tab[3])
    gra_r[...] = p_re * back_re + p_im * back_im
    gra_i[...] = p_re * back_im - p_im * back_re
    grad_re = jnp.sum((w_re * back_re + w_im * back_im).reshape(PAIRS, 64, 128), axis=0)
    grad_im = jnp.sum((w_re * back_im - w_im * back_re).reshape(PAIRS, 64, 128), axis=0)
    grad_re = grad_re + swap(grad_re)
    grad_im = grad_im + swap(grad_im)
    probe_part[...] = jnp.where(lanes((64, 128)) < 64, grad_re, grad_im)

    def place(q, carry):
        at = pl.multiple_of(q * 64, 64)
        for h in range(2):
            turn = (cols_ref[0, 2 * q + h] + 128 - 64 * h) % 128
            for c, ref in ((0, gra_r), (1, gra_i)):
                slot = pl.multiple_of((4 * q + 2 * h + c) * 192 + 64, 64)
                pad[pl.ds(slot, 64), :] = pltpu.roll(ref[pl.ds(at, 64), :], turn, 1)
        return carry

    lax.fori_loop(0, PAIRS, place, 0)

    def to_x(stage, step, src, dst):
        peer = lax.rem(me_p + step, PB)
        return pltpu.make_async_remote_copy(
            src_ref=src,
            dst_ref=dst,
            send_sem=x_send.at[stage * 3 + step - 1],
            recv_sem=x_recv.at[stage * 3 + step - 1],
            device_id={"pb": peer},
            device_id_type=pl.DeviceIdType.MESH,
        )

    pl.semaphore_wait(barrier, CHIPS + PB - 1)
    reduces = []
    for step in (2, 1, 3, 0):
        tile = lax.rem(me_p + step, PB)
        for c in range(2):

            def add(n, total, c=c, tile=tile):
                moved = pad[pl.ds((2 * n + c) * 192 + 64 - rows_ref[0, n], 128), :]
                column = lanes((128, 128)) + (tile * 128 - cols_ref[0, n])
                return total + jnp.where((column >= 0) & (column < 64), moved, 0.0)

            at = step * SHARE + c * 128
            acc[at : at + 128, :] = lax.fori_loop(
                0, POS, add, jnp.zeros((128, 128), F32), unroll=4
            )
        acc[step * SHARE + 256 : (step + 1) * SHARE, :] = probe_part[
            pl.ds(pl.multiple_of(tile * 16, 16), 16), :
        ]
        if step > 0:
            copy = to_x(
                0,
                step,
                acc.at[pl.ds(step * SHARE, SHARE)],
                share.at[pl.ds((step - 1) * SHARE, SHARE)],
            )
            copy.start()
            reduces.append(copy)

    for copy in obj_in:
        copy.wait()

    def fold(q, carry):
        for t in range(4):
            even = obj[pl.ds(t * 512 + 2 * q, 8, stride=64), :]
            odd = obj[pl.ds(t * 512 + 2 * q + 1, 8, stride=64), :]
            first, second = interleave(even, odd)
            at = pl.multiple_of(q * 64 + t * 16, 16)
            lhs[pl.ds(at, 16), :] = jnp.concatenate([first, second], axis=0)
        return carry

    lax.fori_loop(0, 32, fold, 0, unroll=4)
    own_stk = pl.multiple_of(me_p * KEYS, KEYS)
    for half in range(2):
        products = jnp.zeros((64, WIDE), F32)
        for c in range(4):
            wts_in[half * 4 + c].wait()
            part = jnp.concatenate(
                [lhs[(c * 8 + n) * 64 : (c * 8 + n + 1) * 64, :] for n in range(8)], axis=1
            ).astype(BF16)
            products = products + dot(
                part, wts[c * 1024 : (c + 1) * 1024, half * WIDE : (half + 1) * WIDE]
            )
        for i in range(3):
            t = half * 3 + i
            ptile[t * 64 : (t + 1) * 64, :] = products[:, i * 128 : (i + 1) * 128]
            lists = [[], []], [[], []]
            for br in range(2):
                part = [ptile[pl.ds(t * 64 + cz * 2 + br, 8, stride=8), :] for cz in range(ZC)]
                for c in range(2):
                    even, odd = interleave(part[2 * c], part[2 * c + 1])
                    lists[0][c].append(even)
                    lists[1][c].append(odd)
            for h in range(2):
                for c in range(2):
                    stk[
                        pl.ds(pl.multiple_of(own_stk + (2 * t + h) * 16, 16), 16),
                        c * 128 : (c + 1) * 128,
                    ] = jnp.concatenate(lists[h][c], axis=0).astype(BF16)

    others["blocks"].wait()
    others["tables"].wait()
    keys = []
    for jj in range(2):
        there = pl.ds(me_p * 2 + jj, LIST, stride=NB)
        block = blocks[there, :]
        keys.append((block // OWN) * KEYS + tables[there, :] * OWN + block % OWN)
    keys = jnp.concatenate(
        [jnp.concatenate(keys, axis=1), jnp.zeros((128 - LIST, 128), jnp.int32)], axis=0
    )
    keys = jnp.transpose(keys.astype(F32)).astype(jnp.int32)
    for t in range(6):
        column = lanes((128, 128)) + t * 128
        total = jnp.zeros((128, 128), F32)
        for e in range(LIST):
            total = total + jnp.where(keys[:, e : e + 1] == column, 1.0, 0.0)
        hit_r[:, t * 128 : (t + 1) * 128] = total.astype(BF16)

    for p in range(PB):
        parts = []
        for jj in range(2):
            there = pl.ds(p * 2 + jj, LIST, stride=NB)
            block = blocks[there, :]
            place = tables[there, :] * OWN + block % OWN
            parts.append(jnp.where(block // OWN == me_p, place, -1))
        colkey[:, p * 128 : (p + 1) * 128] = jnp.concatenate(parts, axis=1)
    for r in range(3):
        mine = lax.broadcasted_iota(jnp.int32, (64, 512), 0) + r * 64
        total = jnp.zeros((64, 512), F32)
        for e in range(LIST):
            total = total + jnp.where(colkey[e : e + 1, :] == mine, 1.0, 0.0)
        hit_c[r * 64 : (r + 1) * 64, :] = total.astype(BF16)

    def to_a(stage, peer, src, dst):
        return pltpu.make_async_remote_copy(
            src_ref=src,
            dst_ref=dst,
            send_sem=a_send.at[stage],
            recv_sem=a_recv.at[stage],
            device_id={"aa": peer},
            device_id_type=pl.DeviceIdType.MESH,
        )

    def swap_cores(stage, loose, extra, across, arrived):
        for k in range(4):
            across[k * 32 : k * 32 + 32, :] = loose[pl.ds(k * 64 + 1 - core, 32, stride=2), :]
        if extra is not None:
            across[128:144, :] = extra
        rows = 128 if extra is None else 144
        copy = to_a(stage, sibling, across.at[pl.ds(0, rows)], arrived.at[pl.ds(0, rows)])
        copy.start()
        return copy

    def fill(loose, arrived, message):
        for k in range(4):
            message[pl.ds(core * 4 + k, 32, stride=SLOT), :] = loose[
                pl.ds(k * 64 + core, 32, stride=2), :
            ]
            message[pl.ds((1 - core) * 4 + k, 32, stride=SLOT), :] = arrived[
                k * 32 : k * 32 + 32, :
            ]

    def exchange(stage, message, target, count):
        here = pl.ds(pl.multiple_of(chip * SLOT, SLOT), count)
        for dz, dy in OFFSETS:
            there = chip_at(dz, dy)
            to_a(
                stage,
                there * 2 + core,
                message.at[pl.ds(pl.multiple_of(there * SLOT, SLOT), count)],
                target.at[here],
            ).start()
        target[here, :] = message[here, :]
        rows = (CHIPS - 1) * count
        return to_a(
            stage,
            chip_at(0, 1) * 2 + core,
            message.at[pl.ds(0, rows)],
            target.at[pl.ds(0, rows)],
        )

    others["dual"].wait()
    mine = wave[pl.ds(pl.multiple_of(me_p * 256, 256), 256), :]
    for copy in reduces:
        copy.wait_recv()
    gradient = acc[:256, :]
    probe_share = acc[256:SHARE, :]
    for n in range(PB - 1):
        gradient = gradient + share[n * SHARE : n * SHARE + 256, :]
        probe_share = probe_share + share[n * SHARE + 256 : (n + 1) * SHARE, :]
    base[...] = mine - WAVE_STEP * (gradient + PENALTY * (mine + dual[...]))
    for c in range(2):
        for z in range(2):
            there = pl.ds(c * 128 + z, 64, stride=2)
            k = 2 * c + z
            loose1[k * 64 : k * 64 + 64, :] = base[there, :] + dual[there, :]
    swap1 = swap_cores(0, loose1, probe_share, across1, arrived1)
    own_block = stk.at[pl.ds(own_stk, KEYS)]
    gathers = [to_x(1, step, own_block, own_block) for step in (2, 1, 3)]
    for copy in gathers:
        copy.start()
    swap1.wait_recv()
    fill(loose1, arrived1, message1)
    probe_chip = probe_share + arrived1[128:144, :]
    message1[pl.ds(8, 32, stride=SLOT), :] = jnp.concatenate([probe_chip] * 2, axis=0)
    move1 = exchange(1, message1, recv1, 9)

    for copy in gathers:
        copy.wait_recv()
    projection = dot(hit_r[...], stk[...])
    for c in range(2):
        first, second = interleave(
            projection[:64, c * 128 : (c + 1) * 128], projection[64:, c * 128 : (c + 1) * 128]
        )
        loose2[2 * c * 64 : 2 * c * 64 + 64, :] = first
        loose2[2 * c * 64 + 64 : 2 * c * 64 + 128, :] = second

    swap2 = swap_cores(2, loose2, None, across2, arrived2)
    swap2.wait_recv()
    fill(loose2, arrived2, message2)

    move1.wait_recv()
    for half in range(2):
        for k in range(4):
            there = pl.ds(k * 64 + half, 32, stride=2)
            own = loose2[there, :]
            rest = recv1[pl.ds(half * 4 + k, 32, stride=SLOT), :]
            misfit[there, :] = own - (rest + (WAVE_STEP * PENALTY) * own)
    own_rays = pl.multiple_of(me_p * 128, 128)
    for c in range(2):
        first, second = interleave(
            misfit[2 * c * 64 : 2 * c * 64 + 64, :], misfit[2 * c * 64 + 64 : 2 * c * 64 + 128, :]
        )
        rays[pl.ds(own_rays, 128), c * 128 : (c + 1) * 128] = jnp.concatenate(
            [first, second], axis=0
        ).astype(BF16)
    own_rows = rays.at[pl.ds(own_rays, 128)]
    ray_moves = [to_x(2, step, own_rows, own_rows) for step in (2, 1, 3)]
    for copy in ray_moves:
        copy.start()

    own_row = pl.ds(pl.multiple_of(me_p * 8, 8), 1)
    prow[own_row, :] = jnp.sum(recv1[pl.ds(8, 32, stride=SLOT), :], axis=0, keepdims=True)
    probe_x = [to_x(3, step, prow.at[own_row], prow.at[own_row]) for step in (2, 1, 3)]
    for copy in probe_x:
        copy.start()

    move2 = exchange(3, message2, recv2, 8)

    for copy in probe_x:
        copy.wait_recv()
    kind = chip % 16
    own_four = pl.ds(pl.multiple_of(kind * 8, 8), 4)
    pfull[own_four, :] = jnp.concatenate([prow[p * 8 : p * 8 + 1, :] for p in range(PB)], axis=0)

    def share_rows(step):
        four = pfull.at[own_four]
        return to_a(4, (chip - kind + lax.rem(kind + step, 16)) * 2 + core, four, four)

    for step in range(1, 16):
        share_rows(step).start()

    for copy in ray_moves:
        copy.wait_recv()

    sums = dot(hit_c[...], rays[...]).astype(BF16).astype(F32)
    for t in range(6):
        for br in range(2):
            for c in range(2):
                at = 2 * t * 16 + br * 8
                first, second = interleave(
                    sums[at : at + 8, c * 128 : (c + 1) * 128],
                    sums[at + 16 : at + 24, c * 128 : (c + 1) * 128],
                )
                spread[pl.ds(t * 64 + 4 * c + br, 8, stride=8), :] = first
                spread[pl.ds(t * 64 + 4 * c + 2 + br, 8, stride=8), :] = second
    table = jnp.concatenate(
        [spread[t * 64 : (t + 1) * 64, :] for t in range(6)], axis=1
    ).astype(BF16)

    for n in range(WCH):
        grad = lax.dot_general(
            table,
            wts[n * WROWS : (n + 1) * WROWS, :],
            (((1,), (1,)), ((), ())),
            preferred_element_type=F32,
        )
        per = 32 // WCH
        for s in range(per):
            q = n * per + s
            for t in range(4):
                first, second = interleave(
                    grad[t * 16 : t * 16 + 8, s * 128 : (s + 1) * 128],
                    grad[t * 16 + 8 : t * 16 + 16, s * 128 : (s + 1) * 128],
                )
                even = pl.ds(t * 512 + 2 * q, 8, stride=64)
                odd = pl.ds(t * 512 + 2 * q + 1, 8, stride=64)
                onew[even, :] = obj[even, :] - OBJECT_STEP * first
                onew[odd, :] = obj[odd, :] - OBJECT_STEP * second

    move2.wait_recv()
    for half in range(2):
        for c in range(2):
            for z in range(2):
                there = pl.ds(c * 128 + 2 * half + z, 32, stride=4)
                here = recv2[pl.ds(half * 4 + 2 * c + z, 32, stride=SLOT), :]
                wnext[there, :] = base[there, :] + (WAVE_STEP * PENALTY) * here
    sixty = pfull.at[pl.ds(0, 60)]
    probe_all = to_a(4, (chip - kind + lax.rem(kind + 1, 16)) * 2 + core, sixty, sixty)
    probe_all.wait_recv()
    total = jnp.concatenate([pfull[pl.ds(p, 16, stride=8), :] for p in range(PB)], axis=0)
    scale = PROBE_STEP / (AA * POS * PB)
    pnext[0] = probe[0] - scale * total[:, :64]
    pnext[1] = probe[1] - scale * swap(total)[:, :64]

    for copy in gathers + reduces + probe_x + ray_moves + [swap1, move1, swap2, move2, probe_all]:
        copy.wait_send()


def tail(wnext, pnext, onew, wave_out, probe_out, obj_out, sem):
    pairs = [
        (onew.at[pl.ds(t * 512, 512)], obj_out.at[:, pl.ds(t * 128, 128)]) for t in range(4)
    ] + [(wnext, wave_out), (pnext, probe_out)]
    copies = [pltpu.make_async_copy(src, dst, sem.at[n]) for n, (src, dst) in enumerate(pairs)]
    for copy in copies:
        copy.start()
    for copy in copies:
        copy.wait()


def shards(
    tables,
    wave_field,
    scaled_dual,
    intensity,
    probe_field,
    scan_rows,
    scan_cols,
    sample_mask,
    object_field,
    ray_blocks,
    ray_tables,
    radon_weights,
):
    smem = pl.BlockSpec(memory_space=pltpu.SMEM)
    vmem = pltpu.VMEM
    hbm_spec = pl.BlockSpec(memory_space=pltpu.HBM)
    vmem_spec = pl.BlockSpec(memory_space=pltpu.VMEM)
    kept = pl.pallas_call(
        kernel,
        out_shape=(
            pltpu.VMEM((256, 128), F32),
            pltpu.VMEM((2, 64, 64), F32),
            pltpu.VMEM((2048, 128), F32),
        ),
        in_specs=[smem] * 3 + [hbm_spec] * 9,
        out_specs=[vmem_spec] * 3,
        scratch_shapes=[
            vmem((4096, 768), BF16),
            vmem((2048, 128), F32),
            vmem((1024, 128), F32),
            vmem((256, 128), F32),
            vmem((POS, 4096), F32),
            vmem((POS * 32, 128), F32),
            vmem((2, 64, 64), F32),
            vmem((640, 256), F32),
            vmem((6, 256, 256), BF16),
            vmem((LIST * NB, AA), jnp.int32),
            vmem((LIST * NB, AA), jnp.int32),
            vmem((LIST, 512), jnp.int32),
            vmem((2048, 128), F32),
            vmem((384, 128), F32),
            vmem((768, 256), BF16),
            vmem((128, 768), BF16),
            vmem((KEYS, 512), BF16),
            vmem((512, 128), F32),
            vmem((512, 128), F32),
            vmem((512, 128), F32),
            vmem((512, 128), F32),
            vmem((2 * POS * 192, 128), F32),
            vmem((PB * SHARE, 128), F32),
            vmem(((PB - 1) * SHARE, 128), F32),
            vmem((256, 128), F32),
            vmem((256, 128), F32),
            vmem((144, 128), F32),
            vmem((144, 128), F32),
            vmem((CHIPS * SLOT, 128), F32),
            vmem((CHIPS * SLOT, 128), F32),
            vmem((256, 128), F32),
            vmem((256, 128), F32),
            vmem((128, 128), F32),
            vmem((128, 128), F32),
            vmem((CHIPS * SLOT, 128), F32),
            vmem((CHIPS * SLOT, 128), F32),
            vmem((512, 256), BF16),
            vmem((384, 128), F32),
            vmem((32, 128), F32),
            vmem((128, 128), F32),
            vmem((64, 128), F32),
            pltpu.SemaphoreType.DMA((14,)),
            pltpu.SemaphoreType.DMA((WCH,)),
            pltpu.SemaphoreType.DMA((12,)),
            pltpu.SemaphoreType.DMA((12,)),
            pltpu.SemaphoreType.DMA((5,)),
            pltpu.SemaphoreType.DMA((5,)),
        ],
        compiler_params=pltpu.CompilerParams(
            collective_id=0, has_side_effects=True, vmem_limit_bytes=60 * 1024 * 1024
        ),
        name="admm",
    )(
        scan_rows,
        scan_cols,
        sample_mask,
        object_field.reshape(512, 512),
        radon_weights,
        wave_field.reshape(256, 512),
        scaled_dual.reshape(256, 128),
        intensity.reshape(POS, 4096),
        probe_field,
        tables,
        ray_blocks.transpose(2, 1, 0).reshape(LIST * NB, AA),
        ray_tables.transpose(2, 1, 0).reshape(LIST * NB, AA),
    )
    wave_next, probe_next, object_next = pl.pallas_call(
        tail,
        out_shape=(
            jax.ShapeDtypeStruct((256, 128), F32),
            jax.ShapeDtypeStruct((2, 64, 64), F32),
            jax.ShapeDtypeStruct((512, 512), F32),
        ),
        in_specs=[vmem_spec] * 3,
        out_specs=[hbm_spec] * 3,
        scratch_shapes=[pltpu.SemaphoreType.DMA((6,))],
        compiler_params=pltpu.CompilerParams(vmem_limit_bytes=16 * 1024 * 1024),
        name="tail",
    )(*kept)
    return (
        wave_next.reshape(1, 2, 128, 128),
        probe_next,
        object_next.reshape(2, 2, 128, 512),
    )


def solution(mesh):
    specs = (
        P("aa", None, None, None),
        P("aa", None, None, "pb"),
        P("aa", "pb", None),
        P(),
        P("aa", "pb"),
        P("aa", "pb"),
        P("aa", "pb"),
        P(None, "aa", "pb", None),
        P(),
        P(),
        P(),
    )
    mapped = jax.shard_map(
        shards,
        mesh=mesh,
        in_specs=(P(),) + specs,
        out_specs=(P("aa", None, None, "pb"), P(), P(None, "aa", "pb", None)),
        check_vma=False,
    )

    def step(*arrays):
        return mapped(jnp.asarray(dft_constants()), *arrays)

    return step
```

```python
import math

import jax
import jax.numpy as jnp
import numpy as np
from jax import lax
from jax.experimental import pallas as pl
from jax.experimental.pallas import tpu as pltpu
from jax.sharding import PartitionSpec as P

BLK = 64
NW = 12
NB = 8
LIST = 12
AA = 64
PB = 4
ZC = 4
POS = 16
PAIRS = 8
OWN = 64 // PB
KEYS = 192
CHIPS = 32
SLOT = 16
SHARE = 272
FIRST = 144
WCH = 8
WROWS = 4096 // WCH
WIDE = 384

WAVE_STEP = 0.05
PENALTY = 1.0
PROBE_STEP = 0.05
OBJECT_STEP = 1.0

F32 = jnp.float32
BF16 = jnp.bfloat16


def dft_constants():
    index = np.arange(BLK)
    phase = (index[:, None] * index[None, :]) % BLK
    angle = phase.astype(np.float64) * (-2.0 * math.pi / BLK)
    f_re, f_im = np.cos(angle) / math.sqrt(BLK), np.sin(angle) / math.sqrt(BLK)
    pair = np.eye(2)

    def right(re, im):
        dre, dim = np.kron(pair, re), np.kron(pair, im)
        return np.block([[dre, dim], [-dim, dre]])

    def left(re, im):
        return np.block([[re, -im], [im, re]])

    order = np.concatenate([np.arange(0, BLK, 2), np.arange(1, BLK, 2)])
    rights = [right(f_re, f_im), right(f_re, -f_im)]
    lefts = np.concatenate(
        [left(f_re[order, :], f_im[order, :]), left(f_re[:, order], -f_im[:, order])], axis=1
    )
    return np.concatenate(rights + [lefts], axis=0).astype(np.float32)


def halves(value):
    high = value.astype(BF16)
    low = (value - high.astype(F32)).astype(BF16)
    return high, low


def dot(lhs, rhs):
    return jnp.dot(lhs, rhs, preferred_element_type=F32)


def right_apply(re, im, g_hi, g_lo):
    high, low = halves(jnp.concatenate([re, im], axis=1))
    out = dot(high, g_hi) + dot(low, g_hi) + dot(high, g_lo)
    return out[:, :128], out[:, 128:]


def left_apply(re, im, table):
    high, low = halves(jnp.concatenate([re, im], axis=0))
    out = dot(table, jnp.concatenate([high, low], axis=0))
    out = out[:128] + out[128:]
    return out[:64], out[64:]


def rows_to_lanes(value):
    return jnp.concatenate([value[q * 64 : (q + 1) * 64] for q in range(PAIRS)], axis=1)


def lanes_to_rows(value):
    return jnp.concatenate([value[:, q * 128 : (q + 1) * 128] for q in range(PAIRS)], axis=0)


def swap(value):
    return pltpu.roll(value, 64, 1)


def interleave(first, second):
    low = lax.broadcasted_iota(jnp.int32, first.shape, 1) < 64
    return jnp.where(low, first, swap(second)), jnp.where(low, swap(first), second)


def kernel(
    rows_ref,
    cols_ref,
    mask_ref,
    obj_hbm,
    wts_hbm,
    wave_hbm,
    dual_hbm,
    int_hbm,
    probe_hbm,
    tab_hbm,
    blocks_hbm,
    tables_hbm,
    wnext,
    pnext,
    onew,
    wts,
    obj,
    wave,
    dual,
    int_raw,
    inten,
    probe,
    tab_raw,
    tab,
    blocks,
    tables,
    colkey,
    lhs,
    ptile,
    stk,
    hit_r,
    hit_c,
    win_r,
    win_i,
    gra_r,
    gra_i,
    pad,
    acc,
    share,
    base,
    loose1,
    across1,
    arrived1,
    message1,
    recv1,
    loose2,
    misfit,
    across2,
    arrived2,
    message2,
    recv2,
    rays,
    spread,
    prow,
    pfull,
    probe_part,
    in_sem,
    w_sem,
    x_send,
    x_recv,
    a_send,
    a_recv,
):
    me_a = lax.axis_index("aa")
    me_p = lax.axis_index("pb")
    core = me_a % 2
    chip = me_a // 2
    sibling = me_a + 1 - 2 * core

    def lanes(shape):
        return lax.broadcasted_iota(jnp.int32, shape, 1)

    obj_in = [
        pltpu.make_async_copy(
            obj_hbm.at[:, pl.ds(t * 128, 128)], obj.at[pl.ds(t * 512, 512)], in_sem.at[t]
        )
        for t in range(4)
    ]
    wts_in = [
        pltpu.make_async_copy(
            wts_hbm.at[pl.ds(c * 1024, 1024), pl.ds(h * WIDE, WIDE)],
            wts.at[pl.ds(c * 1024, 1024), pl.ds(h * WIDE, WIDE)],
            w_sem.at[h * 4 + c],
        )
        for h in range(2)
        for c in range(4)
    ]
    wave_in = [
        pltpu.make_async_copy(
            wave_hbm.at[:, pl.ds(t * 128, 128)], wave.at[pl.ds(t * 256, 256)], in_sem.at[4 + t]
        )
        for t in range(4)
    ]
    others = {
        name: pltpu.make_async_copy(src, dst, in_sem.at[8 + n])
        for n, (name, src, dst) in enumerate(
            [
                ("blocks", blocks_hbm, blocks),
                ("tables", tables_hbm, tables),
                ("probe", probe_hbm, probe),
                ("tab", tab_hbm, tab_raw),
                ("inten", int_hbm, int_raw),
                ("dual", dual_hbm, dual),
            ]
        )
    }
    for copy in wave_in:
        copy.start()
    for name in ("probe", "tab", "inten"):
        others[name].start()
    barrier = pltpu.get_barrier_semaphore()

    for step in range(1, PB):
        pl.semaphore_signal(
            barrier,
            inc=1,
            device_id={"pb": lax.rem(me_p + step, PB)},
            device_id_type=pl.DeviceIdType.MESH,
        )
    for peer in [lax.rem(chip + step, CHIPS) * 2 + core for step in range(1, CHIPS)] + [sibling]:
        pl.semaphore_signal(
            barrier, inc=1, device_id={"aa": peer}, device_id_type=pl.DeviceIdType.MESH
        )
    for copy in obj_in + wts_in:
        copy.start()
    for name in ("dual", "blocks", "tables"):
        others[name].start()

    def clear(n, carry):
        for at in (0, 128):
            pad[pl.ds(pl.multiple_of(n * 192 + at, 64), 64), :] = jnp.zeros((64, 128), F32)
        return carry

    lax.fori_loop(0, 2 * POS, clear, 0)

    for copy in wave_in:
        copy.wait()

    def windows(q, carry):
        at = pl.multiple_of(q * 64, 64)
        for c, ref in ((0, win_r), (1, win_i)):
            found = []
            for h in range(2):
                row = rows_ref[0, 2 * q + h]
                col = cols_ref[0, 2 * q + h]
                tile = col // 128
                off = col % 128
                near = wave[pl.ds(tile * 256 + c * 128 + row, 64), :]
                far = wave[pl.ds(jnp.minimum(tile + 1, 3) * 256 + c * 128 + row, 64), :]
                both = jnp.where(lanes((64, 128)) >= off, near, far)
                found.append(pltpu.roll(both, (128 + 64 * h - off) % 128, 1))
            ref[pl.ds(at, 64), :] = jnp.where(lanes((64, 128)) < 64, found[0], found[1])
        return carry

    lax.fori_loop(0, PAIRS, windows, 0)
    others["probe"].wait()
    others["tab"].wait()
    others["inten"].wait()
    for octet in range(2):
        for t in range(32):
            inten[pl.ds(octet * 256 + t, 8, stride=32), :] = int_raw[
                octet * 8 : octet * 8 + 8, t * 128 : (t + 1) * 128
            ]
    for n in range(2):
        tab[2 * n], tab[2 * n + 1] = halves(tab_raw[n * 256 : (n + 1) * 256, :])
        high, low = halves(tab_raw[512:640, n * 128 : (n + 1) * 128])
        tab[4 + n] = jnp.concatenate(
            [jnp.concatenate([high] * 2, axis=1), jnp.concatenate([low] * 2, axis=1)], axis=0
        )
    one_re = jnp.concatenate([probe[0]] * 2, axis=1)
    one_im = jnp.concatenate([probe[1]] * 2, axis=1)
    p_re = jnp.concatenate([one_re] * PAIRS, axis=0)
    p_im = jnp.concatenate([one_im] * PAIRS, axis=0)
    w_re, w_im = win_r[...], win_i[...]
    half_re, half_im = right_apply(
        p_re * w_re - p_im * w_im, p_re * w_im + p_im * w_re, tab[0], tab[1]
    )
    far_re, far_im = left_apply(rows_to_lanes(half_re), rows_to_lanes(half_im), tab[4])
    measured, live = [], []
    for q in range(PAIRS):
        even, odd = interleave(
            inten[2 * q * 32 : 2 * q * 32 + 32, :], inten[2 * q * 32 + 32 : 2 * q * 32 + 64, :]
        )
        measured.append(jnp.concatenate([even, odd], axis=0))
        live.append(
            jnp.where(
                lanes((1, 128)) < 64, mask_ref[0, 2 * q].astype(F32), mask_ref[0, 2 * q + 1].astype(F32)
            )
        )
    measured = jnp.concatenate(measured, axis=1)
    live = jnp.concatenate(live, axis=1)
    factor = live * (far_re * far_re + far_im * far_im - measured)
    half_re, half_im = left_apply(factor * far_re, factor * far_im, tab[5])
    back_re, back_im = right_apply(lanes_to_rows(half_re), lanes_to_rows(half_im), tab[2], tab[3])
    gra_r[...] = p_re * back_re + p_im * back_im
    gra_i[...] = p_re * back_im - p_im * back_re
    grad_re = jnp.sum((w_re * back_re + w_im * back_im).reshape(PAIRS, 64, 128), axis=0)
    grad_im = jnp.sum((w_re * back_im - w_im * back_re).reshape(PAIRS, 64, 128), axis=0)
    grad_re = grad_re + swap(grad_re)
    grad_im = grad_im + swap(grad_im)
    probe_part[...] = jnp.where(lanes((64, 128)) < 64, grad_re, grad_im)

    def place(q, carry):
        at = pl.multiple_of(q * 64, 64)
        for h in range(2):
            turn = (cols_ref[0, 2 * q + h] + 128 - 64 * h) % 128
            for c, ref in ((0, gra_r), (1, gra_i)):
                slot = pl.multiple_of((4 * q + 2 * h + c) * 192 + 64, 64)
                pad[pl.ds(slot, 64), :] = pltpu.roll(ref[pl.ds(at, 64), :], turn, 1)
        return carry

    lax.fori_loop(0, PAIRS, place, 0)

    def to_x(stage, step, src, dst):
        peer = lax.rem(me_p + step, PB)
        return pltpu.make_async_remote_copy(
            src_ref=src,
            dst_ref=dst,
            send_sem=x_send.at[stage * 3 + step - 1],
            recv_sem=x_recv.at[stage * 3 + step - 1],
            device_id={"pb": peer},
            device_id_type=pl.DeviceIdType.MESH,
        )

    pl.semaphore_wait(barrier, CHIPS + PB - 1)
    reduces = [[], []]
    for half in range(2):
        for step in (2, 1, 3, 0):
            tile = lax.rem(me_p + step, PB)
            at = step * SHARE + half * FIRST
            for c in range(2):

                def add(n, total, c=c, tile=tile, half=half):
                    top = (2 * n + c) * 192 + 64 + half * 64 - rows_ref[0, n]
                    column = lanes((64, 128)) + (tile * 128 - cols_ref[0, n])
                    inside = (column >= 0) & (column < 64)
                    return total + jnp.where(inside, pad[pl.ds(top, 64), :], 0.0)

                acc[at + c * 64 : at + c * 64 + 64, :] = lax.fori_loop(
                    0, POS, add, jnp.zeros((64, 128), F32), unroll=8
                )
            if half == 0:
                acc[at + 128 : at + FIRST, :] = probe_part[
                    pl.ds(pl.multiple_of(tile * 16, 16), 16), :
                ]
            if step > 0:
                rows = FIRST if half == 0 else SHARE - FIRST
                copy = to_x(
                    half,
                    step,
                    acc.at[pl.ds(at, rows)],
                    share.at[pl.ds((step - 1) * SHARE + half * FIRST, rows)],
                )
                copy.start()
                reduces[half].append(copy)

    for copy in obj_in:
        copy.wait()

    def fold(q, carry):
        for t in range(4):
            even = obj[pl.ds(t * 512 + 2 * q, 8, stride=64), :]
            odd = obj[pl.ds(t * 512 + 2 * q + 1, 8, stride=64), :]
            first, second = interleave(even, odd)
            at = pl.multiple_of(q * 64 + t * 16, 16)
            lhs[pl.ds(at, 16), :] = jnp.concatenate([first, second], axis=0)
        return carry

    lax.fori_loop(0, 32, fold, 0, unroll=4)
    own_stk = pl.multiple_of(me_p * KEYS, KEYS)
    for half in range(2):
        products = jnp.zeros((64, WIDE), F32)
        for c in range(4):
            wts_in[half * 4 + c].wait()
            part = jnp.concatenate(
                [lhs[(c * 8 + n) * 64 : (c * 8 + n + 1) * 64, :] for n in range(8)], axis=1
            ).astype(BF16)
            products = products + dot(
                part, wts[c * 1024 : (c + 1) * 1024, half * WIDE : (half + 1) * WIDE]
            )
        for i in range(3):
            t = half * 3 + i
            ptile[t * 64 : (t + 1) * 64, :] = products[:, i * 128 : (i + 1) * 128]
            lists = [[], []], [[], []]
            for br in range(2):
                part = [ptile[pl.ds(t * 64 + cz * 2 + br, 8, stride=8), :] for cz in range(ZC)]
                for c in range(2):
                    even, odd = interleave(part[2 * c], part[2 * c + 1])
                    lists[0][c].append(even)
                    lists[1][c].append(odd)
            for h in range(2):
                for c in range(2):
                    stk[
                        pl.ds(pl.multiple_of(own_stk + (2 * t + h) * 16, 16), 16),
                        c * 128 : (c + 1) * 128,
                    ] = jnp.concatenate(lists[h][c], axis=0).astype(BF16)

    own_block = stk.at[pl.ds(own_stk, KEYS)]
    gathers = [to_x(2, step, own_block, own_block) for step in (2, 1, 3)]
    for copy in gathers:
        copy.start()

    others["blocks"].wait()
    others["tables"].wait()
    keys = []
    for jj in range(2):
        there = pl.ds(me_p * 2 + jj, LIST, stride=NB)
        block = blocks[there, :]
        keys.append((block // OWN) * KEYS + tables[there, :] * OWN + block % OWN)
    keys = jnp.concatenate(
        [jnp.concatenate(keys, axis=1), jnp.zeros((128 - LIST, 128), jnp.int32)], axis=0
    )
    keys = jnp.transpose(keys.astype(F32)).astype(jnp.int32)
    for t in range(6):
        column = lanes((128, 128)) + t * 128
        total = jnp.zeros((128, 128), F32)
        for e in range(LIST):
            total = total + jnp.where(keys[:, e : e + 1] == column, 1.0, 0.0)
        hit_r[:, t * 128 : (t + 1) * 128] = total.astype(BF16)

    for p in range(PB):
        parts = []
        for jj in range(2):
            there = pl.ds(p * 2 + jj, LIST, stride=NB)
            block = blocks[there, :]
            place = tables[there, :] * OWN + block % OWN
            parts.append(jnp.where(block // OWN == me_p, place, -1))
        colkey[:, p * 128 : (p + 1) * 128] = jnp.concatenate(parts, axis=1)
    for r in range(3):
        mine = lax.broadcasted_iota(jnp.int32, (64, 512), 0) + r * 64
        total = jnp.zeros((64, 512), F32)
        for e in range(LIST):
            total = total + jnp.where(colkey[e : e + 1, :] == mine, 1.0, 0.0)
        hit_c[r * 64 : (r + 1) * 64, :] = total.astype(BF16)

    def to_a(stage, peer, src, dst):
        return pltpu.make_async_remote_copy(
            src_ref=src,
            dst_ref=dst,
            send_sem=a_send.at[stage],
            recv_sem=a_recv.at[stage],
            device_id={"aa": peer},
            device_id_type=pl.DeviceIdType.MESH,
        )

    def swap_cores(stage, half, loose, extra, across, arrived):
        at = half * 80
        for k in range(4):
            across[at + k * 16 : at + k * 16 + 16, :] = loose[
                pl.ds(k * 64 + half * 32 + 1 - core, 16, stride=2), :
            ]
        rows = 64
        if extra is not None:
            across[64:80, :] = extra
            rows = 80
        copy = to_a(stage, sibling, across.at[pl.ds(at, rows)], arrived.at[pl.ds(at, rows)])
        copy.start()
        return copy

    def fill(half, loose, arrived, message):
        for k in range(4):
            message[pl.ds(half * 256 + core * 4 + k, 16, stride=SLOT), :] = loose[
                pl.ds(k * 64 + half * 32 + core, 16, stride=2), :
            ]
            message[pl.ds(half * 256 + (1 - core) * 4 + k, 16, stride=SLOT), :] = arrived[
                half * 80 + k * 16 : half * 80 + k * 16 + 16, :
            ]

    def exchange(stage, half, message, target, count):
        here = pl.ds(pl.multiple_of(chip * SLOT, SLOT), count)

        def send(step):
            there = half * 16 + lax.rem(chip + step, 16)
            to_a(
                stage,
                there * 2 + core,
                message.at[pl.ds(pl.multiple_of(there * SLOT, SLOT), count)],
                target.at[here],
            ).start()

        for step in range(1, 16):
            send(step)
        pl.when(chip // 16 != half)(lambda: send(0))

        @pl.when(chip // 16 == half)
        def _():
            target[here, :] = message[here, :]

        rows = (CHIPS - 1) * count
        return to_a(
            stage,
            lax.rem(chip + 1, CHIPS) * 2 + core,
            message.at[pl.ds(0, rows)],
            target.at[pl.ds(0, rows)],
        )

    others["dual"].wait()
    swaps = []
    for half in range(2):
        for copy in reduces[half]:
            copy.wait_recv()
        for c in range(2):
            at = half * FIRST + c * 64
            gradient = acc[at : at + 64, :]
            for n in range(PB - 1):
                gradient = gradient + share[n * SHARE + at : n * SHARE + at + 64, :]
            top = c * 128 + half * 64
            mine = wave[pl.ds(pl.multiple_of(me_p * 256 + top, 64), 64), :]
            base[top : top + 64, :] = mine - WAVE_STEP * (
                gradient + PENALTY * (mine + dual[top : top + 64, :])
            )
            for z in range(2):
                there = pl.ds(top + z, 32, stride=2)
                k = 2 * c + z
                loose1[k * 64 + half * 32 : k * 64 + half * 32 + 32, :] = (
                    base[there, :] + dual[there, :]
                )
        probe_share = None
        if half == 0:
            probe_share = acc[128:FIRST, :]
            for n in range(PB - 1):
                probe_share = probe_share + share[n * SHARE + 128 : n * SHARE + FIRST, :]
        swaps.append(swap_cores(half, half, loose1, probe_share, across1, arrived1))
        swaps[-1].wait_recv()
        fill(half, loose1, arrived1, message1)
        if half == 0:
            probe_chip = probe_share + arrived1[64:80, :]
            message1[pl.ds(8, 32, stride=SLOT), :] = jnp.concatenate([probe_chip] * 2, axis=0)
        move1 = exchange(2, half, message1, recv1, 9)

    for copy in gathers:
        copy.wait_recv()
    projection = dot(hit_r[...], stk[...])
    for c in range(2):
        first, second = interleave(
            projection[:64, c * 128 : (c + 1) * 128], projection[64:, c * 128 : (c + 1) * 128]
        )
        loose2[2 * c * 64 : 2 * c * 64 + 64, :] = first
        loose2[2 * c * 64 + 64 : 2 * c * 64 + 128, :] = second

    later = [swap_cores(3 + half, half, loose2, None, across2, arrived2) for half in range(2)]
    for half in range(2):
        later[half].wait_recv()
        fill(half, loose2, arrived2, message2)
    swaps += later

    move1.wait_recv()
    for half in range(2):
        for k in range(4):
            there = pl.ds(k * 64 + half, 32, stride=2)
            own = loose2[there, :]
            rest = recv1[pl.ds(half * 4 + k, 32, stride=SLOT), :]
            misfit[there, :] = own - (rest + (WAVE_STEP * PENALTY) * own)
    own_rays = pl.multiple_of(me_p * 128, 128)
    for c in range(2):
        first, second = interleave(
            misfit[2 * c * 64 : 2 * c * 64 + 64, :], misfit[2 * c * 64 + 64 : 2 * c * 64 + 128, :]
        )
        rays[pl.ds(own_rays, 128), c * 128 : (c + 1) * 128] = jnp.concatenate(
            [first, second], axis=0
        ).astype(BF16)
    own_rows = rays.at[pl.ds(own_rays, 128)]
    ray_moves = [to_x(3, step, own_rows, own_rows) for step in (2, 1, 3)]
    for copy in ray_moves:
        copy.start()

    own_row = pl.ds(pl.multiple_of(me_p * 8, 8), 1)
    prow[own_row, :] = jnp.sum(recv1[pl.ds(8, 32, stride=SLOT), :], axis=0, keepdims=True)
    probe_x = [to_x(4, step, prow.at[own_row], prow.at[own_row]) for step in (2, 1, 3)]
    for copy in probe_x:
        copy.start()

    for half in range(2):
        move2 = exchange(5, half, message2, recv2, 8)

    for copy in probe_x:
        copy.wait_recv()
    kind = chip % 16
    own_four = pl.ds(pl.multiple_of(kind * 8, 8), 4)
    pfull[own_four, :] = jnp.concatenate([prow[p * 8 : p * 8 + 1, :] for p in range(PB)], axis=0)

    def share_rows(step):
        four = pfull.at[own_four]
        return to_a(6, (chip - kind + lax.rem(kind + step, 16)) * 2 + core, four, four)

    for step in range(1, 16):
        share_rows(step).start()

    for copy in ray_moves:
        copy.wait_recv()

    sums = dot(hit_c[...], rays[...]).astype(BF16).astype(F32)
    for t in range(6):
        for br in range(2):
            for c in range(2):
                at = 2 * t * 16 + br * 8
                first, second = interleave(
                    sums[at : at + 8, c * 128 : (c + 1) * 128],
                    sums[at + 16 : at + 24, c * 128 : (c + 1) * 128],
                )
                spread[pl.ds(t * 64 + 4 * c + br, 8, stride=8), :] = first
                spread[pl.ds(t * 64 + 4 * c + 2 + br, 8, stride=8), :] = second
    table = jnp.concatenate(
        [spread[t * 64 : (t + 1) * 64, :] for t in range(6)], axis=1
    ).astype(BF16)

    for n in range(WCH):
        grad = lax.dot_general(
            table,
            wts[n * WROWS : (n + 1) * WROWS, :],
            (((1,), (1,)), ((), ())),
            preferred_element_type=F32,
        )
        per = 32 // WCH
        for s in range(per):
            q = n * per + s
            for t in range(4):
                first, second = interleave(
                    grad[t * 16 : t * 16 + 8, s * 128 : (s + 1) * 128],
                    grad[t * 16 + 8 : t * 16 + 16, s * 128 : (s + 1) * 128],
                )
                even = pl.ds(t * 512 + 2 * q, 8, stride=64)
                odd = pl.ds(t * 512 + 2 * q + 1, 8, stride=64)
                onew[even, :] = obj[even, :] - OBJECT_STEP * first
                onew[odd, :] = obj[odd, :] - OBJECT_STEP * second

    move2.wait_recv()
    for half in range(2):
        for c in range(2):
            for z in range(2):
                there = pl.ds(c * 128 + 2 * half + z, 32, stride=4)
                here = recv2[pl.ds(half * 4 + 2 * c + z, 32, stride=SLOT), :]
                wnext[there, :] = base[there, :] + (WAVE_STEP * PENALTY) * here
    sixty = pfull.at[pl.ds(0, 60)]
    probe_all = to_a(6, (chip - kind + lax.rem(kind + 1, 16)) * 2 + core, sixty, sixty)
    probe_all.wait_recv()
    total = jnp.concatenate([pfull[pl.ds(p, 16, stride=8), :] for p in range(PB)], axis=0)
    scale = PROBE_STEP / (AA * POS * PB)
    pnext[0] = probe[0] - scale * total[:, :64]
    pnext[1] = probe[1] - scale * swap(total)[:, :64]

    xs = gathers + reduces[0] + reduces[1] + probe_x + ray_moves
    for copy in xs + swaps + [move1, move2, probe_all]:
        copy.wait_send()


def tail(wnext, pnext, onew, wave_out, probe_out, obj_out, sem):
    pairs = [
        (onew.at[pl.ds(t * 512, 512)], obj_out.at[:, pl.ds(t * 128, 128)]) for t in range(4)
    ] + [(wnext, wave_out), (pnext, probe_out)]
    copies = [pltpu.make_async_copy(src, dst, sem.at[n]) for n, (src, dst) in enumerate(pairs)]
    for copy in copies:
        copy.start()
    for copy in copies:
        copy.wait()


def shards(
    tables,
    wave_field,
    scaled_dual,
    intensity,
    probe_field,
    scan_rows,
    scan_cols,
    sample_mask,
    object_field,
    ray_blocks,
    ray_tables,
    radon_weights,
):
    smem = pl.BlockSpec(memory_space=pltpu.SMEM)
    vmem = pltpu.VMEM
    hbm_spec = pl.BlockSpec(memory_space=pltpu.HBM)
    vmem_spec = pl.BlockSpec(memory_space=pltpu.VMEM)
    kept = pl.pallas_call(
        kernel,
        out_shape=(
            pltpu.VMEM((256, 128), F32),
            pltpu.VMEM((2, 64, 64), F32),
            pltpu.VMEM((2048, 128), F32),
        ),
        in_specs=[smem] * 3 + [hbm_spec] * 9,
        out_specs=[vmem_spec] * 3,
        scratch_shapes=[
            vmem((4096, 768), BF16),
            vmem((2048, 128), F32),
            vmem((1024, 128), F32),
            vmem((256, 128), F32),
            vmem((POS, 4096), F32),
            vmem((POS * 32, 128), F32),
            vmem((2, 64, 64), F32),
            vmem((640, 256), F32),
            vmem((6, 256, 256), BF16),
            vmem((LIST * NB, AA), jnp.int32),
            vmem((LIST * NB, AA), jnp.int32),
            vmem((LIST, 512), jnp.int32),
            vmem((2048, 128), F32),
            vmem((384, 128), F32),
            vmem((768, 256), BF16),
            vmem((128, 768), BF16),
            vmem((KEYS, 512), BF16),
            vmem((512, 128), F32),
            vmem((512, 128), F32),
            vmem((512, 128), F32),
            vmem((512, 128), F32),
            vmem((2 * POS * 192, 128), F32),
            vmem((PB * SHARE, 128), F32),
            vmem(((PB - 1) * SHARE, 128), F32),
            vmem((256, 128), F32),
            vmem((256, 128), F32),
            vmem((144, 128), F32),
            vmem((144, 128), F32),
            vmem((CHIPS * SLOT, 128), F32),
            vmem((CHIPS * SLOT, 128), F32),
            vmem((256, 128), F32),
            vmem((256, 128), F32),
            vmem((144, 128), F32),
            vmem((144, 128), F32),
            vmem((CHIPS * SLOT, 128), F32),
            vmem((CHIPS * SLOT, 128), F32),
            vmem((512, 256), BF16),
            vmem((384, 128), F32),
            vmem((32, 128), F32),
            vmem((128, 128), F32),
            vmem((64, 128), F32),
            pltpu.SemaphoreType.DMA((14,)),
            pltpu.SemaphoreType.DMA((WCH,)),
            pltpu.SemaphoreType.DMA((15,)),
            pltpu.SemaphoreType.DMA((15,)),
            pltpu.SemaphoreType.DMA((7,)),
            pltpu.SemaphoreType.DMA((7,)),
        ],
        compiler_params=pltpu.CompilerParams(
            collective_id=0, has_side_effects=True, vmem_limit_bytes=60 * 1024 * 1024
        ),
        name="admm",
    )(
        scan_rows,
        scan_cols,
        sample_mask,
        object_field.reshape(512, 512),
        radon_weights,
        wave_field.reshape(256, 512),
        scaled_dual.reshape(256, 128),
        intensity.reshape(POS, 4096),
        probe_field,
        tables,
        ray_blocks.transpose(2, 1, 0).reshape(LIST * NB, AA),
        ray_tables.transpose(2, 1, 0).reshape(LIST * NB, AA),
    )
    wave_next, probe_next, object_next = pl.pallas_call(
        tail,
        out_shape=(
            jax.ShapeDtypeStruct((256, 128), F32),
            jax.ShapeDtypeStruct((2, 64, 64), F32),
            jax.ShapeDtypeStruct((512, 512), F32),
        ),
        in_specs=[vmem_spec] * 3,
        out_specs=[hbm_spec] * 3,
        scratch_shapes=[pltpu.SemaphoreType.DMA((6,))],
        compiler_params=pltpu.CompilerParams(vmem_limit_bytes=16 * 1024 * 1024),
        name="tail",
    )(*kept)
    return (
        wave_next.reshape(1, 2, 128, 128),
        probe_next,
        object_next.reshape(2, 2, 128, 512),
    )


def solution(mesh):
    specs = (
        P("aa", None, None, None),
        P("aa", None, None, "pb"),
        P("aa", "pb", None),
        P(),
        P("aa", "pb"),
        P("aa", "pb"),
        P("aa", "pb"),
        P(None, "aa", "pb", None),
        P(),
        P(),
        P(),
    )
    mapped = jax.shard_map(
        shards,
        mesh=mesh,
        in_specs=(P(),) + specs,
        out_specs=(P("aa", None, None, "pb"), P(), P(None, "aa", "pb", None)),
        check_vma=False,
    )

    def step(*arrays):
        return mapped(jnp.asarray(dft_constants()), *arrays)

    return step
```

```python
import math

import jax
import jax.numpy as jnp
import numpy as np
from jax import lax
from jax.experimental import pallas as pl
from jax.experimental.pallas import tpu as pltpu
from jax.sharding import PartitionSpec as P

BLK = 64
NW = 12
NB = 8
LIST = 12
AA = 64
PB = 4
ZC = 4
POS = 16
PAIRS = 8
OWN = 64 // PB
KEYS = 192
CHIPS = 32
SLOT = 16
SHARE = 272
FIRST = 144
WCH = 8
WROWS = 4096 // WCH
WIDE = 384

WAVE_STEP = 0.05
PENALTY = 1.0
PROBE_STEP = 0.05
OBJECT_STEP = 1.0

F32 = jnp.float32
BF16 = jnp.bfloat16


def dft_constants():
    index = np.arange(BLK)
    phase = (index[:, None] * index[None, :]) % BLK
    angle = phase.astype(np.float64) * (-2.0 * math.pi / BLK)
    f_re, f_im = np.cos(angle) / math.sqrt(BLK), np.sin(angle) / math.sqrt(BLK)
    pair = np.eye(2)

    def right(re, im):
        dre, dim = np.kron(pair, re), np.kron(pair, im)
        return np.block([[dre, dim], [-dim, dre]])

    def left(re, im):
        return np.block([[re, -im], [im, re]])

    order = np.concatenate([np.arange(0, BLK, 2), np.arange(1, BLK, 2)])
    rights = [right(f_re, f_im), right(f_re, -f_im)]
    lefts = np.concatenate(
        [left(f_re[order, :], f_im[order, :]), left(f_re[:, order], -f_im[:, order])], axis=1
    )
    return np.concatenate(rights + [lefts], axis=0).astype(np.float32)


def halves(value):
    high = value.astype(BF16)
    low = (value - high.astype(F32)).astype(BF16)
    return high, low


def dot(lhs, rhs):
    return jnp.dot(lhs, rhs, preferred_element_type=F32)


def right_apply(re, im, g_hi, g_lo):
    high, low = halves(jnp.concatenate([re, im], axis=1))
    out = dot(high, g_hi) + dot(low, g_hi) + dot(high, g_lo)
    return out[:, :128], out[:, 128:]


def left_apply(re, im, table):
    high, low = halves(jnp.concatenate([re, im], axis=0))
    out = dot(table, jnp.concatenate([high, low], axis=0))
    out = out[:128] + out[128:]
    return out[:64], out[64:]


def rows_to_lanes(value):
    return jnp.concatenate([value[q * 64 : (q + 1) * 64] for q in range(PAIRS)], axis=1)


def lanes_to_rows(value):
    return jnp.concatenate([value[:, q * 128 : (q + 1) * 128] for q in range(PAIRS)], axis=0)


def swap(value):
    return pltpu.roll(value, 64, 1)


def interleave(first, second):
    low = lax.broadcasted_iota(jnp.int32, first.shape, 1) < 64
    return jnp.where(low, first, swap(second)), jnp.where(low, swap(first), second)


def kernel(
    rows_ref,
    cols_ref,
    mask_ref,
    obj_hbm,
    wts_hbm,
    wave_hbm,
    dual_hbm,
    int_hbm,
    probe_hbm,
    tab_hbm,
    blocks_hbm,
    tables_hbm,
    wnext,
    pnext,
    onew,
    wts,
    wts_t,
    obj,
    wave,
    dual,
    int_raw,
    inten,
    probe,
    tab_raw,
    tab,
    blocks,
    tables,
    colkey,
    lhs,
    ptile,
    stk,
    hit_r,
    hit_c,
    win_r,
    win_i,
    gra_r,
    gra_i,
    pad,
    acc,
    share,
    base,
    loose1,
    across1,
    arrived1,
    message1,
    recv1,
    loose2,
    misfit,
    across2,
    arrived2,
    message2,
    recv2,
    rays,
    spread,
    prow,
    pfull,
    probe_part,
    in_sem,
    w_sem,
    x_send,
    x_recv,
    a_send,
    a_recv,
):
    me_a = lax.axis_index("aa")
    me_p = lax.axis_index("pb")
    core = me_a % 2
    chip = me_a // 2
    sibling = me_a + 1 - 2 * core

    def lanes(shape):
        return lax.broadcasted_iota(jnp.int32, shape, 1)

    obj_in = [
        pltpu.make_async_copy(
            obj_hbm.at[:, pl.ds(t * 128, 128)], obj.at[pl.ds(t * 512, 512)], in_sem.at[t]
        )
        for t in range(4)
    ]
    wts_in = [
        pltpu.make_async_copy(
            wts_hbm.at[pl.ds(c * 1024, 1024), pl.ds(h * WIDE, WIDE)],
            wts.at[pl.ds(c * 1024, 1024), pl.ds(h * WIDE, WIDE)],
            w_sem.at[h * 4 + c],
        )
        for h in range(2)
        for c in range(4)
    ]
    wave_in = [
        pltpu.make_async_copy(
            wave_hbm.at[:, pl.ds(t * 128, 128)], wave.at[pl.ds(t * 256, 256)], in_sem.at[4 + t]
        )
        for t in range(4)
    ]
    others = {
        name: pltpu.make_async_copy(src, dst, in_sem.at[8 + n])
        for n, (name, src, dst) in enumerate(
            [
                ("blocks", blocks_hbm, blocks),
                ("tables", tables_hbm, tables),
                ("probe", probe_hbm, probe),
                ("tab", tab_hbm, tab_raw),
                ("inten", int_hbm, int_raw),
                ("dual", dual_hbm, dual),
            ]
        )
    }
    for copy in wave_in:
        copy.start()
    for name in ("probe", "tab", "inten"):
        others[name].start()
    barrier = pltpu.get_barrier_semaphore()

    for step in range(1, PB):
        pl.semaphore_signal(
            barrier,
            inc=1,
            device_id={"pb": lax.rem(me_p + step, PB)},
            device_id_type=pl.DeviceIdType.MESH,
        )
    for peer in [lax.rem(chip + step, CHIPS) * 2 + core for step in range(1, CHIPS)] + [sibling]:
        pl.semaphore_signal(
            barrier, inc=1, device_id={"aa": peer}, device_id_type=pl.DeviceIdType.MESH
        )
    for copy in obj_in + wts_in:
        copy.start()
    for name in ("dual", "blocks", "tables"):
        others[name].start()

    def clear(n, carry):
        for at in (0, 128):
            pad[pl.ds(pl.multiple_of(n * 192 + at, 64), 64), :] = jnp.zeros((64, 128), F32)
        return carry

    lax.fori_loop(0, 2 * POS, clear, 0)

    for copy in wave_in:
        copy.wait()

    def windows(q, carry):
        at = pl.multiple_of(q * 64, 64)
        for c, ref in ((0, win_r), (1, win_i)):
            found = []
            for h in range(2):
                row = rows_ref[0, 2 * q + h]
                col = cols_ref[0, 2 * q + h]
                tile = col // 128
                off = col % 128
                near = wave[pl.ds(tile * 256 + c * 128 + row, 64), :]
                far = wave[pl.ds(jnp.minimum(tile + 1, 3) * 256 + c * 128 + row, 64), :]
                both = jnp.where(lanes((64, 128)) >= off, near, far)
                found.append(pltpu.roll(both, (128 + 64 * h - off) % 128, 1))
            ref[pl.ds(at, 64), :] = jnp.where(lanes((64, 128)) < 64, found[0], found[1])
        return carry

    lax.fori_loop(0, PAIRS, windows, 0)
    others["probe"].wait()
    others["tab"].wait()
    others["inten"].wait()
    for octet in range(2):
        for t in range(32):
            inten[pl.ds(octet * 256 + t, 8, stride=32), :] = int_raw[
                octet * 8 : octet * 8 + 8, t * 128 : (t + 1) * 128
            ]
    for n in range(2):
        tab[2 * n], tab[2 * n + 1] = halves(tab_raw[n * 256 : (n + 1) * 256, :])
        high, low = halves(tab_raw[512:640, n * 128 : (n + 1) * 128])
        tab[4 + n] = jnp.concatenate(
            [jnp.concatenate([high] * 2, axis=1), jnp.concatenate([low] * 2, axis=1)], axis=0
        )
    one_re = jnp.concatenate([probe[0]] * 2, axis=1)
    one_im = jnp.concatenate([probe[1]] * 2, axis=1)
    p_re = jnp.concatenate([one_re] * PAIRS, axis=0)
    p_im = jnp.concatenate([one_im] * PAIRS, axis=0)
    w_re, w_im = win_r[...], win_i[...]
    half_re, half_im = right_apply(
        p_re * w_re - p_im * w_im, p_re * w_im + p_im * w_re, tab[0], tab[1]
    )
    far_re, far_im = left_apply(rows_to_lanes(half_re), rows_to_lanes(half_im), tab[4])
    measured, live = [], []
    for q in range(PAIRS):
        even, odd = interleave(
            inten[2 * q * 32 : 2 * q * 32 + 32, :], inten[2 * q * 32 + 32 : 2 * q * 32 + 64, :]
        )
        measured.append(jnp.concatenate([even, odd], axis=0))
        live.append(
            jnp.where(
                lanes((1, 128)) < 64, mask_ref[0, 2 * q].astype(F32), mask_ref[0, 2 * q + 1].astype(F32)
            )
        )
    measured = jnp.concatenate(measured, axis=1)
    live = jnp.concatenate(live, axis=1)
    factor = live * (far_re * far_re + far_im * far_im - measured)
    half_re, half_im = left_apply(factor * far_re, factor * far_im, tab[5])
    back_re, back_im = right_apply(lanes_to_rows(half_re), lanes_to_rows(half_im), tab[2], tab[3])
    gra_r[...] = p_re * back_re + p_im * back_im
    gra_i[...] = p_re * back_im - p_im * back_re
    grad_re = jnp.sum((w_re * back_re + w_im * back_im).reshape(PAIRS, 64, 128), axis=0)
    grad_im = jnp.sum((w_re * back_im - w_im * back_re).reshape(PAIRS, 64, 128), axis=0)
    grad_re = grad_re + swap(grad_re)
    grad_im = grad_im + swap(grad_im)
    probe_part[...] = jnp.where(lanes((64, 128)) < 64, grad_re, grad_im)

    def place(q, carry):
        at = pl.multiple_of(q * 64, 64)
        for h in range(2):
            turn = (cols_ref[0, 2 * q + h] + 128 - 64 * h) % 128
            for c, ref in ((0, gra_r), (1, gra_i)):
                slot = pl.multiple_of((4 * q + 2 * h + c) * 192 + 64, 64)
                pad[pl.ds(slot, 64), :] = pltpu.roll(ref[pl.ds(at, 64), :], turn, 1)
        return carry

    lax.fori_loop(0, PAIRS, place, 0)

    def to_x(stage, step, src, dst):
        peer = lax.rem(me_p + step, PB)
        return pltpu.make_async_remote_copy(
            src_ref=src,
            dst_ref=dst,
            send_sem=x_send.at[stage * 3 + step - 1],
            recv_sem=x_recv.at[stage * 3 + step - 1],
            device_id={"pb": peer},
            device_id_type=pl.DeviceIdType.MESH,
        )

    early = chip // 4 < 2

    def turn():
        for n in range(WCH):
            part = slice(n * WROWS, (n + 1) * WROWS)
            wts_t[:, part] = jnp.transpose(wts[part, :])

    @pl.when(early)
    def _():
        for copy in wts_in:
            copy.wait()
        turn()

    pfull[...] = jnp.zeros_like(pfull)
    pl.semaphore_wait(barrier, CHIPS + PB - 1)
    reduces = [[], []]
    for half in range(2):
        for step in (2, 1, 3, 0):
            tile = lax.rem(me_p + step, PB)
            at = step * SHARE + half * FIRST
            for c in range(2):

                def add(n, total, c=c, tile=tile, half=half):
                    top = (2 * n + c) * 192 + 64 + half * 64 - rows_ref[0, n]
                    column = lanes((64, 128)) + (tile * 128 - cols_ref[0, n])
                    inside = (column >= 0) & (column < 64)
                    return total + jnp.where(inside, pad[pl.ds(top, 64), :], 0.0)

                acc[at + c * 64 : at + c * 64 + 64, :] = lax.fori_loop(
                    0, POS, add, jnp.zeros((64, 128), F32), unroll=8
                )
            if half == 0:
                acc[at + 128 : at + FIRST, :] = probe_part[
                    pl.ds(pl.multiple_of(tile * 16, 16), 16), :
                ]
            if step > 0:
                rows = FIRST if half == 0 else SHARE - FIRST
                copy = to_x(
                    half,
                    step,
                    acc.at[pl.ds(at, rows)],
                    share.at[pl.ds((step - 1) * SHARE + half * FIRST, rows)],
                )
                copy.start()
                reduces[half].append(copy)

    for copy in obj_in:
        copy.wait()

    def fold(q, carry):
        for t in range(4):
            even = obj[pl.ds(t * 512 + 2 * q, 8, stride=64), :]
            odd = obj[pl.ds(t * 512 + 2 * q + 1, 8, stride=64), :]
            first, second = interleave(even, odd)
            at = pl.multiple_of(q * 64 + t * 16, 16)
            lhs[pl.ds(at, 16), :] = jnp.concatenate([first, second], axis=0)
        return carry

    lax.fori_loop(0, 32, fold, 0, unroll=4)
    own_stk = pl.multiple_of(me_p * KEYS, KEYS)
    for half in range(2):
        products = jnp.zeros((64, WIDE), F32)
        for c in range(4):
            pl.when(jnp.logical_not(early))(wts_in[half * 4 + c].wait)
            part = jnp.concatenate(
                [lhs[(c * 8 + n) * 64 : (c * 8 + n + 1) * 64, :] for n in range(8)], axis=1
            ).astype(BF16)
            products = products + dot(
                part, wts[c * 1024 : (c + 1) * 1024, half * WIDE : (half + 1) * WIDE]
            )
        for i in range(3):
            t = half * 3 + i
            ptile[t * 64 : (t + 1) * 64, :] = products[:, i * 128 : (i + 1) * 128]
            lists = [[], []], [[], []]
            for br in range(2):
                part = [ptile[pl.ds(t * 64 + cz * 2 + br, 8, stride=8), :] for cz in range(ZC)]
                for c in range(2):
                    even, odd = interleave(part[2 * c], part[2 * c + 1])
                    lists[0][c].append(even)
                    lists[1][c].append(odd)
            for h in range(2):
                for c in range(2):
                    stk[
                        pl.ds(pl.multiple_of(own_stk + (2 * t + h) * 16, 16), 16),
                        c * 128 : (c + 1) * 128,
                    ] = jnp.concatenate(lists[h][c], axis=0).astype(BF16)

    own_block = stk.at[pl.ds(own_stk, KEYS)]
    gathers = [to_x(2, step, own_block, own_block) for step in (2, 1, 3)]
    for copy in gathers:
        copy.start()

    others["blocks"].wait()
    others["tables"].wait()
    keys = []
    for jj in range(2):
        there = pl.ds(me_p * 2 + jj, LIST, stride=NB)
        block = blocks[there, :]
        keys.append((block // OWN) * KEYS + tables[there, :] * OWN + block % OWN)
    keys = jnp.concatenate(
        [jnp.concatenate(keys, axis=1), jnp.zeros((128 - LIST, 128), jnp.int32)], axis=0
    )
    keys = jnp.transpose(keys.astype(F32)).astype(jnp.int32)
    for t in range(6):
        column = lanes((128, 128)) + t * 128
        total = jnp.zeros((128, 128), F32)
        for e in range(LIST):
            total = total + jnp.where(keys[:, e : e + 1] == column, 1.0, 0.0)
        hit_r[:, t * 128 : (t + 1) * 128] = total.astype(BF16)

    for p in range(PB):
        parts = []
        for jj in range(2):
            there = pl.ds(p * 2 + jj, LIST, stride=NB)
            block = blocks[there, :]
            place = tables[there, :] * OWN + block % OWN
            parts.append(jnp.where(block // OWN == me_p, place, -1))
        colkey[:, p * 128 : (p + 1) * 128] = jnp.concatenate(parts, axis=1)
    for r in range(3):
        mine = lax.broadcasted_iota(jnp.int32, (64, 512), 0) + r * 64
        total = jnp.zeros((64, 512), F32)
        for e in range(LIST):
            total = total + jnp.where(colkey[e : e + 1, :] == mine, 1.0, 0.0)
        hit_c[r * 64 : (r + 1) * 64, :] = total.astype(BF16)

    def to_a(stage, peer, src, dst):
        return pltpu.make_async_remote_copy(
            src_ref=src,
            dst_ref=dst,
            send_sem=a_send.at[stage],
            recv_sem=a_recv.at[stage],
            device_id={"aa": peer},
            device_id_type=pl.DeviceIdType.MESH,
        )

    def swap_cores(stage, half, loose, extra, across, arrived):
        at = half * 80
        for k in range(4):
            across[at + k * 16 : at + k * 16 + 16, :] = loose[
                pl.ds(k * 64 + half * 32 + 1 - core, 16, stride=2), :
            ]
        rows = 64
        if extra is not None:
            across[64:80, :] = extra
            rows = 80
        copy = to_a(stage, sibling, across.at[pl.ds(at, rows)], arrived.at[pl.ds(at, rows)])
        copy.start()
        return copy

    def fill(half, loose, arrived, message):
        for k in range(4):
            message[pl.ds(half * 256 + core * 4 + k, 16, stride=SLOT), :] = loose[
                pl.ds(k * 64 + half * 32 + core, 16, stride=2), :
            ]
            message[pl.ds(half * 256 + (1 - core) * 4 + k, 16, stride=SLOT), :] = arrived[
                half * 80 + k * 16 : half * 80 + k * 16 + 16, :
            ]

    def exchange(stage, half, message, target, count):
        here = pl.ds(pl.multiple_of(chip * SLOT, SLOT), count)

        def send(step):
            there = half * 16 + lax.rem(chip + step, 16)
            to_a(
                stage,
                there * 2 + core,
                message.at[pl.ds(pl.multiple_of(there * SLOT, SLOT), count)],
                target.at[here],
            ).start()

        for step in range(1, 16):
            send(step)
        pl.when(chip // 16 != half)(lambda: send(0))

        @pl.when(chip // 16 == half)
        def _():
            target[here, :] = message[here, :]

        rows = (CHIPS - 1) * count
        return to_a(
            stage,
            lax.rem(chip + 1, CHIPS) * 2 + core,
            message.at[pl.ds(0, rows)],
            target.at[pl.ds(0, rows)],
        )

    others["dual"].wait()
    swaps = []
    for half in range(2):
        for copy in reduces[half]:
            copy.wait_recv()
        for c in range(2):
            at = half * FIRST + c * 64
            gradient = acc[at : at + 64, :]
            for n in range(PB - 1):
                gradient = gradient + share[n * SHARE + at : n * SHARE + at + 64, :]
            top = c * 128 + half * 64
            mine = wave[pl.ds(pl.multiple_of(me_p * 256 + top, 64), 64), :]
            base[top : top + 64, :] = mine - WAVE_STEP * (
                gradient + PENALTY * (mine + dual[top : top + 64, :])
            )
            for z in range(2):
                there = pl.ds(top + z, 32, stride=2)
                k = 2 * c + z
                loose1[k * 64 + half * 32 : k * 64 + half * 32 + 32, :] = (
                    base[there, :] + dual[there, :]
                )
        probe_share = None
        if half == 0:
            probe_share = acc[128:FIRST, :]
            for n in range(PB - 1):
                probe_share = probe_share + share[n * SHARE + 128 : n * SHARE + FIRST, :]
        swaps.append(swap_cores(half, half, loose1, probe_share, across1, arrived1))
        swaps[-1].wait_recv()
        fill(half, loose1, arrived1, message1)
        if half == 0:
            probe_chip = probe_share + arrived1[64:80, :]
            message1[pl.ds(8, 32, stride=SLOT), :] = jnp.concatenate([probe_chip] * 2, axis=0)
        move1 = exchange(2, half, message1, recv1, 9)
    pl.when(jnp.logical_not(early))(turn)

    for copy in gathers:
        copy.wait_recv()
    projection = dot(hit_r[...], stk[...])
    for c in range(2):
        first, second = interleave(
            projection[:64, c * 128 : (c + 1) * 128], projection[64:, c * 128 : (c + 1) * 128]
        )
        loose2[2 * c * 64 : 2 * c * 64 + 64, :] = first
        loose2[2 * c * 64 + 64 : 2 * c * 64 + 128, :] = second

    later = [swap_cores(3 + half, half, loose2, None, across2, arrived2) for half in range(2)]
    for half in range(2):
        later[half].wait_recv()
        fill(half, loose2, arrived2, message2)
    swaps += later

    move1.wait_recv()
    for half in range(2):
        for k in range(4):
            there = pl.ds(k * 64 + half, 32, stride=2)
            own = loose2[there, :]
            rest = recv1[pl.ds(half * 4 + k, 32, stride=SLOT), :]
            misfit[there, :] = own - (rest + (WAVE_STEP * PENALTY) * own)
    own_rays = pl.multiple_of(me_p * 128, 128)
    for c in range(2):
        first, second = interleave(
            misfit[2 * c * 64 : 2 * c * 64 + 64, :], misfit[2 * c * 64 + 64 : 2 * c * 64 + 128, :]
        )
        rays[pl.ds(own_rays, 128), c * 128 : (c + 1) * 128] = jnp.concatenate(
            [first, second], axis=0
        ).astype(BF16)
    own_rows = rays.at[pl.ds(own_rays, 128)]
    ray_moves = [to_x(3, step, own_rows, own_rows) for step in (2, 1, 3)]
    for copy in ray_moves:
        copy.start()

    own_row = pl.ds(pl.multiple_of(me_p * 8, 8), 1)
    prow[own_row, :] = jnp.sum(recv1[pl.ds(8, 32, stride=SLOT), :], axis=0, keepdims=True)
    probe_x = [to_x(4, step, prow.at[own_row], prow.at[own_row]) for step in (2, 1, 3)]
    for copy in probe_x:
        copy.start()

    for half in range(2):
        move2 = exchange(5, half, message2, recv2, 8)

    for copy in probe_x:
        copy.wait_recv()
    kind = chip % 16
    own_four = pl.ds(pl.multiple_of(kind * 8, 8), 4)
    pfull[own_four, :] = jnp.concatenate([prow[p * 8 : p * 8 + 1, :] for p in range(PB)], axis=0)

    def along_y(step, rows):
        peer = chip - chip % 4 + lax.rem(chip + step, 4)
        return to_a(6, peer * 2 + core, rows, rows)

    def along_z(step, rows):
        peer = chip - kind + lax.rem(kind + 4 * step, 16)
        return to_a(7, peer * 2 + core, rows, rows)

    for step in range(1, 4):
        along_y(step, pfull.at[own_four]).start()

    for copy in ray_moves:
        copy.wait_recv()

    sums = dot(hit_c[...], rays[...]).astype(BF16).astype(F32)
    for t in range(6):
        for br in range(2):
            for c in range(2):
                at = 2 * t * 16 + br * 8
                first, second = interleave(
                    sums[at : at + 8, c * 128 : (c + 1) * 128],
                    sums[at + 16 : at + 24, c * 128 : (c + 1) * 128],
                )
                spread[pl.ds(t * 64 + 4 * c + br, 8, stride=8), :] = first
                spread[pl.ds(t * 64 + 4 * c + 2 + br, 8, stride=8), :] = second
    table = jnp.concatenate(
        [spread[t * 64 : (t + 1) * 64, :] for t in range(6)], axis=1
    ).astype(BF16)

    probe_y = along_y(1, pfull.at[pl.ds(0, 12)])
    probe_y.wait_recv()
    for step in range(1, 4):
        along_z(step, pfull.at[pl.ds(pl.multiple_of((kind // 4) * 32, 32), 32)]).start()
    for n in range(WCH):
        grad = dot(table, wts_t[:, n * WROWS : (n + 1) * WROWS])
        per = 32 // WCH
        for s in range(per):
            q = n * per + s
            for t in range(4):
                first, second = interleave(
                    grad[t * 16 : t * 16 + 8, s * 128 : (s + 1) * 128],
                    grad[t * 16 + 8 : t * 16 + 16, s * 128 : (s + 1) * 128],
                )
                even = pl.ds(t * 512 + 2 * q, 8, stride=64)
                odd = pl.ds(t * 512 + 2 * q + 1, 8, stride=64)
                onew[even, :] = obj[even, :] - OBJECT_STEP * first
                onew[odd, :] = obj[odd, :] - OBJECT_STEP * second

    move2.wait_recv()
    for half in range(2):
        for c in range(2):
            for z in range(2):
                there = pl.ds(c * 128 + 2 * half + z, 32, stride=4)
                here = recv2[pl.ds(half * 4 + 2 * c + z, 32, stride=SLOT), :]
                wnext[there, :] = base[there, :] + (WAVE_STEP * PENALTY) * here
    probe_z = along_z(1, pfull.at[pl.ds(0, 96)])
    probe_z.wait_recv()
    total = jnp.concatenate([pfull[pl.ds(p, 16, stride=8), :] for p in range(PB)], axis=0)
    scale = PROBE_STEP / (AA * POS * PB)
    pnext[0] = probe[0] - scale * total[:, :64]
    pnext[1] = probe[1] - scale * swap(total)[:, :64]

    xs = gathers + reduces[0] + reduces[1] + probe_x + ray_moves
    for copy in xs + swaps + [move1, move2, probe_y, probe_z]:
        copy.wait_send()


def tail(wnext, pnext, onew, wave_out, probe_out, obj_out, sem):
    pairs = [
        (onew.at[pl.ds(t * 512, 512)], obj_out.at[:, pl.ds(t * 128, 128)]) for t in range(4)
    ] + [(wnext, wave_out), (pnext, probe_out)]
    copies = [pltpu.make_async_copy(src, dst, sem.at[n]) for n, (src, dst) in enumerate(pairs)]
    for copy in copies:
        copy.start()
    for copy in copies:
        copy.wait()


def shards(
    tables,
    wave_field,
    scaled_dual,
    intensity,
    probe_field,
    scan_rows,
    scan_cols,
    sample_mask,
    object_field,
    ray_blocks,
    ray_tables,
    radon_weights,
):
    smem = pl.BlockSpec(memory_space=pltpu.SMEM)
    vmem = pltpu.VMEM
    hbm_spec = pl.BlockSpec(memory_space=pltpu.HBM)
    vmem_spec = pl.BlockSpec(memory_space=pltpu.VMEM)
    kept = pl.pallas_call(
        kernel,
        out_shape=(
            pltpu.VMEM((256, 128), F32),
            pltpu.VMEM((2, 64, 64), F32),
            pltpu.VMEM((2048, 128), F32),
        ),
        in_specs=[smem] * 3 + [hbm_spec] * 9,
        out_specs=[vmem_spec] * 3,
        scratch_shapes=[
            vmem((4096, 768), BF16),
            vmem((768, 4096), BF16),
            vmem((2048, 128), F32),
            vmem((1024, 128), F32),
            vmem((256, 128), F32),
            vmem((POS, 4096), F32),
            vmem((POS * 32, 128), F32),
            vmem((2, 64, 64), F32),
            vmem((640, 256), F32),
            vmem((6, 256, 256), BF16),
            vmem((LIST * NB, AA), jnp.int32),
            vmem((LIST * NB, AA), jnp.int32),
            vmem((LIST, 512), jnp.int32),
            vmem((2048, 128), F32),
            vmem((384, 128), F32),
            vmem((768, 256), BF16),
            vmem((128, 768), BF16),
            vmem((KEYS, 512), BF16),
            vmem((512, 128), F32),
            vmem((512, 128), F32),
            vmem((512, 128), F32),
            vmem((512, 128), F32),
            vmem((2 * POS * 192, 128), F32),
            vmem((PB * SHARE, 128), F32),
            vmem(((PB - 1) * SHARE, 128), F32),
            vmem((256, 128), F32),
            vmem((256, 128), F32),
            vmem((144, 128), F32),
            vmem((144, 128), F32),
            vmem((CHIPS * SLOT, 128), F32),
            vmem((CHIPS * SLOT, 128), F32),
            vmem((256, 128), F32),
            vmem((256, 128), F32),
            vmem((144, 128), F32),
            vmem((144, 128), F32),
            vmem((CHIPS * SLOT, 128), F32),
            vmem((CHIPS * SLOT, 128), F32),
            vmem((512, 256), BF16),
            vmem((384, 128), F32),
            vmem((32, 128), F32),
            vmem((128, 128), F32),
            vmem((64, 128), F32),
            pltpu.SemaphoreType.DMA((14,)),
            pltpu.SemaphoreType.DMA((WCH,)),
            pltpu.SemaphoreType.DMA((15,)),
            pltpu.SemaphoreType.DMA((15,)),
            pltpu.SemaphoreType.DMA((8,)),
            pltpu.SemaphoreType.DMA((8,)),
        ],
        compiler_params=pltpu.CompilerParams(
            collective_id=0, has_side_effects=True, vmem_limit_bytes=60 * 1024 * 1024
        ),
        name="admm",
    )(
        scan_rows,
        scan_cols,
        sample_mask,
        object_field.reshape(512, 512),
        radon_weights,
        wave_field.reshape(256, 512),
        scaled_dual.reshape(256, 128),
        intensity.reshape(POS, 4096),
        probe_field,
        tables,
        ray_blocks.transpose(2, 1, 0).reshape(LIST * NB, AA),
        ray_tables.transpose(2, 1, 0).reshape(LIST * NB, AA),
    )
    wave_next, probe_next, object_next = pl.pallas_call(
        tail,
        out_shape=(
            jax.ShapeDtypeStruct((256, 128), F32),
            jax.ShapeDtypeStruct((2, 64, 64), F32),
            jax.ShapeDtypeStruct((512, 512), F32),
        ),
        in_specs=[vmem_spec] * 3,
        out_specs=[hbm_spec] * 3,
        scratch_shapes=[pltpu.SemaphoreType.DMA((6,))],
        compiler_params=pltpu.CompilerParams(vmem_limit_bytes=16 * 1024 * 1024),
        name="tail",
    )(*kept)
    return (
        wave_next.reshape(1, 2, 128, 128),
        probe_next,
        object_next.reshape(2, 2, 128, 512),
    )


def solution(mesh):
    specs = (
        P("aa", None, None, None),
        P("aa", None, None, "pb"),
        P("aa", "pb", None),
        P(),
        P("aa", "pb"),
        P("aa", "pb"),
        P("aa", "pb"),
        P(None, "aa", "pb", None),
        P(),
        P(),
        P(),
    )
    mapped = jax.shard_map(
        shards,
        mesh=mesh,
        in_specs=(P(),) + specs,
        out_specs=(P("aa", None, None, "pb"), P(), P(None, "aa", "pb", None)),
        check_vma=False,
    )

    def step(*arrays):
        return mapped(jnp.asarray(dft_constants()), *arrays)

    return step
```

```python
import math

import jax
import jax.numpy as jnp
import numpy as np
from jax import lax
from jax.experimental import pallas as pl
from jax.experimental.pallas import tpu as pltpu
from jax.sharding import PartitionSpec as P

BLK = 64
NW = 12
NB = 8
LIST = 12
AA = 64
PB = 4
ZC = 4
POS = 16
PAIRS = 8
OWN = 64 // PB
KEYS = 192
CHIPS = 32
SLOT = 16
SHARE = 272
FIRST = 144
WCH = 8
WROWS = 4096 // WCH
WIDE = 384

WAVE_STEP = 0.05
PENALTY = 1.0
PROBE_STEP = 0.05
OBJECT_STEP = 1.0

F32 = jnp.float32
BF16 = jnp.bfloat16


def dft_constants():
    index = np.arange(BLK)
    phase = (index[:, None] * index[None, :]) % BLK
    angle = phase.astype(np.float64) * (-2.0 * math.pi / BLK)
    f_re, f_im = np.cos(angle) / math.sqrt(BLK), np.sin(angle) / math.sqrt(BLK)
    pair = np.eye(2)

    def right(re, im):
        dre, dim = np.kron(pair, re), np.kron(pair, im)
        return np.block([[dre, dim], [-dim, dre]])

    def left(re, im):
        return np.block([[re, -im], [im, re]])

    order = np.concatenate([np.arange(0, BLK, 2), np.arange(1, BLK, 2)])
    rights = [right(f_re, f_im), right(f_re, -f_im)]
    lefts = np.concatenate(
        [left(f_re[order, :], f_im[order, :]), left(f_re[:, order], -f_im[:, order])], axis=1
    )
    return np.concatenate(rights + [lefts], axis=0).astype(np.float32)


def halves(value):
    high = value.astype(BF16)
    low = (value - high.astype(F32)).astype(BF16)
    return high, low


def dot(lhs, rhs):
    return jnp.dot(lhs, rhs, preferred_element_type=F32)


def right_apply(re, im, g_hi, g_lo):
    high, low = halves(jnp.concatenate([re, im], axis=1))
    out = dot(high, g_hi) + dot(low, g_hi) + dot(high, g_lo)
    return out[:, :128], out[:, 128:]


def left_apply(re, im, table):
    high, low = halves(jnp.concatenate([re, im], axis=0))
    out = dot(table, jnp.concatenate([high, low], axis=0))
    out = out[:128] + out[128:]
    return out[:64], out[64:]


def rows_to_lanes(value):
    return jnp.concatenate([value[q * 64 : (q + 1) * 64] for q in range(PAIRS)], axis=1)


def lanes_to_rows(value):
    return jnp.concatenate([value[:, q * 128 : (q + 1) * 128] for q in range(PAIRS)], axis=0)


def swap(value):
    return pltpu.roll(value, 64, 1)


def interleave(first, second):
    low = lax.broadcasted_iota(jnp.int32, first.shape, 1) < 64
    return jnp.where(low, first, swap(second)), jnp.where(low, swap(first), second)


def kernel(
    rows_ref,
    cols_ref,
    mask_ref,
    obj_hbm,
    wts_hbm,
    wave_hbm,
    dual_hbm,
    int_hbm,
    probe_hbm,
    tab_hbm,
    blocks_hbm,
    tables_hbm,
    wnext,
    pnext,
    onew,
    wts,
    wts_t,
    obj,
    wave,
    dual,
    int_raw,
    inten,
    probe,
    tab_raw,
    tab,
    blocks,
    tables,
    colkey,
    lhs,
    ptile,
    stk,
    hit_r,
    hit_c,
    win_r,
    win_i,
    gra_r,
    gra_i,
    pad,
    acc,
    share,
    base,
    loose1,
    across1,
    arrived1,
    message1,
    recv1,
    loose2,
    misfit,
    across2,
    arrived2,
    message2,
    recv2,
    rays,
    spread,
    prow,
    pfull,
    probe_part,
    in_sem,
    w_sem,
    x_send,
    x_recv,
    a_send,
    a_recv,
):
    me_a = lax.axis_index("aa")
    me_p = lax.axis_index("pb")
    core = me_a % 2
    chip = me_a // 2
    sibling = me_a + 1 - 2 * core

    def lanes(shape):
        return lax.broadcasted_iota(jnp.int32, shape, 1)

    obj_in = [
        pltpu.make_async_copy(
            obj_hbm.at[:, pl.ds(t * 128, 128)], obj.at[pl.ds(t * 512, 512)], in_sem.at[t]
        )
        for t in range(4)
    ]
    wts_in = [
        pltpu.make_async_copy(
            wts_hbm.at[pl.ds(c * 1024, 1024), pl.ds(h * WIDE, WIDE)],
            wts.at[pl.ds(c * 1024, 1024), pl.ds(h * WIDE, WIDE)],
            w_sem.at[h * 4 + c],
        )
        for h in range(2)
        for c in range(4)
    ]
    wave_in = [
        pltpu.make_async_copy(
            wave_hbm.at[:, pl.ds(t * 128, 128)], wave.at[pl.ds(t * 256, 256)], in_sem.at[4 + t]
        )
        for t in range(4)
    ]
    others = {
        name: pltpu.make_async_copy(src, dst, in_sem.at[8 + n])
        for n, (name, src, dst) in enumerate(
            [
                ("blocks", blocks_hbm, blocks),
                ("tables", tables_hbm, tables),
                ("probe", probe_hbm, probe),
                ("tab", tab_hbm, tab_raw),
                ("inten", int_hbm, int_raw),
                ("dual", dual_hbm, dual),
            ]
        )
    }
    for copy in wave_in:
        copy.start()
    for name in ("probe", "tab", "inten"):
        others[name].start()
    barrier = pltpu.get_barrier_semaphore()

    for step in range(1, PB):
        pl.semaphore_signal(
            barrier,
            inc=1,
            device_id={"pb": lax.rem(me_p + step, PB)},
            device_id_type=pl.DeviceIdType.MESH,
        )
    for peer in [lax.rem(chip + step, CHIPS) * 2 + core for step in range(1, CHIPS)] + [sibling]:
        pl.semaphore_signal(
            barrier, inc=1, device_id={"aa": peer}, device_id_type=pl.DeviceIdType.MESH
        )
    for copy in obj_in + wts_in:
        copy.start()
    for name in ("dual", "blocks", "tables"):
        others[name].start()

    def clear(n, carry):
        for at in (0, 128):
            pad[pl.ds(pl.multiple_of(n * 192 + at, 64), 64), :] = jnp.zeros((64, 128), F32)
        return carry

    lax.fori_loop(0, 2 * POS, clear, 0)

    for copy in wave_in:
        copy.wait()

    def windows(q, carry):
        at = pl.multiple_of(q * 64, 64)
        for c, ref in ((0, win_r), (1, win_i)):
            found = []
            for h in range(2):
                row = rows_ref[0, 2 * q + h]
                col = cols_ref[0, 2 * q + h]
                tile = col // 128
                off = col % 128
                near = wave[pl.ds(tile * 256 + c * 128 + row, 64), :]
                far = wave[pl.ds(jnp.minimum(tile + 1, 3) * 256 + c * 128 + row, 64), :]
                both = jnp.where(lanes((64, 128)) >= off, near, far)
                found.append(pltpu.roll(both, (128 + 64 * h - off) % 128, 1))
            ref[pl.ds(at, 64), :] = jnp.where(lanes((64, 128)) < 64, found[0], found[1])
        return carry

    lax.fori_loop(0, PAIRS, windows, 0)
    others["probe"].wait()
    others["tab"].wait()
    others["inten"].wait()
    for octet in range(2):
        for t in range(32):
            inten[pl.ds(octet * 256 + t, 8, stride=32), :] = int_raw[
                octet * 8 : octet * 8 + 8, t * 128 : (t + 1) * 128
            ]
    for n in range(2):
        tab[2 * n], tab[2 * n + 1] = halves(tab_raw[n * 256 : (n + 1) * 256, :])
        high, low = halves(tab_raw[512:640, n * 128 : (n + 1) * 128])
        tab[4 + n] = jnp.concatenate(
            [jnp.concatenate([high] * 2, axis=1), jnp.concatenate([low] * 2, axis=1)], axis=0
        )
    one_re = jnp.concatenate([probe[0]] * 2, axis=1)
    one_im = jnp.concatenate([probe[1]] * 2, axis=1)
    p_re = jnp.concatenate([one_re] * PAIRS, axis=0)
    p_im = jnp.concatenate([one_im] * PAIRS, axis=0)
    w_re, w_im = win_r[...], win_i[...]
    half_re, half_im = right_apply(
        p_re * w_re - p_im * w_im, p_re * w_im + p_im * w_re, tab[0], tab[1]
    )
    far_re, far_im = left_apply(rows_to_lanes(half_re), rows_to_lanes(half_im), tab[4])
    measured, live = [], []
    for q in range(PAIRS):
        even, odd = interleave(
            inten[2 * q * 32 : 2 * q * 32 + 32, :], inten[2 * q * 32 + 32 : 2 * q * 32 + 64, :]
        )
        measured.append(jnp.concatenate([even, odd], axis=0))
        live.append(
            jnp.where(
                lanes((1, 128)) < 64, mask_ref[0, 2 * q].astype(F32), mask_ref[0, 2 * q + 1].astype(F32)
            )
        )
    measured = jnp.concatenate(measured, axis=1)
    live = jnp.concatenate(live, axis=1)
    factor = live * (far_re * far_re + far_im * far_im - measured)
    half_re, half_im = left_apply(factor * far_re, factor * far_im, tab[5])
    back_re, back_im = right_apply(lanes_to_rows(half_re), lanes_to_rows(half_im), tab[2], tab[3])
    gra_r[...] = p_re * back_re + p_im * back_im
    gra_i[...] = p_re * back_im - p_im * back_re
    grad_re = jnp.sum((w_re * back_re + w_im * back_im).reshape(PAIRS, 64, 128), axis=0)
    grad_im = jnp.sum((w_re * back_im - w_im * back_re).reshape(PAIRS, 64, 128), axis=0)
    grad_re = grad_re + swap(grad_re)
    grad_im = grad_im + swap(grad_im)
    probe_part[...] = jnp.where(lanes((64, 128)) < 64, grad_re, grad_im)

    def place(q, carry):
        at = pl.multiple_of(q * 64, 64)
        for h in range(2):
            turn = (cols_ref[0, 2 * q + h] + 128 - 64 * h) % 128
            for c, ref in ((0, gra_r), (1, gra_i)):
                slot = pl.multiple_of((4 * q + 2 * h + c) * 192 + 64, 64)
                pad[pl.ds(slot, 64), :] = pltpu.roll(ref[pl.ds(at, 64), :], turn, 1)
        return carry

    lax.fori_loop(0, PAIRS, place, 0)

    def to_x(stage, step, src, dst):
        peer = lax.rem(me_p + step, PB)
        return pltpu.make_async_remote_copy(
            src_ref=src,
            dst_ref=dst,
            send_sem=x_send.at[stage * 3 + step - 1],
            recv_sem=x_recv.at[stage * 3 + step - 1],
            device_id={"pb": peer},
            device_id_type=pl.DeviceIdType.MESH,
        )

    early = chip // 4 == 0
    late = chip // 16 == 1

    @pl.when(early)
    def _():
        for copy in wts_in:
            copy.wait()
        for n in range(WCH):
            part = slice(n * WROWS, (n + 1) * WROWS)
            wts_t[:, part] = jnp.transpose(wts[part, :])

    pfull[...] = jnp.zeros_like(pfull)
    pl.semaphore_wait(barrier, CHIPS + PB - 1)
    reduces = [[], []]
    for half in range(2):
        for step in (2, 1, 3, 0):
            tile = lax.rem(me_p + step, PB)
            at = step * SHARE + half * FIRST
            for c in range(2):

                def add(n, total, c=c, tile=tile, half=half):
                    top = (2 * n + c) * 192 + 64 + half * 64 - rows_ref[0, n]
                    column = lanes((64, 128)) + (tile * 128 - cols_ref[0, n])
                    inside = (column >= 0) & (column < 64)
                    return total + jnp.where(inside, pad[pl.ds(top, 64), :], 0.0)

                acc[at + c * 64 : at + c * 64 + 64, :] = lax.fori_loop(
                    0, POS, add, jnp.zeros((64, 128), F32), unroll=8
                )
            if half == 0:
                acc[at + 128 : at + FIRST, :] = probe_part[
                    pl.ds(pl.multiple_of(tile * 16, 16), 16), :
                ]
            if step > 0:
                rows = FIRST if half == 0 else SHARE - FIRST
                copy = to_x(
                    half,
                    step,
                    acc.at[pl.ds(at, rows)],
                    share.at[pl.ds((step - 1) * SHARE + half * FIRST, rows)],
                )
                copy.start()
                reduces[half].append(copy)

    for copy in obj_in:
        copy.wait()

    def fold(q, carry):
        for t in range(4):
            even = obj[pl.ds(t * 512 + 2 * q, 8, stride=64), :]
            odd = obj[pl.ds(t * 512 + 2 * q + 1, 8, stride=64), :]
            first, second = interleave(even, odd)
            at = pl.multiple_of(q * 64 + t * 16, 16)
            lhs[pl.ds(at, 16), :] = jnp.concatenate([first, second], axis=0)
        return carry

    lax.fori_loop(0, 32, fold, 0, unroll=4)
    own_stk = pl.multiple_of(me_p * KEYS, KEYS)
    for half in range(2):
        products = jnp.zeros((64, WIDE), F32)
        for c in range(4):
            pl.when(jnp.logical_not(early))(wts_in[half * 4 + c].wait)
            part = jnp.concatenate(
                [lhs[(c * 8 + n) * 64 : (c * 8 + n + 1) * 64, :] for n in range(8)], axis=1
            ).astype(BF16)
            products = products + dot(
                part, wts[c * 1024 : (c + 1) * 1024, half * WIDE : (half + 1) * WIDE]
            )
        for i in range(3):
            t = half * 3 + i
            ptile[t * 64 : (t + 1) * 64, :] = products[:, i * 128 : (i + 1) * 128]
            lists = [[], []], [[], []]
            for br in range(2):
                part = [ptile[pl.ds(t * 64 + cz * 2 + br, 8, stride=8), :] for cz in range(ZC)]
                for c in range(2):
                    even, odd = interleave(part[2 * c], part[2 * c + 1])
                    lists[0][c].append(even)
                    lists[1][c].append(odd)
            for h in range(2):
                for c in range(2):
                    stk[
                        pl.ds(pl.multiple_of(own_stk + (2 * t + h) * 16, 16), 16),
                        c * 128 : (c + 1) * 128,
                    ] = jnp.concatenate(lists[h][c], axis=0).astype(BF16)

    own_block = stk.at[pl.ds(own_stk, KEYS)]
    gathers = [to_x(2, step, own_block, own_block) for step in (2, 1, 3)]
    for copy in gathers:
        copy.start()

    others["blocks"].wait()
    others["tables"].wait()
    keys = []
    for jj in range(2):
        there = pl.ds(me_p * 2 + jj, LIST, stride=NB)
        block = blocks[there, :]
        keys.append((block // OWN) * KEYS + tables[there, :] * OWN + block % OWN)
    keys = jnp.concatenate(
        [jnp.concatenate(keys, axis=1), jnp.zeros((128 - LIST, 128), jnp.int32)], axis=0
    )
    keys = jnp.transpose(keys.astype(F32)).astype(jnp.int32)
    for t in range(6):
        column = lanes((128, 128)) + t * 128
        total = jnp.zeros((128, 128), F32)
        for e in range(LIST):
            total = total + jnp.where(keys[:, e : e + 1] == column, 1.0, 0.0)
        hit_r[:, t * 128 : (t + 1) * 128] = total.astype(BF16)

    for p in range(PB):
        parts = []
        for jj in range(2):
            there = pl.ds(p * 2 + jj, LIST, stride=NB)
            block = blocks[there, :]
            place = tables[there, :] * OWN + block % OWN
            parts.append(jnp.where(block // OWN == me_p, place, -1))
        colkey[:, p * 128 : (p + 1) * 128] = jnp.concatenate(parts, axis=1)
    for r in range(3):
        mine = lax.broadcasted_iota(jnp.int32, (64, 512), 0) + r * 64
        total = jnp.zeros((64, 512), F32)
        for e in range(LIST):
            total = total + jnp.where(colkey[e : e + 1, :] == mine, 1.0, 0.0)
        hit_c[r * 64 : (r + 1) * 64, :] = total.astype(BF16)

    def to_a(stage, peer, src, dst):
        return pltpu.make_async_remote_copy(
            src_ref=src,
            dst_ref=dst,
            send_sem=a_send.at[stage],
            recv_sem=a_recv.at[stage],
            device_id={"aa": peer},
            device_id_type=pl.DeviceIdType.MESH,
        )

    def swap_cores(stage, half, loose, extra, across, arrived):
        at = half * 80
        for k in range(4):
            across[at + k * 16 : at + k * 16 + 16, :] = loose[
                pl.ds(k * 64 + half * 32 + 1 - core, 16, stride=2), :
            ]
        rows = 64
        if extra is not None:
            across[64:80, :] = extra
            rows = 80
        copy = to_a(stage, sibling, across.at[pl.ds(at, rows)], arrived.at[pl.ds(at, rows)])
        copy.start()
        return copy

    def fill(half, loose, arrived, message):
        for k in range(4):
            message[pl.ds(half * 256 + core * 4 + k, 16, stride=SLOT), :] = loose[
                pl.ds(k * 64 + half * 32 + core, 16, stride=2), :
            ]
            message[pl.ds(half * 256 + (1 - core) * 4 + k, 16, stride=SLOT), :] = arrived[
                half * 80 + k * 16 : half * 80 + k * 16 + 16, :
            ]

    def exchange(stage, half, message, target, count):
        here = pl.ds(pl.multiple_of(chip * SLOT, SLOT), count)

        def send(step):
            there = half * 16 + lax.rem(chip + step, 16)
            to_a(
                stage,
                there * 2 + core,
                message.at[pl.ds(pl.multiple_of(there * SLOT, SLOT), count)],
                target.at[here],
            ).start()

        for step in range(1, 16):
            send(step)
        pl.when(chip // 16 != half)(lambda: send(0))

        @pl.when(chip // 16 == half)
        def _():
            target[here, :] = message[here, :]

        rows = (CHIPS - 1) * count
        return to_a(
            stage,
            lax.rem(chip + 1, CHIPS) * 2 + core,
            message.at[pl.ds(0, rows)],
            target.at[pl.ds(0, rows)],
        )

    others["dual"].wait()
    swaps = []
    for half in range(2):
        for copy in reduces[half]:
            copy.wait_recv()
        for c in range(2):
            at = half * FIRST + c * 64
            gradient = acc[at : at + 64, :]
            for n in range(PB - 1):
                gradient = gradient + share[n * SHARE + at : n * SHARE + at + 64, :]
            top = c * 128 + half * 64
            mine = wave[pl.ds(pl.multiple_of(me_p * 256 + top, 64), 64), :]
            base[top : top + 64, :] = mine - WAVE_STEP * (
                gradient + PENALTY * (mine + dual[top : top + 64, :])
            )
            for z in range(2):
                there = pl.ds(top + z, 32, stride=2)
                k = 2 * c + z
                loose1[k * 64 + half * 32 : k * 64 + half * 32 + 32, :] = (
                    base[there, :] + dual[there, :]
                )
        probe_share = None
        if half == 0:
            probe_share = acc[128:FIRST, :]
            for n in range(PB - 1):
                probe_share = probe_share + share[n * SHARE + 128 : n * SHARE + FIRST, :]
        swaps.append(swap_cores(half, half, loose1, probe_share, across1, arrived1))
        swaps[-1].wait_recv()
        fill(half, loose1, arrived1, message1)
        if half == 0:
            probe_chip = probe_share + arrived1[64:80, :]
            message1[pl.ds(8, 32, stride=SLOT), :] = jnp.concatenate([probe_chip] * 2, axis=0)
        move1 = exchange(2, half, message1, recv1, 9)

    for copy in gathers:
        copy.wait_recv()
    projection = dot(hit_r[...], stk[...])
    for c in range(2):
        first, second = interleave(
            projection[:64, c * 128 : (c + 1) * 128], projection[64:, c * 128 : (c + 1) * 128]
        )
        loose2[2 * c * 64 : 2 * c * 64 + 64, :] = first
        loose2[2 * c * 64 + 64 : 2 * c * 64 + 128, :] = second

    later = [swap_cores(3 + half, half, loose2, None, across2, arrived2) for half in range(2)]
    for half in range(2):
        later[half].wait_recv()
        fill(half, loose2, arrived2, message2)
    swaps += later

    @pl.when(late)
    def _():
        exchange(5, 0, message2, recv2, 8)

    move1.wait_recv()
    for half in range(2):
        for k in range(4):
            there = pl.ds(k * 64 + half, 32, stride=2)
            own = loose2[there, :]
            rest = recv1[pl.ds(half * 4 + k, 32, stride=SLOT), :]
            misfit[there, :] = own - (rest + (WAVE_STEP * PENALTY) * own)
    own_rays = pl.multiple_of(me_p * 128, 128)
    for c in range(2):
        first, second = interleave(
            misfit[2 * c * 64 : 2 * c * 64 + 64, :], misfit[2 * c * 64 + 64 : 2 * c * 64 + 128, :]
        )
        rays[pl.ds(own_rays, 128), c * 128 : (c + 1) * 128] = jnp.concatenate(
            [first, second], axis=0
        ).astype(BF16)
    own_rows = rays.at[pl.ds(own_rays, 128)]
    ray_moves = [to_x(3, step, own_rows, own_rows) for step in (2, 1, 3)]
    for copy in ray_moves:
        copy.start()

    own_row = pl.ds(pl.multiple_of(me_p * 8, 8), 1)
    prow[own_row, :] = jnp.sum(recv1[pl.ds(8, 32, stride=SLOT), :], axis=0, keepdims=True)
    probe_x = [to_x(4, step, prow.at[own_row], prow.at[own_row]) for step in (2, 1, 3)]
    for copy in probe_x:
        copy.start()

    @pl.when(jnp.logical_not(late))
    def _():
        exchange(5, 0, message2, recv2, 8)

    move2 = exchange(5, 1, message2, recv2, 8)

    for copy in probe_x:
        copy.wait_recv()
    kind = chip % 16
    own_four = pl.ds(pl.multiple_of(kind * 8, 8), 4)
    pfull[own_four, :] = jnp.concatenate([prow[p * 8 : p * 8 + 1, :] for p in range(PB)], axis=0)

    def along_y(step, rows):
        peer = chip - chip % 4 + lax.rem(chip + step, 4)
        return to_a(6, peer * 2 + core, rows, rows)

    def along_z(step, rows):
        peer = chip - kind + lax.rem(kind + 4 * step, 16)
        return to_a(7, peer * 2 + core, rows, rows)

    for step in range(1, 4):
        along_y(step, pfull.at[own_four]).start()

    for copy in ray_moves:
        copy.wait_recv()

    sums = dot(hit_c[...], rays[...]).astype(BF16).astype(F32)
    for t in range(6):
        for br in range(2):
            for c in range(2):
                at = 2 * t * 16 + br * 8
                first, second = interleave(
                    sums[at : at + 8, c * 128 : (c + 1) * 128],
                    sums[at + 16 : at + 24, c * 128 : (c + 1) * 128],
                )
                spread[pl.ds(t * 64 + 4 * c + br, 8, stride=8), :] = first
                spread[pl.ds(t * 64 + 4 * c + 2 + br, 8, stride=8), :] = second
    table = jnp.concatenate(
        [spread[t * 64 : (t + 1) * 64, :] for t in range(6)], axis=1
    ).astype(BF16)

    probe_y = along_y(1, pfull.at[pl.ds(0, 12)])
    probe_y.wait_recv()
    for step in range(1, 4):
        along_z(step, pfull.at[pl.ds(pl.multiple_of((kind // 4) * 32, 32), 32)]).start()
    def object_step(product):
        per = 32 // WCH
        for n in range(WCH):
            grad = product(slice(n * WROWS, (n + 1) * WROWS))
            for s in range(per):
                q = n * per + s
                for t in range(4):
                    first, second = interleave(
                        grad[t * 16 : t * 16 + 8, s * 128 : (s + 1) * 128],
                        grad[t * 16 + 8 : t * 16 + 16, s * 128 : (s + 1) * 128],
                    )
                    even = pl.ds(t * 512 + 2 * q, 8, stride=64)
                    odd = pl.ds(t * 512 + 2 * q + 1, 8, stride=64)
                    onew[even, :] = obj[even, :] - OBJECT_STEP * first
                    onew[odd, :] = obj[odd, :] - OBJECT_STEP * second

    @pl.when(early)
    def _():
        object_step(lambda part: dot(table, wts_t[:, part]))

    @pl.when(jnp.logical_not(early))
    def _():
        object_step(
            lambda part: lax.dot_general(
                table, wts[part, :], (((1,), (1,)), ((), ())), preferred_element_type=F32
            )
        )

    move2.wait_recv()
    for half in range(2):
        for c in range(2):
            for z in range(2):
                there = pl.ds(c * 128 + 2 * half + z, 32, stride=4)
                here = recv2[pl.ds(half * 4 + 2 * c + z, 32, stride=SLOT), :]
                wnext[there, :] = base[there, :] + (WAVE_STEP * PENALTY) * here
    probe_z = along_z(1, pfull.at[pl.ds(0, 96)])
    probe_z.wait_recv()
    total = jnp.concatenate([pfull[pl.ds(p, 16, stride=8), :] for p in range(PB)], axis=0)
    scale = PROBE_STEP / (AA * POS * PB)
    pnext[0] = probe[0] - scale * total[:, :64]
    pnext[1] = probe[1] - scale * swap(total)[:, :64]

    xs = gathers + reduces[0] + reduces[1] + probe_x + ray_moves
    for copy in xs + swaps + [move1, move2, probe_y, probe_z]:
        copy.wait_send()


def tail(wnext, pnext, onew, wave_out, probe_out, obj_out, sem):
    pairs = [
        (onew.at[pl.ds(t * 512, 512)], obj_out.at[:, pl.ds(t * 128, 128)]) for t in range(4)
    ] + [(wnext, wave_out), (pnext, probe_out)]
    copies = [pltpu.make_async_copy(src, dst, sem.at[n]) for n, (src, dst) in enumerate(pairs)]
    for copy in copies:
        copy.start()
    for copy in copies:
        copy.wait()


def shards(
    tables,
    wave_field,
    scaled_dual,
    intensity,
    probe_field,
    scan_rows,
    scan_cols,
    sample_mask,
    object_field,
    ray_blocks,
    ray_tables,
    radon_weights,
):
    smem = pl.BlockSpec(memory_space=pltpu.SMEM)
    vmem = pltpu.VMEM
    hbm_spec = pl.BlockSpec(memory_space=pltpu.HBM)
    vmem_spec = pl.BlockSpec(memory_space=pltpu.VMEM)
    kept = pl.pallas_call(
        kernel,
        out_shape=(
            pltpu.VMEM((256, 128), F32),
            pltpu.VMEM((2, 64, 64), F32),
            pltpu.VMEM((2048, 128), F32),
        ),
        in_specs=[smem] * 3 + [hbm_spec] * 9,
        out_specs=[vmem_spec] * 3,
        scratch_shapes=[
            vmem((4096, 768), BF16),
            vmem((768, 4096), BF16),
            vmem((2048, 128), F32),
            vmem((1024, 128), F32),
            vmem((256, 128), F32),
            vmem((POS, 4096), F32),
            vmem((POS * 32, 128), F32),
            vmem((2, 64, 64), F32),
            vmem((640, 256), F32),
            vmem((6, 256, 256), BF16),
            vmem((LIST * NB, AA), jnp.int32),
            vmem((LIST * NB, AA), jnp.int32),
            vmem((LIST, 512), jnp.int32),
            vmem((2048, 128), F32),
            vmem((384, 128), F32),
            vmem((768, 256), BF16),
            vmem((128, 768), BF16),
            vmem((KEYS, 512), BF16),
            vmem((512, 128), F32),
            vmem((512, 128), F32),
            vmem((512, 128), F32),
            vmem((512, 128), F32),
            vmem((2 * POS * 192, 128), F32),
            vmem((PB * SHARE, 128), F32),
            vmem(((PB - 1) * SHARE, 128), F32),
            vmem((256, 128), F32),
            vmem((256, 128), F32),
            vmem((144, 128), F32),
            vmem((144, 128), F32),
            vmem((CHIPS * SLOT, 128), F32),
            vmem((CHIPS * SLOT, 128), F32),
            vmem((256, 128), F32),
            vmem((256, 128), F32),
            vmem((144, 128), F32),
            vmem((144, 128), F32),
            vmem((CHIPS * SLOT, 128), F32),
            vmem((CHIPS * SLOT, 128), F32),
            vmem((512, 256), BF16),
            vmem((384, 128), F32),
            vmem((32, 128), F32),
            vmem((128, 128), F32),
            vmem((64, 128), F32),
            pltpu.SemaphoreType.DMA((14,)),
            pltpu.SemaphoreType.DMA((WCH,)),
            pltpu.SemaphoreType.DMA((15,)),
            pltpu.SemaphoreType.DMA((15,)),
            pltpu.SemaphoreType.DMA((8,)),
            pltpu.SemaphoreType.DMA((8,)),
        ],
        compiler_params=pltpu.CompilerParams(
            collective_id=0, has_side_effects=True, vmem_limit_bytes=60 * 1024 * 1024
        ),
        name="admm",
    )(
        scan_rows,
        scan_cols,
        sample_mask,
        object_field.reshape(512, 512),
        radon_weights,
        wave_field.reshape(256, 512),
        scaled_dual.reshape(256, 128),
        intensity.reshape(POS, 4096),
        probe_field,
        tables,
        ray_blocks.transpose(2, 1, 0).reshape(LIST * NB, AA),
        ray_tables.transpose(2, 1, 0).reshape(LIST * NB, AA),
    )
    wave_next, probe_next, object_next = pl.pallas_call(
        tail,
        out_shape=(
            jax.ShapeDtypeStruct((256, 128), F32),
            jax.ShapeDtypeStruct((2, 64, 64), F32),
            jax.ShapeDtypeStruct((512, 512), F32),
        ),
        in_specs=[vmem_spec] * 3,
        out_specs=[hbm_spec] * 3,
        scratch_shapes=[pltpu.SemaphoreType.DMA((6,))],
        compiler_params=pltpu.CompilerParams(vmem_limit_bytes=16 * 1024 * 1024),
        name="tail",
    )(*kept)
    return (
        wave_next.reshape(1, 2, 128, 128),
        probe_next,
        object_next.reshape(2, 2, 128, 512),
    )


def solution(mesh):
    specs = (
        P("aa", None, None, None),
        P("aa", None, None, "pb"),
        P("aa", "pb", None),
        P(),
        P("aa", "pb"),
        P("aa", "pb"),
        P("aa", "pb"),
        P(None, "aa", "pb", None),
        P(),
        P(),
        P(),
    )
    mapped = jax.shard_map(
        shards,
        mesh=mesh,
        in_specs=(P(),) + specs,
        out_specs=(P("aa", None, None, "pb"), P(), P(None, "aa", "pb", None)),
        check_vma=False,
    )

    def step(*arrays):
        return mapped(jnp.asarray(dft_constants()), *arrays)

    return step
```

```python
import math

import jax
import jax.numpy as jnp
import numpy as np
from jax import lax
from jax.experimental import pallas as pl
from jax.experimental.pallas import tpu as pltpu
from jax.sharding import PartitionSpec as P

BLK = 64
NW = 12
NB = 8
LIST = 12
AA = 64
PB = 4
ZC = 4
POS = 16
PAIRS = 8
OWN = 64 // PB
KEYS = 192
CHIPS = 32
SLOT = 16
SHARE = 272
FIRST = 144
WCH = 8
WROWS = 4096 // WCH
WIDE = 384

WAVE_STEP = 0.05
PENALTY = 1.0
PROBE_STEP = 0.05
OBJECT_STEP = 1.0

F32 = jnp.float32
BF16 = jnp.bfloat16


def dft_constants():
    index = np.arange(BLK)
    phase = (index[:, None] * index[None, :]) % BLK
    angle = phase.astype(np.float64) * (-2.0 * math.pi / BLK)
    f_re, f_im = np.cos(angle) / math.sqrt(BLK), np.sin(angle) / math.sqrt(BLK)
    pair = np.eye(2)

    def right(re, im):
        dre, dim = np.kron(pair, re), np.kron(pair, im)
        return np.block([[dre, dim], [-dim, dre]])

    def left(re, im):
        return np.block([[re, -im], [im, re]])

    order = np.concatenate([np.arange(0, BLK, 2), np.arange(1, BLK, 2)])
    rights = [right(f_re, f_im), right(f_re, -f_im)]
    lefts = np.concatenate(
        [left(f_re[order, :], f_im[order, :]), left(f_re[:, order], -f_im[:, order])], axis=1
    )
    return np.concatenate(rights + [lefts], axis=0).astype(np.float32)


def halves(value):
    high = value.astype(BF16)
    low = (value - high.astype(F32)).astype(BF16)
    return high, low


def dot(lhs, rhs):
    return jnp.dot(lhs, rhs, preferred_element_type=F32)


def right_apply(re, im, g_hi, g_lo):
    high, low = halves(jnp.concatenate([re, im], axis=1))
    out = dot(high, g_hi) + dot(low, g_hi) + dot(high, g_lo)
    return out[:, :128], out[:, 128:]


def left_apply(re, im, table):
    high, low = halves(jnp.concatenate([re, im], axis=0))
    out = dot(table, jnp.concatenate([high, low], axis=0))
    out = out[:128] + out[128:]
    return out[:64], out[64:]


def rows_to_lanes(value):
    return jnp.concatenate([value[q * 64 : (q + 1) * 64] for q in range(PAIRS)], axis=1)


def lanes_to_rows(value):
    return jnp.concatenate([value[:, q * 128 : (q + 1) * 128] for q in range(PAIRS)], axis=0)


def swap(value):
    return pltpu.roll(value, 64, 1)


def interleave(first, second):
    low = lax.broadcasted_iota(jnp.int32, first.shape, 1) < 64
    return jnp.where(low, first, swap(second)), jnp.where(low, swap(first), second)


def kernel(
    rows_ref,
    cols_ref,
    mask_ref,
    obj_hbm,
    wts_hbm,
    wave_hbm,
    dual_hbm,
    int_hbm,
    probe_hbm,
    tab_hbm,
    blocks_hbm,
    tables_hbm,
    wnext,
    pnext,
    onew,
    wts,
    wts_t,
    obj,
    wave,
    dual,
    int_raw,
    inten,
    probe,
    tab_raw,
    tab,
    blocks,
    tables,
    colkey,
    lhs,
    ptile,
    stk,
    hit_r,
    hit_c,
    win_r,
    win_i,
    gra_r,
    gra_i,
    pad,
    acc,
    share,
    base,
    loose1,
    across1,
    arrived1,
    message1,
    recv1,
    loose2,
    misfit,
    across2,
    arrived2,
    message2,
    recv2,
    rays,
    spread,
    prow,
    pfull,
    probe_part,
    in_sem,
    w_sem,
    x_send,
    x_recv,
    a_send,
    a_recv,
):
    me_a = lax.axis_index("aa")
    me_p = lax.axis_index("pb")
    core = me_a % 2
    chip = me_a // 2
    sibling = me_a + 1 - 2 * core

    def lanes(shape):
        return lax.broadcasted_iota(jnp.int32, shape, 1)

    obj_in = [
        pltpu.make_async_copy(
            obj_hbm.at[:, pl.ds(t * 128, 128)], obj.at[pl.ds(t * 512, 512)], in_sem.at[t]
        )
        for t in range(4)
    ]
    wts_in = [
        pltpu.make_async_copy(
            wts_hbm.at[pl.ds(c * 1024, 1024), pl.ds(h * WIDE, WIDE)],
            wts.at[pl.ds(c * 1024, 1024), pl.ds(h * WIDE, WIDE)],
            w_sem.at[h * 4 + c],
        )
        for h in range(2)
        for c in range(4)
    ]
    wave_in = [
        pltpu.make_async_copy(
            wave_hbm.at[:, pl.ds(t * 128, 128)], wave.at[pl.ds(t * 256, 256)], in_sem.at[4 + t]
        )
        for t in range(4)
    ]
    others = {
        name: pltpu.make_async_copy(src, dst, in_sem.at[8 + n])
        for n, (name, src, dst) in enumerate(
            [
                ("blocks", blocks_hbm, blocks),
                ("tables", tables_hbm, tables),
                ("probe", probe_hbm, probe),
                ("tab", tab_hbm, tab_raw),
                ("inten", int_hbm, int_raw),
                ("dual", dual_hbm, dual),
            ]
        )
    }
    for copy in wave_in:
        copy.start()
    for name in ("probe", "tab", "inten"):
        others[name].start()
    barrier = pltpu.get_barrier_semaphore()

    for step in range(1, PB):
        pl.semaphore_signal(
            barrier,
            inc=1,
            device_id={"pb": lax.rem(me_p + step, PB)},
            device_id_type=pl.DeviceIdType.MESH,
        )
    for peer in [lax.rem(chip + step, CHIPS) * 2 + core for step in range(1, CHIPS)] + [sibling]:
        pl.semaphore_signal(
            barrier, inc=1, device_id={"aa": peer}, device_id_type=pl.DeviceIdType.MESH
        )
    for copy in obj_in + wts_in:
        copy.start()
    for name in ("dual", "blocks", "tables"):
        others[name].start()

    def clear(n, carry):
        for at in (0, 128):
            pad[pl.ds(pl.multiple_of(n * 192 + at, 64), 64), :] = jnp.zeros((64, 128), F32)
        return carry

    lax.fori_loop(0, 2 * POS, clear, 0)

    for copy in wave_in:
        copy.wait()

    def windows(q, carry):
        at = pl.multiple_of(q * 64, 64)
        for c, ref in ((0, win_r), (1, win_i)):
            found = []
            for h in range(2):
                row = rows_ref[0, 2 * q + h]
                col = cols_ref[0, 2 * q + h]
                tile = col // 128
                off = col % 128
                near = wave[pl.ds(tile * 256 + c * 128 + row, 64), :]
                far = wave[pl.ds(jnp.minimum(tile + 1, 3) * 256 + c * 128 + row, 64), :]
                both = jnp.where(lanes((64, 128)) >= off, near, far)
                found.append(pltpu.roll(both, (128 + 64 * h - off) % 128, 1))
            ref[pl.ds(at, 64), :] = jnp.where(lanes((64, 128)) < 64, found[0], found[1])
        return carry

    lax.fori_loop(0, PAIRS, windows, 0)
    others["probe"].wait()
    others["tab"].wait()
    others["inten"].wait()
    for octet in range(2):
        for t in range(32):
            inten[pl.ds(octet * 256 + t, 8, stride=32), :] = int_raw[
                octet * 8 : octet * 8 + 8, t * 128 : (t + 1) * 128
            ]
    for n in range(2):
        tab[2 * n], tab[2 * n + 1] = halves(tab_raw[n * 256 : (n + 1) * 256, :])
        high, low = halves(tab_raw[512:640, n * 128 : (n + 1) * 128])
        tab[4 + n] = jnp.concatenate(
            [jnp.concatenate([high] * 2, axis=1), jnp.concatenate([low] * 2, axis=1)], axis=0
        )
    one_re = jnp.concatenate([probe[0]] * 2, axis=1)
    one_im = jnp.concatenate([probe[1]] * 2, axis=1)
    p_re = jnp.concatenate([one_re] * PAIRS, axis=0)
    p_im = jnp.concatenate([one_im] * PAIRS, axis=0)
    w_re, w_im = win_r[...], win_i[...]
    half_re, half_im = right_apply(
        p_re * w_re - p_im * w_im, p_re * w_im + p_im * w_re, tab[0], tab[1]
    )
    far_re, far_im = left_apply(rows_to_lanes(half_re), rows_to_lanes(half_im), tab[4])
    measured, live = [], []
    for q in range(PAIRS):
        even, odd = interleave(
            inten[2 * q * 32 : 2 * q * 32 + 32, :], inten[2 * q * 32 + 32 : 2 * q * 32 + 64, :]
        )
        measured.append(jnp.concatenate([even, odd], axis=0))
        live.append(
            jnp.where(
                lanes((1, 128)) < 64, mask_ref[0, 2 * q].astype(F32), mask_ref[0, 2 * q + 1].astype(F32)
            )
        )
    measured = jnp.concatenate(measured, axis=1)
    live = jnp.concatenate(live, axis=1)
    factor = live * (far_re * far_re + far_im * far_im - measured)
    half_re, half_im = left_apply(factor * far_re, factor * far_im, tab[5])
    back_re, back_im = right_apply(lanes_to_rows(half_re), lanes_to_rows(half_im), tab[2], tab[3])
    gra_r[...] = p_re * back_re + p_im * back_im
    gra_i[...] = p_re * back_im - p_im * back_re
    grad_re = jnp.sum((w_re * back_re + w_im * back_im).reshape(PAIRS, 64, 128), axis=0)
    grad_im = jnp.sum((w_re * back_im - w_im * back_re).reshape(PAIRS, 64, 128), axis=0)
    grad_re = grad_re + swap(grad_re)
    grad_im = grad_im + swap(grad_im)
    probe_part[...] = jnp.where(lanes((64, 128)) < 64, grad_re, grad_im)

    def place(q, carry):
        at = pl.multiple_of(q * 64, 64)
        for h in range(2):
            turn = (cols_ref[0, 2 * q + h] + 128 - 64 * h) % 128
            for c, ref in ((0, gra_r), (1, gra_i)):
                slot = pl.multiple_of((4 * q + 2 * h + c) * 192 + 64, 64)
                pad[pl.ds(slot, 64), :] = pltpu.roll(ref[pl.ds(at, 64), :], turn, 1)
        return carry

    lax.fori_loop(0, PAIRS, place, 0)

    def to_x(stage, step, src, dst):
        peer = lax.rem(me_p + step, PB)
        return pltpu.make_async_remote_copy(
            src_ref=src,
            dst_ref=dst,
            send_sem=x_send.at[stage * 3 + step - 1],
            recv_sem=x_recv.at[stage * 3 + step - 1],
            device_id={"pb": peer},
            device_id_type=pl.DeviceIdType.MESH,
        )

    early = chip // 4 == 0
    late = chip // 16 == 1

    @pl.when(early)
    def _():
        for copy in wts_in:
            copy.wait()
        for n in range(WCH):
            part = slice(n * WROWS, (n + 1) * WROWS)
            wts_t[:, part] = jnp.transpose(wts[part, :])

    pl.semaphore_wait(barrier, CHIPS + PB - 1)
    reduces = [[], []]
    for half in range(2):
        for step in (2, 1, 3, 0):
            tile = lax.rem(me_p + step, PB)
            at = step * SHARE + half * FIRST
            for c in range(2):

                def add(n, total, c=c, tile=tile, half=half):
                    top = (2 * n + c) * 192 + 64 + half * 64 - rows_ref[0, n]
                    column = lanes((64, 128)) + (tile * 128 - cols_ref[0, n])
                    inside = (column >= 0) & (column < 64)
                    return total + jnp.where(inside, pad[pl.ds(top, 64), :], 0.0)

                acc[at + c * 64 : at + c * 64 + 64, :] = lax.fori_loop(
                    0, POS, add, jnp.zeros((64, 128), F32), unroll=8
                )
            if half == 0:
                acc[at + 128 : at + FIRST, :] = probe_part[
                    pl.ds(pl.multiple_of(tile * 16, 16), 16), :
                ]
            if step > 0:
                rows = FIRST if half == 0 else SHARE - FIRST
                copy = to_x(
                    half,
                    step,
                    acc.at[pl.ds(at, rows)],
                    share.at[pl.ds((step - 1) * SHARE + half * FIRST, rows)],
                )
                copy.start()
                reduces[half].append(copy)

    for copy in obj_in:
        copy.wait()

    def fold(q, carry):
        for t in range(4):
            even = obj[pl.ds(t * 512 + 2 * q, 8, stride=64), :]
            odd = obj[pl.ds(t * 512 + 2 * q + 1, 8, stride=64), :]
            first, second = interleave(even, odd)
            at = pl.multiple_of(q * 64 + t * 16, 16)
            lhs[pl.ds(at, 16), :] = jnp.concatenate([first, second], axis=0)
        return carry

    lax.fori_loop(0, 32, fold, 0, unroll=4)
    own_stk = pl.multiple_of(me_p * KEYS, KEYS)
    for half in range(2):
        products = jnp.zeros((64, WIDE), F32)
        for c in range(4):
            pl.when(jnp.logical_not(early))(wts_in[half * 4 + c].wait)
            part = jnp.concatenate(
                [lhs[(c * 8 + n) * 64 : (c * 8 + n + 1) * 64, :] for n in range(8)], axis=1
            ).astype(BF16)
            products = products + dot(
                part, wts[c * 1024 : (c + 1) * 1024, half * WIDE : (half + 1) * WIDE]
            )
        for i in range(3):
            t = half * 3 + i
            ptile[t * 64 : (t + 1) * 64, :] = products[:, i * 128 : (i + 1) * 128]
            lists = [[], []], [[], []]
            for br in range(2):
                part = [ptile[pl.ds(t * 64 + cz * 2 + br, 8, stride=8), :] for cz in range(ZC)]
                for c in range(2):
                    even, odd = interleave(part[2 * c], part[2 * c + 1])
                    lists[0][c].append(even)
                    lists[1][c].append(odd)
            for h in range(2):
                for c in range(2):
                    stk[
                        pl.ds(pl.multiple_of(own_stk + (2 * t + h) * 16, 16), 16),
                        c * 128 : (c + 1) * 128,
                    ] = jnp.concatenate(lists[h][c], axis=0).astype(BF16)

    own_block = stk.at[pl.ds(own_stk, KEYS)]
    gathers = [to_x(2, step, own_block, own_block) for step in (2, 1, 3)]
    for copy in gathers:
        copy.start()

    others["blocks"].wait()
    others["tables"].wait()
    keys = []
    for jj in range(2):
        there = pl.ds(me_p * 2 + jj, LIST, stride=NB)
        block = blocks[there, :]
        keys.append((block // OWN) * KEYS + tables[there, :] * OWN + block % OWN)
    keys = jnp.concatenate(
        [jnp.concatenate(keys, axis=1), jnp.zeros((128 - LIST, 128), jnp.int32)], axis=0
    )
    keys = jnp.transpose(keys.astype(F32)).astype(jnp.int32)
    for t in range(6):
        column = lanes((128, 128)) + t * 128
        total = jnp.zeros((128, 128), F32)
        for e in range(LIST):
            total = total + jnp.where(keys[:, e : e + 1] == column, 1.0, 0.0)
        hit_r[:, t * 128 : (t + 1) * 128] = total.astype(BF16)

    for p in range(PB):
        parts = []
        for jj in range(2):
            there = pl.ds(p * 2 + jj, LIST, stride=NB)
            block = blocks[there, :]
            place = tables[there, :] * OWN + block % OWN
            parts.append(jnp.where(block // OWN == me_p, place, -1))
        colkey[:, p * 128 : (p + 1) * 128] = jnp.concatenate(parts, axis=1)
    for r in range(3):
        mine = lax.broadcasted_iota(jnp.int32, (64, 512), 0) + r * 64
        total = jnp.zeros((64, 512), F32)
        for e in range(LIST):
            total = total + jnp.where(colkey[e : e + 1, :] == mine, 1.0, 0.0)
        hit_c[r * 64 : (r + 1) * 64, :] = total.astype(BF16)

    def to_a(stage, peer, src, dst):
        return pltpu.make_async_remote_copy(
            src_ref=src,
            dst_ref=dst,
            send_sem=a_send.at[stage],
            recv_sem=a_recv.at[stage],
            device_id={"aa": peer},
            device_id_type=pl.DeviceIdType.MESH,
        )

    def swap_cores(stage, half, loose, extra, across, arrived):
        at = half * 80
        for k in range(4):
            across[at + k * 16 : at + k * 16 + 16, :] = loose[
                pl.ds(k * 64 + half * 32 + 1 - core, 16, stride=2), :
            ]
        rows = 64
        if extra is not None:
            across[64:80, :] = extra
            rows = 80
        copy = to_a(stage, sibling, across.at[pl.ds(at, rows)], arrived.at[pl.ds(at, rows)])
        copy.start()
        return copy

    def fill(half, loose, arrived, message):
        for k in range(4):
            message[pl.ds(half * 256 + core * 4 + k, 16, stride=SLOT), :] = loose[
                pl.ds(k * 64 + half * 32 + core, 16, stride=2), :
            ]
            message[pl.ds(half * 256 + (1 - core) * 4 + k, 16, stride=SLOT), :] = arrived[
                half * 80 + k * 16 : half * 80 + k * 16 + 16, :
            ]

    def exchange(stage, half, message, target, count):
        here = pl.ds(pl.multiple_of(chip * SLOT, SLOT), count)

        def send(step):
            there = half * 16 + lax.rem(chip + step, 16)
            to_a(
                stage,
                there * 2 + core,
                message.at[pl.ds(pl.multiple_of(there * SLOT, SLOT), count)],
                target.at[here],
            ).start()

        for step in range(1, 16):
            send(step)
        pl.when(chip // 16 != half)(lambda: send(0))

        @pl.when(chip // 16 == half)
        def _():
            target[here, :] = message[here, :]

        rows = (CHIPS - 1) * count
        return to_a(
            stage,
            lax.rem(chip + 1, CHIPS) * 2 + core,
            message.at[pl.ds(0, rows)],
            target.at[pl.ds(0, rows)],
        )

    others["dual"].wait()
    swaps = []
    for half in range(2):
        for copy in reduces[half]:
            copy.wait_recv()
        for c in range(2):
            at = half * FIRST + c * 64
            gradient = acc[at : at + 64, :]
            for n in range(PB - 1):
                gradient = gradient + share[n * SHARE + at : n * SHARE + at + 64, :]
            top = c * 128 + half * 64
            mine = wave[pl.ds(pl.multiple_of(me_p * 256 + top, 64), 64), :]
            base[top : top + 64, :] = mine - WAVE_STEP * (
                gradient + PENALTY * (mine + dual[top : top + 64, :])
            )
            for z in range(2):
                there = pl.ds(top + z, 32, stride=2)
                k = 2 * c + z
                loose1[k * 64 + half * 32 : k * 64 + half * 32 + 32, :] = (
                    base[there, :] + dual[there, :]
                )
        probe_share = None
        if half == 0:
            probe_share = acc[128:FIRST, :]
            for n in range(PB - 1):
                probe_share = probe_share + share[n * SHARE + 128 : n * SHARE + FIRST, :]
        swaps.append(swap_cores(half, half, loose1, probe_share, across1, arrived1))
        swaps[-1].wait_recv()
        fill(half, loose1, arrived1, message1)
        if half == 0:
            probe_chip = probe_share + arrived1[64:80, :]
            message1[pl.ds(8, 32, stride=SLOT), :] = jnp.concatenate([probe_chip] * 2, axis=0)
        move1 = exchange(2, half, message1, recv1, 9)

    for copy in gathers:
        copy.wait_recv()
    projection = dot(hit_r[...], stk[...])
    for c in range(2):
        first, second = interleave(
            projection[:64, c * 128 : (c + 1) * 128], projection[64:, c * 128 : (c + 1) * 128]
        )
        loose2[2 * c * 64 : 2 * c * 64 + 64, :] = first
        loose2[2 * c * 64 + 64 : 2 * c * 64 + 128, :] = second

    later = [swap_cores(3 + half, half, loose2, None, across2, arrived2) for half in range(2)]
    for half in range(2):
        later[half].wait_recv()
        fill(half, loose2, arrived2, message2)
    swaps += later

    @pl.when(late)
    def _():
        exchange(5, 0, message2, recv2, 8)

    move1.wait_recv()
    for half in range(2):
        for k in range(4):
            there = pl.ds(k * 64 + half, 32, stride=2)
            own = loose2[there, :]
            rest = recv1[pl.ds(half * 4 + k, 32, stride=SLOT), :]
            misfit[there, :] = own - (rest + (WAVE_STEP * PENALTY) * own)
    own_rays = pl.multiple_of(me_p * 128, 128)
    for c in range(2):
        first, second = interleave(
            misfit[2 * c * 64 : 2 * c * 64 + 64, :], misfit[2 * c * 64 + 64 : 2 * c * 64 + 128, :]
        )
        rays[pl.ds(own_rays, 128), c * 128 : (c + 1) * 128] = jnp.concatenate(
            [first, second], axis=0
        ).astype(BF16)
    own_rows = rays.at[pl.ds(own_rays, 128)]
    ray_moves = [to_x(3, step, own_rows, own_rows) for step in (2, 1, 3)]
    for copy in ray_moves:
        copy.start()

    own_row = pl.ds(pl.multiple_of(me_p * 8, 8), 1)
    prow[own_row, :] = jnp.sum(recv1[pl.ds(8, 32, stride=SLOT), :], axis=0, keepdims=True)
    probe_x = [to_x(4, step, prow.at[own_row], prow.at[own_row]) for step in (2, 1, 3)]
    for copy in probe_x:
        copy.start()

    @pl.when(jnp.logical_not(late))
    def _():
        exchange(5, 0, message2, recv2, 8)

    move2 = exchange(5, 1, message2, recv2, 8)

    for copy in probe_x:
        copy.wait_recv()
    kind = chip % 16
    own_four = pl.ds(pl.multiple_of(kind * 8, 8), 4)
    pfull[own_four, :] = jnp.concatenate([prow[p * 8 : p * 8 + 1, :] for p in range(PB)], axis=0)

    def share_rows(step, rows):
        peer = chip - kind + lax.rem(kind + step, 16)
        return to_a(6, peer * 2 + core, rows, rows)

    for step in range(1, 16):
        share_rows(step, pfull.at[own_four]).start()

    for copy in ray_moves:
        copy.wait_recv()

    sums = dot(hit_c[...], rays[...]).astype(BF16).astype(F32)
    for t in range(6):
        for br in range(2):
            for c in range(2):
                at = 2 * t * 16 + br * 8
                first, second = interleave(
                    sums[at : at + 8, c * 128 : (c + 1) * 128],
                    sums[at + 16 : at + 24, c * 128 : (c + 1) * 128],
                )
                spread[pl.ds(t * 64 + 4 * c + br, 8, stride=8), :] = first
                spread[pl.ds(t * 64 + 4 * c + 2 + br, 8, stride=8), :] = second
    table = jnp.concatenate(
        [spread[t * 64 : (t + 1) * 64, :] for t in range(6)], axis=1
    ).astype(BF16)

    def object_step(product):
        per = 32 // WCH
        for n in range(WCH):
            grad = product(slice(n * WROWS, (n + 1) * WROWS))
            for s in range(per):
                q = n * per + s
                for t in range(4):
                    first, second = interleave(
                        grad[t * 16 : t * 16 + 8, s * 128 : (s + 1) * 128],
                        grad[t * 16 + 8 : t * 16 + 16, s * 128 : (s + 1) * 128],
                    )
                    even = pl.ds(t * 512 + 2 * q, 8, stride=64)
                    odd = pl.ds(t * 512 + 2 * q + 1, 8, stride=64)
                    onew[even, :] = obj[even, :] - OBJECT_STEP * first
                    onew[odd, :] = obj[odd, :] - OBJECT_STEP * second

    @pl.when(early)
    def _():
        object_step(lambda part: dot(table, wts_t[:, part]))

    @pl.when(jnp.logical_not(early))
    def _():
        object_step(
            lambda part: lax.dot_general(
                table, wts[part, :], (((1,), (1,)), ((), ())), preferred_element_type=F32
            )
        )

    move2.wait_recv()
    for half in range(2):
        for c in range(2):
            for z in range(2):
                there = pl.ds(c * 128 + 2 * half + z, 32, stride=4)
                here = recv2[pl.ds(half * 4 + 2 * c + z, 32, stride=SLOT), :]
                wnext[there, :] = base[there, :] + (WAVE_STEP * PENALTY) * here
    probe_all = share_rows(1, pfull.at[pl.ds(0, 60)])
    probe_all.wait_recv()
    total = jnp.concatenate([pfull[pl.ds(p, 16, stride=8), :] for p in range(PB)], axis=0)
    scale = PROBE_STEP / (AA * POS * PB)
    pnext[0] = probe[0] - scale * total[:, :64]
    pnext[1] = probe[1] - scale * swap(total)[:, :64]

    xs = gathers + reduces[0] + reduces[1] + probe_x + ray_moves
    for copy in xs + swaps + [move1, move2, probe_all]:
        copy.wait_send()


def tail(wnext, pnext, onew, wave_out, probe_out, obj_out, sem):
    pairs = [
        (onew.at[pl.ds(t * 512, 512)], obj_out.at[:, pl.ds(t * 128, 128)]) for t in range(4)
    ] + [(wnext, wave_out), (pnext, probe_out)]
    copies = [pltpu.make_async_copy(src, dst, sem.at[n]) for n, (src, dst) in enumerate(pairs)]
    for copy in copies:
        copy.start()
    for copy in copies:
        copy.wait()


def shards(
    tables,
    wave_field,
    scaled_dual,
    intensity,
    probe_field,
    scan_rows,
    scan_cols,
    sample_mask,
    object_field,
    ray_blocks,
    ray_tables,
    radon_weights,
):
    smem = pl.BlockSpec(memory_space=pltpu.SMEM)
    vmem = pltpu.VMEM
    hbm_spec = pl.BlockSpec(memory_space=pltpu.HBM)
    vmem_spec = pl.BlockSpec(memory_space=pltpu.VMEM)
    kept = pl.pallas_call(
        kernel,
        out_shape=(
            pltpu.VMEM((256, 128), F32),
            pltpu.VMEM((2, 64, 64), F32),
            pltpu.VMEM((2048, 128), F32),
        ),
        in_specs=[smem] * 3 + [hbm_spec] * 9,
        out_specs=[vmem_spec] * 3,
        scratch_shapes=[
            vmem((4096, 768), BF16),
            vmem((768, 4096), BF16),
            vmem((2048, 128), F32),
            vmem((1024, 128), F32),
            vmem((256, 128), F32),
            vmem((POS, 4096), F32),
            vmem((POS * 32, 128), F32),
            vmem((2, 64, 64), F32),
            vmem((640, 256), F32),
            vmem((6, 256, 256), BF16),
            vmem((LIST * NB, AA), jnp.int32),
            vmem((LIST * NB, AA), jnp.int32),
            vmem((LIST, 512), jnp.int32),
            vmem((2048, 128), F32),
            vmem((384, 128), F32),
            vmem((768, 256), BF16),
            vmem((128, 768), BF16),
            vmem((KEYS, 512), BF16),
            vmem((512, 128), F32),
            vmem((512, 128), F32),
            vmem((512, 128), F32),
            vmem((512, 128), F32),
            vmem((2 * POS * 192, 128), F32),
            vmem((PB * SHARE, 128), F32),
            vmem(((PB - 1) * SHARE, 128), F32),
            vmem((256, 128), F32),
            vmem((256, 128), F32),
            vmem((144, 128), F32),
            vmem((144, 128), F32),
            vmem((CHIPS * SLOT, 128), F32),
            vmem((CHIPS * SLOT, 128), F32),
            vmem((256, 128), F32),
            vmem((256, 128), F32),
            vmem((144, 128), F32),
            vmem((144, 128), F32),
            vmem((CHIPS * SLOT, 128), F32),
            vmem((CHIPS * SLOT, 128), F32),
            vmem((512, 256), BF16),
            vmem((384, 128), F32),
            vmem((32, 128), F32),
            vmem((128, 128), F32),
            vmem((64, 128), F32),
            pltpu.SemaphoreType.DMA((14,)),
            pltpu.SemaphoreType.DMA((WCH,)),
            pltpu.SemaphoreType.DMA((15,)),
            pltpu.SemaphoreType.DMA((15,)),
            pltpu.SemaphoreType.DMA((7,)),
            pltpu.SemaphoreType.DMA((7,)),
        ],
        compiler_params=pltpu.CompilerParams(
            collective_id=0, has_side_effects=True, vmem_limit_bytes=60 * 1024 * 1024
        ),
        name="admm",
    )(
        scan_rows,
        scan_cols,
        sample_mask,
        object_field.reshape(512, 512),
        radon_weights,
        wave_field.reshape(256, 512),
        scaled_dual.reshape(256, 128),
        intensity.reshape(POS, 4096),
        probe_field,
        tables,
        ray_blocks.transpose(2, 1, 0).reshape(LIST * NB, AA),
        ray_tables.transpose(2, 1, 0).reshape(LIST * NB, AA),
    )
    wave_next, probe_next, object_next = pl.pallas_call(
        tail,
        out_shape=(
            jax.ShapeDtypeStruct((256, 128), F32),
            jax.ShapeDtypeStruct((2, 64, 64), F32),
            jax.ShapeDtypeStruct((512, 512), F32),
        ),
        in_specs=[vmem_spec] * 3,
        out_specs=[hbm_spec] * 3,
        scratch_shapes=[pltpu.SemaphoreType.DMA((6,))],
        compiler_params=pltpu.CompilerParams(vmem_limit_bytes=16 * 1024 * 1024),
        name="tail",
    )(*kept)
    return (
        wave_next.reshape(1, 2, 128, 128),
        probe_next,
        object_next.reshape(2, 2, 128, 512),
    )


def solution(mesh):
    specs = (
        P("aa", None, None, None),
        P("aa", None, None, "pb"),
        P("aa", "pb", None),
        P(),
        P("aa", "pb"),
        P("aa", "pb"),
        P("aa", "pb"),
        P(None, "aa", "pb", None),
        P(),
        P(),
        P(),
    )
    mapped = jax.shard_map(
        shards,
        mesh=mesh,
        in_specs=(P(),) + specs,
        out_specs=(P("aa", None, None, "pb"), P(), P(None, "aa", "pb", None)),
        check_vma=False,
    )

    def step(*arrays):
        return mapped(jnp.asarray(dft_constants()), *arrays)

    return step
```

```python
import math

import jax
import jax.numpy as jnp
import numpy as np
from jax import lax
from jax.experimental import pallas as pl
from jax.experimental.pallas import tpu as pltpu
from jax.sharding import PartitionSpec as P

BLK = 64
NW = 12
NB = 8
LIST = 12
AA = 64
PB = 4
ZC = 4
POS = 16
PAIRS = 8
OWN = 64 // PB
KEYS = 192
CHIPS = 32
SLOT = 16
SHARE = 272
FIRST = 144
WCH = 8
WROWS = 4096 // WCH
WIDE = 384

WAVE_STEP = 0.05
PENALTY = 1.0
PROBE_STEP = 0.05
OBJECT_STEP = 1.0

F32 = jnp.float32
BF16 = jnp.bfloat16


def dft_constants():
    index = np.arange(BLK)
    phase = (index[:, None] * index[None, :]) % BLK
    angle = phase.astype(np.float64) * (-2.0 * math.pi / BLK)
    f_re, f_im = np.cos(angle) / math.sqrt(BLK), np.sin(angle) / math.sqrt(BLK)
    pair = np.eye(2)

    def right(re, im):
        dre, dim = np.kron(pair, re), np.kron(pair, im)
        return np.block([[dre, dim], [-dim, dre]])

    def left(re, im):
        return np.block([[re, -im], [im, re]])

    order = np.concatenate([np.arange(0, BLK, 2), np.arange(1, BLK, 2)])
    rights = [right(f_re, f_im), right(f_re, -f_im)]
    lefts = np.concatenate(
        [left(f_re[order, :], f_im[order, :]), left(f_re[:, order], -f_im[:, order])], axis=1
    )
    return np.concatenate(rights + [lefts], axis=0).astype(np.float32)


def halves(value):
    high = value.astype(BF16)
    low = (value - high.astype(F32)).astype(BF16)
    return high, low


def dot(lhs, rhs):
    return jnp.dot(lhs, rhs, preferred_element_type=F32)


def right_apply(re, im, g_hi, g_lo):
    high, low = halves(jnp.concatenate([re, im], axis=1))
    out = dot(high, g_hi) + dot(low, g_hi) + dot(high, g_lo)
    return out[:, :128], out[:, 128:]


def left_apply(re, im, table):
    high, low = halves(jnp.concatenate([re, im], axis=0))
    out = dot(table, jnp.concatenate([high, low], axis=0))
    out = out[:128] + out[128:]
    return out[:64], out[64:]


def rows_to_lanes(value):
    return jnp.concatenate([value[q * 64 : (q + 1) * 64] for q in range(PAIRS)], axis=1)


def lanes_to_rows(value):
    return jnp.concatenate([value[:, q * 128 : (q + 1) * 128] for q in range(PAIRS)], axis=0)


def swap(value):
    return pltpu.roll(value, 64, 1)


def interleave(first, second):
    low = lax.broadcasted_iota(jnp.int32, first.shape, 1) < 64
    return jnp.where(low, first, swap(second)), jnp.where(low, swap(first), second)


def kernel(
    rows_ref,
    cols_ref,
    mask_ref,
    obj_hbm,
    wts_hbm,
    wave_hbm,
    dual_hbm,
    int_hbm,
    probe_hbm,
    tab_hbm,
    blocks_hbm,
    tables_hbm,
    wnext,
    pnext,
    onew,
    wts,
    wts_t,
    obj,
    wave,
    dual,
    int_raw,
    inten,
    probe,
    tab_raw,
    tab,
    blocks,
    tables,
    colkey,
    lhs,
    ptile,
    stk,
    hit_r,
    hit_c,
    win_r,
    win_i,
    gra_r,
    gra_i,
    pad,
    acc,
    share,
    base,
    loose1,
    across1,
    arrived1,
    message1,
    recv1,
    loose2,
    misfit,
    across2,
    arrived2,
    message2,
    recv2,
    rays,
    spread,
    prow,
    pfull,
    probe_part,
    in_sem,
    w_sem,
    x_send,
    x_recv,
    a_send,
    a_recv,
):
    me_a = lax.axis_index("aa")
    me_p = lax.axis_index("pb")
    core = me_a % 2
    chip = me_a // 2
    sibling = me_a + 1 - 2 * core

    def lanes(shape):
        return lax.broadcasted_iota(jnp.int32, shape, 1)

    obj_in = [
        pltpu.make_async_copy(
            obj_hbm.at[:, pl.ds(t * 128, 128)], obj.at[pl.ds(t * 512, 512)], in_sem.at[t]
        )
        for t in range(4)
    ]
    wts_in = [
        pltpu.make_async_copy(
            wts_hbm.at[pl.ds(c * 1024, 1024), pl.ds(h * WIDE, WIDE)],
            wts.at[pl.ds(c * 1024, 1024), pl.ds(h * WIDE, WIDE)],
            w_sem.at[h * 4 + c],
        )
        for h in range(2)
        for c in range(4)
    ]
    wave_in = [
        pltpu.make_async_copy(
            wave_hbm.at[:, pl.ds(t * 128, 128)], wave.at[pl.ds(t * 256, 256)], in_sem.at[4 + t]
        )
        for t in range(4)
    ]
    others = {
        name: pltpu.make_async_copy(src, dst, in_sem.at[8 + n])
        for n, (name, src, dst) in enumerate(
            [
                ("blocks", blocks_hbm, blocks),
                ("tables", tables_hbm, tables),
                ("probe", probe_hbm, probe),
                ("tab", tab_hbm, tab_raw),
                ("inten", int_hbm, int_raw),
                ("dual", dual_hbm, dual),
            ]
        )
    }
    for copy in wave_in:
        copy.start()
    for name in ("probe", "tab", "inten"):
        others[name].start()
    barrier = pltpu.get_barrier_semaphore()

    for step in range(1, PB):
        pl.semaphore_signal(
            barrier,
            inc=1,
            device_id={"pb": lax.rem(me_p + step, PB)},
            device_id_type=pl.DeviceIdType.MESH,
        )
    for peer in [lax.rem(chip + step, CHIPS) * 2 + core for step in range(1, CHIPS)] + [sibling]:
        pl.semaphore_signal(
            barrier, inc=1, device_id={"aa": peer}, device_id_type=pl.DeviceIdType.MESH
        )
    for copy in obj_in + wts_in:
        copy.start()
    for name in ("dual", "blocks", "tables"):
        others[name].start()

    def clear(n, carry):
        for at in (0, 128):
            pad[pl.ds(pl.multiple_of(n * 192 + at, 64), 64), :] = jnp.zeros((64, 128), F32)
        return carry

    lax.fori_loop(0, 2 * POS, clear, 0)

    for copy in wave_in:
        copy.wait()

    def windows(q, carry):
        at = pl.multiple_of(q * 64, 64)
        for c, ref in ((0, win_r), (1, win_i)):
            found = []
            for h in range(2):
                row = rows_ref[0, 2 * q + h]
                col = cols_ref[0, 2 * q + h]
                tile = col // 128
                off = col % 128
                near = wave[pl.ds(tile * 256 + c * 128 + row, 64), :]
                far = wave[pl.ds(jnp.minimum(tile + 1, 3) * 256 + c * 128 + row, 64), :]
                both = jnp.where(lanes((64, 128)) >= off, near, far)
                found.append(pltpu.roll(both, (128 + 64 * h - off) % 128, 1))
            ref[pl.ds(at, 64), :] = jnp.where(lanes((64, 128)) < 64, found[0], found[1])
        return carry

    lax.fori_loop(0, PAIRS, windows, 0)
    others["probe"].wait()
    others["tab"].wait()
    others["inten"].wait()
    for octet in range(2):
        for t in range(32):
            inten[pl.ds(octet * 256 + t, 8, stride=32), :] = int_raw[
                octet * 8 : octet * 8 + 8, t * 128 : (t + 1) * 128
            ]
    for n in range(2):
        tab[2 * n], tab[2 * n + 1] = halves(tab_raw[n * 256 : (n + 1) * 256, :])
        high, low = halves(tab_raw[512:640, n * 128 : (n + 1) * 128])
        tab[4 + n] = jnp.concatenate(
            [jnp.concatenate([high] * 2, axis=1), jnp.concatenate([low] * 2, axis=1)], axis=0
        )
    one_re = jnp.concatenate([probe[0]] * 2, axis=1)
    one_im = jnp.concatenate([probe[1]] * 2, axis=1)
    p_re = jnp.concatenate([one_re] * PAIRS, axis=0)
    p_im = jnp.concatenate([one_im] * PAIRS, axis=0)
    w_re, w_im = win_r[...], win_i[...]
    half_re, half_im = right_apply(
        p_re * w_re - p_im * w_im, p_re * w_im + p_im * w_re, tab[0], tab[1]
    )
    far_re, far_im = left_apply(rows_to_lanes(half_re), rows_to_lanes(half_im), tab[4])
    measured, live = [], []
    for q in range(PAIRS):
        even, odd = interleave(
            inten[2 * q * 32 : 2 * q * 32 + 32, :], inten[2 * q * 32 + 32 : 2 * q * 32 + 64, :]
        )
        measured.append(jnp.concatenate([even, odd], axis=0))
        live.append(
            jnp.where(
                lanes((1, 128)) < 64, mask_ref[0, 2 * q].astype(F32), mask_ref[0, 2 * q + 1].astype(F32)
            )
        )
    measured = jnp.concatenate(measured, axis=1)
    live = jnp.concatenate(live, axis=1)
    factor = live * (far_re * far_re + far_im * far_im - measured)
    half_re, half_im = left_apply(factor * far_re, factor * far_im, tab[5])
    back_re, back_im = right_apply(lanes_to_rows(half_re), lanes_to_rows(half_im), tab[2], tab[3])
    gra_r[...] = p_re * back_re + p_im * back_im
    gra_i[...] = p_re * back_im - p_im * back_re
    grad_re = jnp.sum((w_re * back_re + w_im * back_im).reshape(PAIRS, 64, 128), axis=0)
    grad_im = jnp.sum((w_re * back_im - w_im * back_re).reshape(PAIRS, 64, 128), axis=0)
    grad_re = grad_re + swap(grad_re)
    grad_im = grad_im + swap(grad_im)
    probe_part[...] = jnp.where(lanes((64, 128)) < 64, grad_re, grad_im)

    def place(q, carry):
        at = pl.multiple_of(q * 64, 64)
        for h in range(2):
            turn = (cols_ref[0, 2 * q + h] + 128 - 64 * h) % 128
            for c, ref in ((0, gra_r), (1, gra_i)):
                slot = pl.multiple_of((4 * q + 2 * h + c) * 192 + 64, 64)
                pad[pl.ds(slot, 64), :] = pltpu.roll(ref[pl.ds(at, 64), :], turn, 1)
        return carry

    lax.fori_loop(0, PAIRS, place, 0)

    def to_x(stage, step, src, dst):
        peer = lax.rem(me_p + step, PB)
        return pltpu.make_async_remote_copy(
            src_ref=src,
            dst_ref=dst,
            send_sem=x_send.at[stage * 3 + step - 1],
            recv_sem=x_recv.at[stage * 3 + step - 1],
            device_id={"pb": peer},
            device_id_type=pl.DeviceIdType.MESH,
        )

    early = chip // 4 == 0
    late = chip // 16 == 1

    @pl.when(early)
    def _():
        for copy in wts_in:
            copy.wait()
        for n in range(WCH):
            part = slice(n * WROWS, (n + 1) * WROWS)
            wts_t[:, part] = jnp.transpose(wts[part, :])

    pl.semaphore_wait(barrier, CHIPS + PB - 1)
    reduces = [[], []]
    for half in range(2):
        for step in (2, 1, 3, 0):
            tile = lax.rem(me_p + step, PB)
            at = step * SHARE + half * FIRST
            for c in range(2):

                def add(n, total, c=c, tile=tile, half=half):
                    top = (2 * n + c) * 192 + 64 + half * 64 - rows_ref[0, n]
                    column = lanes((64, 128)) + (tile * 128 - cols_ref[0, n])
                    inside = (column >= 0) & (column < 64)
                    return total + jnp.where(inside, pad[pl.ds(top, 64), :], 0.0)

                acc[at + c * 64 : at + c * 64 + 64, :] = lax.fori_loop(
                    0, POS, add, jnp.zeros((64, 128), F32), unroll=8
                )
            if half == 0:
                acc[at + 128 : at + FIRST, :] = probe_part[
                    pl.ds(pl.multiple_of(tile * 16, 16), 16), :
                ]
            if step > 0:
                rows = FIRST if half == 0 else SHARE - FIRST
                copy = to_x(
                    half,
                    step,
                    acc.at[pl.ds(at, rows)],
                    share.at[pl.ds((step - 1) * SHARE + half * FIRST, rows)],
                )
                copy.start()
                reduces[half].append(copy)

    for copy in obj_in:
        copy.wait()

    def fold(q, carry):
        for t in range(4):
            even = obj[pl.ds(t * 512 + 2 * q, 8, stride=64), :]
            odd = obj[pl.ds(t * 512 + 2 * q + 1, 8, stride=64), :]
            first, second = interleave(even, odd)
            at = pl.multiple_of(q * 64 + t * 16, 16)
            lhs[pl.ds(at, 16), :] = jnp.concatenate([first, second], axis=0)
        return carry

    lax.fori_loop(0, 32, fold, 0, unroll=4)
    own_stk = pl.multiple_of(me_p * KEYS, KEYS)
    for half in range(2):
        products = jnp.zeros((64, WIDE), F32)
        for c in range(4):
            pl.when(jnp.logical_not(early))(wts_in[half * 4 + c].wait)
            part = jnp.concatenate(
                [lhs[(c * 8 + n) * 64 : (c * 8 + n + 1) * 64, :] for n in range(8)], axis=1
            ).astype(BF16)
            products = products + dot(
                part, wts[c * 1024 : (c + 1) * 1024, half * WIDE : (half + 1) * WIDE]
            )
        for i in range(3):
            t = half * 3 + i
            ptile[t * 64 : (t + 1) * 64, :] = products[:, i * 128 : (i + 1) * 128]
            lists = [[], []], [[], []]
            for br in range(2):
                part = [ptile[pl.ds(t * 64 + cz * 2 + br, 8, stride=8), :] for cz in range(ZC)]
                for c in range(2):
                    even, odd = interleave(part[2 * c], part[2 * c + 1])
                    lists[0][c].append(even)
                    lists[1][c].append(odd)
            for h in range(2):
                for c in range(2):
                    stk[
                        pl.ds(pl.multiple_of(own_stk + (2 * t + h) * 16, 16), 16),
                        c * 128 : (c + 1) * 128,
                    ] = jnp.concatenate(lists[h][c], axis=0).astype(BF16)

    own_block = stk.at[pl.ds(own_stk, KEYS)]
    gathers = [to_x(2, step, own_block, own_block) for step in (2, 1, 3)]
    for copy in gathers:
        copy.start()

    others["blocks"].wait()
    others["tables"].wait()
    keys = []
    for jj in range(2):
        there = pl.ds(me_p * 2 + jj, LIST, stride=NB)
        block = blocks[there, :]
        keys.append((block // OWN) * KEYS + tables[there, :] * OWN + block % OWN)
    keys = jnp.concatenate(
        [jnp.concatenate(keys, axis=1), jnp.zeros((128 - LIST, 128), jnp.int32)], axis=0
    )
    keys = jnp.transpose(keys.astype(F32)).astype(jnp.int32)
    for t in range(6):
        column = lanes((128, 128)) + t * 128
        total = jnp.zeros((128, 128), F32)
        for e in range(LIST):
            total = total + jnp.where(keys[:, e : e + 1] == column, 1.0, 0.0)
        hit_r[:, t * 128 : (t + 1) * 128] = total.astype(BF16)

    for p in range(PB):
        parts = []
        for jj in range(2):
            there = pl.ds(p * 2 + jj, LIST, stride=NB)
            block = blocks[there, :]
            place = tables[there, :] * OWN + block % OWN
            parts.append(jnp.where(block // OWN == me_p, place, -1))
        colkey[:, p * 128 : (p + 1) * 128] = jnp.concatenate(parts, axis=1)
    for r in range(3):
        mine = lax.broadcasted_iota(jnp.int32, (64, 512), 0) + r * 64
        total = jnp.zeros((64, 512), F32)
        for e in range(LIST):
            total = total + jnp.where(colkey[e : e + 1, :] == mine, 1.0, 0.0)
        hit_c[r * 64 : (r + 1) * 64, :] = total.astype(BF16)

    def to_a(stage, peer, src, dst):
        return pltpu.make_async_remote_copy(
            src_ref=src,
            dst_ref=dst,
            send_sem=a_send.at[stage],
            recv_sem=a_recv.at[stage],
            device_id={"aa": peer},
            device_id_type=pl.DeviceIdType.MESH,
        )

    def swap_cores(stage, half, loose, extra, across, arrived):
        at = half * 80
        for k in range(4):
            across[at + k * 16 : at + k * 16 + 16, :] = loose[
                pl.ds(k * 64 + half * 32 + 1 - core, 16, stride=2), :
            ]
        rows = 64
        if extra is not None:
            across[64:80, :] = extra
            rows = 80
        copy = to_a(stage, sibling, across.at[pl.ds(at, rows)], arrived.at[pl.ds(at, rows)])
        copy.start()
        return copy

    def fill(half, loose, arrived, message):
        for k in range(4):
            message[pl.ds(half * 256 + core * 4 + k, 16, stride=SLOT), :] = loose[
                pl.ds(k * 64 + half * 32 + core, 16, stride=2), :
            ]
            message[pl.ds(half * 256 + (1 - core) * 4 + k, 16, stride=SLOT), :] = arrived[
                half * 80 + k * 16 : half * 80 + k * 16 + 16, :
            ]

    def exchange(stage, half, message, target, count):
        here = pl.ds(pl.multiple_of(chip * SLOT, SLOT), count)

        def send(step):
            there = half * 16 + lax.rem(chip + step, 16)
            to_a(
                stage,
                there * 2 + core,
                message.at[pl.ds(pl.multiple_of(there * SLOT, SLOT), count)],
                target.at[here],
            ).start()

        for step in range(1, 16):
            send(step)
        pl.when(chip // 16 != half)(lambda: send(0))

        @pl.when(chip // 16 == half)
        def _():
            target[here, :] = message[here, :]

        rows = (CHIPS - 1) * count
        return to_a(
            stage,
            lax.rem(chip + 1, CHIPS) * 2 + core,
            message.at[pl.ds(0, rows)],
            target.at[pl.ds(0, rows)],
        )

    others["dual"].wait()
    swaps = []
    for half in range(2):
        for copy in reduces[half]:
            copy.wait_recv()
        for c in range(2):
            at = half * FIRST + c * 64
            gradient = acc[at : at + 64, :]
            for n in range(PB - 1):
                gradient = gradient + share[n * SHARE + at : n * SHARE + at + 64, :]
            top = c * 128 + half * 64
            mine = wave[pl.ds(pl.multiple_of(me_p * 256 + top, 64), 64), :]
            base[top : top + 64, :] = mine - WAVE_STEP * (
                gradient + PENALTY * (mine + dual[top : top + 64, :])
            )
            for z in range(2):
                there = pl.ds(top + z, 32, stride=2)
                k = 2 * c + z
                loose1[k * 64 + half * 32 : k * 64 + half * 32 + 32, :] = (
                    base[there, :] + dual[there, :]
                )
        probe_share = None
        if half == 0:
            probe_share = acc[128:FIRST, :]
            for n in range(PB - 1):
                probe_share = probe_share + share[n * SHARE + 128 : n * SHARE + FIRST, :]
        swaps.append(swap_cores(half, half, loose1, probe_share, across1, arrived1))
        swaps[-1].wait_recv()
        fill(half, loose1, arrived1, message1)
        if half == 0:
            probe_chip = probe_share + arrived1[64:80, :]
            message1[pl.ds(8, 32, stride=SLOT), :] = jnp.concatenate([probe_chip] * 2, axis=0)
        move1 = exchange(2, half, message1, recv1, 9)

    for copy in gathers:
        copy.wait_recv()
    projection = dot(hit_r[...], stk[...])
    for c in range(2):
        first, second = interleave(
            projection[:64, c * 128 : (c + 1) * 128], projection[64:, c * 128 : (c + 1) * 128]
        )
        loose2[2 * c * 64 : 2 * c * 64 + 64, :] = first
        loose2[2 * c * 64 + 64 : 2 * c * 64 + 128, :] = second

    later = [swap_cores(3 + half, half, loose2, None, across2, arrived2) for half in range(2)]
    for half in range(2):
        later[half].wait_recv()
        fill(half, loose2, arrived2, message2)
    swaps += later

    @pl.when(late)
    def _():
        exchange(5, 0, message2, recv2, 8)

    move1.wait_recv()
    for half in range(2):
        for k in range(4):
            there = pl.ds(k * 64 + half, 32, stride=2)
            own = loose2[there, :]
            rest = recv1[pl.ds(half * 4 + k, 32, stride=SLOT), :]
            misfit[there, :] = own - (rest + (WAVE_STEP * PENALTY) * own)
    own_rays = pl.multiple_of(me_p * 128, 128)
    for c in range(2):
        first, second = interleave(
            misfit[2 * c * 64 : 2 * c * 64 + 64, :], misfit[2 * c * 64 + 64 : 2 * c * 64 + 128, :]
        )
        rays[pl.ds(own_rays, 128), c * 128 : (c + 1) * 128] = jnp.concatenate(
            [first, second], axis=0
        ).astype(BF16)
    own_rows = rays.at[pl.ds(own_rays, 128)]
    ray_moves = [to_x(3, step, own_rows, own_rows) for step in (2, 1, 3)]
    for copy in ray_moves:
        copy.start()

    own_row = pl.ds(pl.multiple_of(me_p * 8, 8), 1)
    probe_x = [to_x(4, step, prow.at[own_row], prow.at[own_row]) for step in (2, 1, 3)]

    @pl.when(late)
    def _():
        prow[own_row, :] = jnp.sum(recv1[pl.ds(8, 32, stride=SLOT), :], axis=0, keepdims=True)
        for copy in probe_x:
            copy.start()

    @pl.when(jnp.logical_not(late))
    def _():
        exchange(5, 0, message2, recv2, 8)

    move2 = exchange(5, 1, message2, recv2, 8)

    kind = chip % 16
    own_four = pl.ds(pl.multiple_of(kind * 8, 8), 4)

    def share_rows(first, step, rows):
        return to_a(6, (first + lax.rem(kind + step, 16)) * 2 + core, rows, rows)

    @pl.when(late)
    def _():
        for copy in probe_x:
            copy.wait_recv()
        pfull[own_four, :] = jnp.concatenate(
            [prow[p * 8 : p * 8 + 1, :] for p in range(PB)], axis=0
        )
        for step in range(16):
            share_rows(0, step, pfull.at[own_four]).start()
        for step in range(1, 16):
            share_rows(16, step, pfull.at[own_four]).start()

    for copy in ray_moves:
        copy.wait_recv()

    sums = dot(hit_c[...], rays[...]).astype(BF16).astype(F32)
    for t in range(6):
        for br in range(2):
            for c in range(2):
                at = 2 * t * 16 + br * 8
                first, second = interleave(
                    sums[at : at + 8, c * 128 : (c + 1) * 128],
                    sums[at + 16 : at + 24, c * 128 : (c + 1) * 128],
                )
                spread[pl.ds(t * 64 + 4 * c + br, 8, stride=8), :] = first
                spread[pl.ds(t * 64 + 4 * c + 2 + br, 8, stride=8), :] = second
    table = jnp.concatenate(
        [spread[t * 64 : (t + 1) * 64, :] for t in range(6)], axis=1
    ).astype(BF16)

    def object_step(product):
        per = 32 // WCH
        for n in range(WCH):
            grad = product(slice(n * WROWS, (n + 1) * WROWS))
            for s in range(per):
                q = n * per + s
                for t in range(4):
                    first, second = interleave(
                        grad[t * 16 : t * 16 + 8, s * 128 : (s + 1) * 128],
                        grad[t * 16 + 8 : t * 16 + 16, s * 128 : (s + 1) * 128],
                    )
                    even = pl.ds(t * 512 + 2 * q, 8, stride=64)
                    odd = pl.ds(t * 512 + 2 * q + 1, 8, stride=64)
                    onew[even, :] = obj[even, :] - OBJECT_STEP * first
                    onew[odd, :] = obj[odd, :] - OBJECT_STEP * second

    @pl.when(early)
    def _():
        object_step(lambda part: dot(table, wts_t[:, part]))

    @pl.when(jnp.logical_not(early))
    def _():
        object_step(
            lambda part: lax.dot_general(
                table, wts[part, :], (((1,), (1,)), ((), ())), preferred_element_type=F32
            )
        )

    move2.wait_recv()
    for half in range(2):
        for c in range(2):
            for z in range(2):
                there = pl.ds(c * 128 + 2 * half + z, 32, stride=4)
                here = recv2[pl.ds(half * 4 + 2 * c + z, 32, stride=SLOT), :]
                wnext[there, :] = base[there, :] + (WAVE_STEP * PENALTY) * here
    @pl.when(late)
    def _():
        rows = pfull.at[pl.ds(0, 60)]
        share_rows(16, 1, rows).wait_recv()
        rows = pfull.at[pl.ds(0, 124)]
        share_rows(16, 1, rows).wait_send()
        for copy in probe_x:
            copy.wait_send()

    @pl.when(jnp.logical_not(late))
    def _():
        rows = pfull.at[pl.ds(0, 64)]
        to_a(6, (16 + kind) * 2 + core, rows, rows).wait_recv()

    total = jnp.concatenate([pfull[pl.ds(p, 16, stride=8), :] for p in range(PB)], axis=0)
    scale = PROBE_STEP / (AA * POS * PB)
    pnext[0] = probe[0] - scale * total[:, :64]
    pnext[1] = probe[1] - scale * swap(total)[:, :64]

    xs = gathers + reduces[0] + reduces[1] + ray_moves
    for copy in xs + swaps + [move1, move2]:
        copy.wait_send()


def tail(wnext, pnext, onew, wave_out, probe_out, obj_out, sem):
    pairs = [
        (onew.at[pl.ds(t * 512, 512)], obj_out.at[:, pl.ds(t * 128, 128)]) for t in range(4)
    ] + [(wnext, wave_out), (pnext, probe_out)]
    copies = [pltpu.make_async_copy(src, dst, sem.at[n]) for n, (src, dst) in enumerate(pairs)]
    for copy in copies:
        copy.start()
    for copy in copies:
        copy.wait()


def shards(
    tables,
    wave_field,
    scaled_dual,
    intensity,
    probe_field,
    scan_rows,
    scan_cols,
    sample_mask,
    object_field,
    ray_blocks,
    ray_tables,
    radon_weights,
):
    smem = pl.BlockSpec(memory_space=pltpu.SMEM)
    vmem = pltpu.VMEM
    hbm_spec = pl.BlockSpec(memory_space=pltpu.HBM)
    vmem_spec = pl.BlockSpec(memory_space=pltpu.VMEM)
    kept = pl.pallas_call(
        kernel,
        out_shape=(
            pltpu.VMEM((256, 128), F32),
            pltpu.VMEM((2, 64, 64), F32),
            pltpu.VMEM((2048, 128), F32),
        ),
        in_specs=[smem] * 3 + [hbm_spec] * 9,
        out_specs=[vmem_spec] * 3,
        scratch_shapes=[
            vmem((4096, 768), BF16),
            vmem((768, 4096), BF16),
            vmem((2048, 128), F32),
            vmem((1024, 128), F32),
            vmem((256, 128), F32),
            vmem((POS, 4096), F32),
            vmem((POS * 32, 128), F32),
            vmem((2, 64, 64), F32),
            vmem((640, 256), F32),
            vmem((6, 256, 256), BF16),
            vmem((LIST * NB, AA), jnp.int32),
            vmem((LIST * NB, AA), jnp.int32),
            vmem((LIST, 512), jnp.int32),
            vmem((2048, 128), F32),
            vmem((384, 128), F32),
            vmem((768, 256), BF16),
            vmem((128, 768), BF16),
            vmem((KEYS, 512), BF16),
            vmem((512, 128), F32),
            vmem((512, 128), F32),
            vmem((512, 128), F32),
            vmem((512, 128), F32),
            vmem((2 * POS * 192, 128), F32),
            vmem((PB * SHARE, 128), F32),
            vmem(((PB - 1) * SHARE, 128), F32),
            vmem((256, 128), F32),
            vmem((256, 128), F32),
            vmem((144, 128), F32),
            vmem((144, 128), F32),
            vmem((CHIPS * SLOT, 128), F32),
            vmem((CHIPS * SLOT, 128), F32),
            vmem((256, 128), F32),
            vmem((256, 128), F32),
            vmem((144, 128), F32),
            vmem((144, 128), F32),
            vmem((CHIPS * SLOT, 128), F32),
            vmem((CHIPS * SLOT, 128), F32),
            vmem((512, 256), BF16),
            vmem((384, 128), F32),
            vmem((32, 128), F32),
            vmem((128, 128), F32),
            vmem((64, 128), F32),
            pltpu.SemaphoreType.DMA((14,)),
            pltpu.SemaphoreType.DMA((WCH,)),
            pltpu.SemaphoreType.DMA((15,)),
            pltpu.SemaphoreType.DMA((15,)),
            pltpu.SemaphoreType.DMA((7,)),
            pltpu.SemaphoreType.DMA((7,)),
        ],
        compiler_params=pltpu.CompilerParams(
            collective_id=0, has_side_effects=True, vmem_limit_bytes=60 * 1024 * 1024
        ),
        name="admm",
    )(
        scan_rows,
        scan_cols,
        sample_mask,
        object_field.reshape(512, 512),
        radon_weights,
        wave_field.reshape(256, 512),
        scaled_dual.reshape(256, 128),
        intensity.reshape(POS, 4096),
        probe_field,
        tables,
        ray_blocks.transpose(2, 1, 0).reshape(LIST * NB, AA),
        ray_tables.transpose(2, 1, 0).reshape(LIST * NB, AA),
    )
    wave_next, probe_next, object_next = pl.pallas_call(
        tail,
        out_shape=(
            jax.ShapeDtypeStruct((256, 128), F32),
            jax.ShapeDtypeStruct((2, 64, 64), F32),
            jax.ShapeDtypeStruct((512, 512), F32),
        ),
        in_specs=[vmem_spec] * 3,
        out_specs=[hbm_spec] * 3,
        scratch_shapes=[pltpu.SemaphoreType.DMA((6,))],
        compiler_params=pltpu.CompilerParams(vmem_limit_bytes=16 * 1024 * 1024),
        name="tail",
    )(*kept)
    return (
        wave_next.reshape(1, 2, 128, 128),
        probe_next,
        object_next.reshape(2, 2, 128, 512),
    )


def solution(mesh):
    specs = (
        P("aa", None, None, None),
        P("aa", None, None, "pb"),
        P("aa", "pb", None),
        P(),
        P("aa", "pb"),
        P("aa", "pb"),
        P("aa", "pb"),
        P(None, "aa", "pb", None),
        P(),
        P(),
        P(),
    )
    mapped = jax.shard_map(
        shards,
        mesh=mesh,
        in_specs=(P(),) + specs,
        out_specs=(P("aa", None, None, "pb"), P(), P(None, "aa", "pb", None)),
        check_vma=False,
    )

    def step(*arrays):
        return mapped(jnp.asarray(dft_constants()), *arrays)

    return step
```
